128 devices in a mesh: row: 4 (over z_lo, core), col: 32 (over x, z_hi, y).
Axes of the slice: x: 4, y: 4, z: 4 (z_hi: 2, z_lo: 2; z = z_hi * 2 + z_lo), core: 2. Of those that a mesh axis runs over, the one named last changes fastest.
Arguments:
- target_points: float32 [3, 65536], P(None, 'row'), may hold values from 0 to 1.5
- source_points: float32 [3, 65536], P(None, 'col'), may hold values from 0 to 1.5
- target_mass: float32 [65536, 128], P(('row', 'col')), may hold values from 0.1 to 1
- source_mass: float32 [65536, 128], P(('col', 'row')), may hold values from 0.1 to 1
- start_dual: bfloat16 [65536, 128], P(('col', 'row')), may hold values from 0.5 to 2
- tile_row: int32 [6144], P(('row', 'col')), may hold values from 0 to 63, as said below
- tile_column: int32 [6144], P(('row', 'col')), may hold values from 0 to 7, as said below
- tile_count: int32 [128], P(('row', 'col')), may hold values from 4 to 48, as said below
Outputs:
- target_dual: float32 [65536, 128], P(('row', 'col'))
- source_dual: float32 [65536, 128], P(('col', 'row'))
The draws below stay inside these ranges and needn't reach their ends.
Inputs may be any that keep to these rules, and one draw needn't show every extreme that they name: `tile_row`: each device owns 48 consecutive slots, devices in the order row then col; entries give tile rows within the device's band of 64; slots at or past the device's count are padding. Every tile row and every tile column of the whole kernel has a live tile on some device, and no device lists a tile twice among its live slots. `tile_column`: tile columns within the device's band of 8, for the same slots. `tile_count`: live slots of each device; some device is full.
All inputs are finite; a program needn't handle non-finite values.
Results may differ from the reference program's by a relative error of at most 0.00066.
Values may be sent and summed in bfloat16 or wider, within the bound.
A program may use at most 128 MiB of HBM per device.

```python
import math
import jax
import jax.numpy as jnp
from jax import lax

TILE = 256
MEASURES = 128
ROW_TILES = 64
COLUMN_TILES = 8
SLOTS = 48
ITERS = 2
TARGETS = 65536
SOURCES = 65536
N_ROW = 4
N_COL = 32


def tile_pattern(key):
    devices = N_ROW * N_COL
    positions = ROW_TILES * COLUMN_TILES
    key_base, key_heavy, key_high, key_order = jax.random.split(key, 4)
    base_count = jax.random.randint(key_base, (devices,), 8, 33)
    ranking = jax.random.permutation(key_heavy, devices)
    heavy_count = jax.random.randint(key_high, (devices,), 30, SLOTS + 1)
    tile_counts = jnp.where(ranking < max(devices // 8, 1), heavy_count, base_count)
    tile_counts = jnp.where(ranking == 0, SLOTS, tile_counts)
    tile_counts = jnp.minimum(jnp.maximum(tile_counts, ROW_TILES // N_COL + COLUMN_TILES // N_ROW), SLOTS)
    device = jnp.arange(devices, dtype=jnp.int32)[:, None, None]
    row_group = device // N_COL
    col_group = device % N_COL
    local_row = jnp.arange(ROW_TILES, dtype=jnp.int32)[None, :, None]
    local_col = jnp.arange(COLUMN_TILES, dtype=jnp.int32)[None, None, :]
    forced = (local_row % N_COL == col_group) & (local_col == local_row // N_COL % COLUMN_TILES) | (local_col % N_ROW == row_group) & (local_row == local_col // N_ROW % ROW_TILES)
    random_part = jax.random.randint(key_order, (devices, ROW_TILES, COLUMN_TILES), 0, 4096)
    priority = random_part * positions + local_row * COLUMN_TILES + local_col + forced.astype(jnp.int32) * (4096 * positions)
    flat_score = priority.reshape(devices, positions)
    values_top, chosen = lax.top_k(flat_score, SLOTS)
    slot_rows = (chosen // COLUMN_TILES).reshape(-1).astype(jnp.int32)
    slot_cols = (chosen % COLUMN_TILES).reshape(-1).astype(jnp.int32)
    return (slot_rows, slot_cols, tile_counts.astype(jnp.int32))


def draw_tile_row(key, part):
    return tile_pattern(key)[0]


def draw_tile_column(key, part):
    return tile_pattern(key)[1]


def draw_tile_count(key, part):
    return tile_pattern(key)[2]


def block_levels(rng, dims, cuts, low, high):
    gain = 1.0
    for position, parts in cuts:
        draws = jax.random.uniform(jax.random.fold_in(jax.random.fold_in(rng, 6), position), (parts,), jnp.float32, low / len(cuts), high / len(cuts))
        gain = gain * jnp.repeat(jnp.exp(draws), dims[position] // parts).reshape((-1,) + (1,) * (len(dims) - 1 - position))
    return gain


def setup_inputs(seed: int = 0) -> dict:
    key_of = jax.random.split(jax.random.key(seed), 9)
    return {
        "target_points": jnp.clip(1.5 * jax.random.uniform(key_of[0], (3, TARGETS), jnp.float32) ** block_levels(key_of[0], (3, TARGETS), ((1, 4),), -0.2, 0.2), 0.0, 1.5),
        "source_points": jnp.clip(1.5 * jax.random.uniform(key_of[1], (3, SOURCES), jnp.float32) ** block_levels(key_of[1], (3, SOURCES), ((1, 32),), -0.2, 0.2), 0.0, 1.5),
        "target_mass": jnp.clip(jnp.exp(math.log(1.0) - 2.3025851 * jax.random.uniform(key_of[2], (TARGETS, MEASURES), jnp.float32) ** block_levels(key_of[2], (TARGETS, MEASURES), ((0, 128),), -0.2, 0.2)), 0.1, 1.0),
        "source_mass": jnp.clip(jnp.exp(math.log(1.0) - 2.3025851 * jax.random.uniform(key_of[3], (SOURCES, MEASURES), jnp.float32) ** block_levels(key_of[3], (SOURCES, MEASURES), ((0, 128),), -0.2, 0.2)), 0.1, 1.0),
        "start_dual": jnp.clip(jnp.exp(math.log(2.0) - 1.3862944 * jax.random.uniform(key_of[4], (SOURCES, MEASURES), jnp.float32) ** block_levels(key_of[4], (SOURCES, MEASURES), ((0, 128),), -0.2, 0.2)), 0.5, 2.0).astype(jnp.bfloat16),
        "tile_row": draw_tile_row(jax.random.fold_in(key_of[8], 71), 0),
        "tile_column": draw_tile_column(jax.random.fold_in(key_of[8], 71), 0),
        "tile_count": draw_tile_count(jax.random.fold_in(key_of[8], 71), 0),
    }


KERNEL_SCALE = 0.2


def tile_weights(target_block, source_block, live_weight):
    distance = (target_block[0][:, None] - source_block[0][None, :]) ** 2
    distance = distance + (target_block[1][:, None] - source_block[1][None, :]) ** 2
    distance = distance + (target_block[2][:, None] - source_block[2][None, :]) ** 2
    return (jnp.exp(-distance / KERNEL_SCALE) / TILE * live_weight).astype(jnp.bfloat16)


def reference(target_points, source_points, target_mass, source_mass, start_dual, tile_row, tile_column, tile_count):
    total_rows = ROW_TILES * N_ROW
    total_cols = COLUMN_TILES * N_COL
    target_tiles = target_points.reshape(3, total_rows, TILE)
    source_tiles = source_points.reshape(3, total_cols, TILE)
    slot_index = jnp.arange(N_ROW * N_COL * SLOTS, dtype=jnp.int32)
    device = slot_index // SLOTS
    global_row = ((device // N_COL) * ROW_TILES + tile_row).astype(jnp.int32)
    global_col = ((device % N_COL) * COLUMN_TILES + tile_column).astype(jnp.int32)
    live_weight = (slot_index % SLOTS < tile_count[device]).astype(jnp.float32)

    def weights(r, c, w):
        return tile_weights(lax.dynamic_index_in_dim(target_tiles, r, 1, False),
                            lax.dynamic_index_in_dim(source_tiles, c, 1, False), w)

    def row_sweep(dual_tiles):
        def advance(totals, slot_item):
            r, c, w = slot_item
            kernel = weights(r, c, w)
            product = jnp.dot(kernel, lax.dynamic_index_in_dim(dual_tiles, c, 0, False), preferred_element_type=jnp.float32)
            current = lax.dynamic_index_in_dim(totals, r, 0, False)
            return lax.dynamic_update_index_in_dim(totals, current + product, r, 0), None
        totals, _ = lax.scan(advance, jnp.zeros((total_rows, TILE, MEASURES), jnp.float32), (global_row, global_col, live_weight))
        return totals.reshape(total_rows * TILE, MEASURES)

    def column_sweep(dual_tiles):
        def advance(totals, slot_item):
            r, c, w = slot_item
            kernel = weights(r, c, w)
            product = jnp.dot(kernel.T, lax.dynamic_index_in_dim(dual_tiles, r, 0, False), preferred_element_type=jnp.float32)
            current = lax.dynamic_index_in_dim(totals, c, 0, False)
            return lax.dynamic_update_index_in_dim(totals, current + product, c, 0), None
        totals, _ = lax.scan(advance, jnp.zeros((total_cols, TILE, MEASURES), jnp.float32), (global_row, global_col, live_weight))
        return totals.reshape(total_cols * TILE, MEASURES)

    source_low = start_dual
    target_dual = target_mass
    source_dual = source_mass
    for iteration in range(ITERS):
        row_sums = row_sweep(source_low.reshape(total_cols, TILE, MEASURES))
        target_dual = target_mass / row_sums
        target_low = target_dual.astype(jnp.bfloat16)
        column_sums = column_sweep(target_low.reshape(total_rows, TILE, MEASURES))
        source_dual = source_mass / column_sums
        source_low = source_dual.astype(jnp.bfloat16)
    return target_dual, source_dual
```

```python
import functools

import jax
import jax.numpy as jnp
from jax import lax
from jax.experimental import pallas as pl
from jax.experimental.pallas import tpu as pltpu
from jax.sharding import PartitionSpec as P

MESH = pl.DeviceIdType.MESH
ITERS = 2
FINE = 2896.0
COARSE = 256.0
F32 = jnp.float32
BF16 = jnp.bfloat16
I16 = jnp.int16
I32 = jnp.int32


def encode(x):
    level = jnp.log(jnp.maximum(x, 1e-37))
    ref = (level[0:1] * COARSE + 32768.5).astype(I32) - 32768
    fine = (level - ref.astype(F32) * (1.0 / COARSE)) * FINE + 32768.5
    code = jnp.clip(fine, 0.5, 65535.0).astype(I32) - 32768
    return code.astype(I16), ref


def decode(code, ref):
    return jnp.exp(
        code.astype(I32).astype(F32) * (1.0 / FINE) + ref.astype(F32) * (1.0 / COARSE)
    )


def kernel(
    slots,
    tp, sp, tm, sm, sd, tr, tc, tn,
    td_out, so_out,
    meta_own, meta_in, meta, tp_in, sp_in, tm_in, tt, sb, kt, acc,
    src_own, s_band, x0_send, x0_recv, r1_send, r1_recv, r2_send, r2_recv, part,
    t_band, z_send, z_recv, td_own,
    p_send, p_recv, s_send, s_recv, x_send, x_recv, a_send, a_recv, b_send, b_recv,
    q_send, q_recv, g_send, g_recv, c_send, c_recv, w_send, w_recv, o_send, o_recv, m_sem,
):
    tile = kt.shape[1]
    measures = acc.shape[1]
    half = measures // 2
    row = lax.axis_index("row")
    col = lax.axis_index("col")
    z_lo, core = row // 2, row % 2
    x, z_hi, y = col // 8, (col // 4) % 2, col % 4
    z = z_hi * 2 + z_lo
    other = 1 - core
    own_role = core == z_hi
    swapped = core != z_hi

    def device(x_, y_, z_, core_):
        return ((z_ % 2) * 2 + core_, x_ * 8 + (z_ // 2) * 4 + y_)

    sibling = device(x, y, z, other)
    partner = device(x, y, core * 2 + z_lo, z_hi)

    def on_ring(axis, step):
        if axis == 0:
            return device((x + step) % 4, y, z, core)
        return device(x, (y + step) % 4, z, core)

    def remote(src, dst, send, recv, target):
        return pltpu.make_async_remote_copy(
            src_ref=src, dst_ref=dst, send_sem=send, recv_sem=recv,
            device_id=target, device_id_type=MESH,
        )

    barrier = pltpu.get_barrier_semaphore()
    friends = [device(x, y, (z + dz) % 4, (core + dk) % 2)
               for dz in range(4) for dk in range(2) if dz or dk]
    friends += [on_ring(axis, step) for axis in (0, 1) for step in (1, 3)]
    for friend in friends:
        pl.semaphore_signal(barrier, inc=1, device_id=friend, device_id_type=MESH)

    meta_own[...] = jnp.zeros_like(meta_own)
    meta_own[0:1, 0:slots] = jnp.clip(tr[...], 0, 63)
    meta_own[1:2, 0:slots] = jnp.clip(tc[...], 0, 7)
    lane = lax.broadcasted_iota(I32, (128, 128), 1)
    sub = lax.broadcasted_iota(I32, (128, 128), 0)
    alive = sub < tn[0]
    for k in range(2):
        across = jnp.broadcast_to(meta_own[k:k + 1, :], (128, 128))
        down = across.T
        same = (down == across) & (sub < lane) & alive
        found = jnp.max(jnp.where(same, sub, -1), axis=0, keepdims=True)
        meta_own[2 + k:3 + k, :] = jnp.where(found < 0, slots, found)
        same = (down == lane) & alive
        found = jnp.max(jnp.where(same, sub, -1), axis=0, keepdims=True)
        meta_own[4 + k:5 + k, :] = jnp.where(found < 0, slots, found)
    index = meta_own[0:1, :]
    share = index // 2
    sx, sh, sy = share // 8, (share // 4) % 2, share % 4
    even = ((sh * 2 + 0) * 4 + sx) * 4 + sy
    odd = ((sh * 2 + 1) * 4 + sy) * 4 + sx
    meta_own[6:7, :] = jnp.where(index % 2 == 0, even, odd)

    pl.semaphore_wait(barrier, len(friends))

    points_out = remote(tp, tp_in, p_send.at[0], p_recv.at[0], sibling)
    sp_copy = remote(sp, sp_in, p_send.at[1], p_recv.at[1], partner)
    meta_copy = remote(meta_own, meta_in, p_send.at[2], p_recv.at[2], partner)
    tm_copy = remote(tm, tm_in, p_send.at[3], p_recv.at[3], partner)

    @pl.when(own_role)
    def _():
        points_out.start()
        sp_in[...] = sp[...]
        tp_in[...] = tp[...]
        tm_in[...] = tm[...]
        meta_in[...] = meta_own[...]

    @pl.when(swapped)
    def _():
        meta_copy.start()
        sp_copy.start()

    def source_copy(it, step):
        return remote(
            src_own.at[it], s_band.at[it, pl.ds(2 * row, 2)],
            s_send.at[step], s_recv.at[it, row], device(x, y, (z + step) % 4, z_hi),
        )

    def source_send(it):
        for step in (1, 2, 3):
            source_copy(it, step).start()

        @pl.when(swapped)
        def _():
            source_copy(it, 0).start()

        @pl.when(own_role)
        def _():
            s_band[it, pl.ds(2 * row, 2)] = src_own[it]

    def source_sent(it):
        for step in (1, 2, 3):
            source_copy(it, step).wait_send()

        @pl.when(swapped)
        def _():
            source_copy(it, 0).wait_send()

    def source_arrived(it):
        for r in range(4):
            @pl.when(jnp.logical_or(swapped, row != r))
            def _():
                remote(src_own.at[it], s_band.at[it, 2 * r:2 * r + 2], s_send.at[0],
                       s_recv.at[it, r], sibling).wait_recv()

    for k in range(2):
        src_own[0, k] = sd[k * tile:(k + 1) * tile, :].astype(F32).T.astype(BF16)
    source_send(0)

    @pl.when(swapped)
    def _():
        tm_copy.start()
        meta_copy.wait_recv()
        sp_copy.wait_recv()
        points_out.wait_recv()

    to_scalar = pltpu.make_async_copy(meta_in, meta, m_sem)
    to_scalar.start()

    @pl.loop(0, 8)
    def _(c):
        start = pl.multiple_of(c * tile, tile)
        for k in range(3):
            line = sp_in[k:k + 1, pl.ds(start, tile)]
            sb[c, k] = jnp.broadcast_to(line, (128, tile)).T

    @pl.loop(0, 64)
    def _(r):
        tt[r, 0:3] = tp_in[:, pl.ds(pl.multiple_of(r * tile, tile), tile)]

    to_scalar.wait()

    @pl.loop(0, slots)
    def _(s):
        r, c = meta[0, s], meta[1, s]
        for part_at in range(tile // 128):
            lanes = slice(part_at * 128, (part_at + 1) * 128)
            distance = (sb[c, 0] - tt[r, 0:1, lanes]) ** 2
            distance = distance + (sb[c, 1] - tt[r, 1:2, lanes]) ** 2
            distance = distance + (sb[c, 2] - tt[r, 2:3, lanes]) ** 2
            weight = jnp.exp(distance * -5.0) * (1.0 / 256.0)
            kt[s, :, part_at * 128:(part_at + 1) * 128] = weight.astype(BF16)

    acc[slots] = jnp.zeros((measures, tile), F32)

    @pl.when(swapped)
    def _():
        tm_copy.wait_recv()

    def total(a, g, u, h):
        gx, gy = (g, u) if a == 0 else (u, g)
        return acc[meta[4, 2 * (gx * 8 + h * 4 + gy) + a]]

    def write_block(ref, n, value):
        rows = value(0).shape[0]
        line = lax.broadcasted_iota(I32, (16, tile), 0)

        def piece(i, refs):
            code, ref_row = encode(value(i))
            ref[pl.ds(pl.multiple_of(i * rows, 16), rows), :] = code
            return jnp.where(line == i, ref_row, refs)

        refs = lax.fori_loop(0, n, piece, jnp.zeros((16, tile), I32))
        ref[n * rows:n * rows + 16, :] = refs.astype(I16)

    def read_block(ref, n, rows, i):
        refs = ref[n * rows:n * rows + 16, :].astype(I32)
        line = lax.broadcasted_iota(I32, (16, tile), 0)
        ref_row = jnp.sum(jnp.where(line == i, refs, 0), axis=0, keepdims=True)
        return decode(ref[pl.ds(pl.multiple_of(i * rows, 16), rows), :], ref_row)

    def iteration(it, _):
        source_arrived(it)

        @pl.loop(0, slots // 2)
        def _(pair):
            products = [
                jnp.dot(s_band[it, meta[1, 2 * pair + m]], kt[2 * pair + m],
                        preferred_element_type=F32)
                for m in range(2)
            ]
            for m in range(2):
                acc[2 * pair + m] = products[m] + acc[meta[2, 2 * pair + m]]

        def x0_copy(a, d):
            return remote(x0_send.at[a, d], x0_recv.at[a, d], x_send.at[a, d],
                          x_recv.at[it, a, d], sibling)

        place = ((x, y), (y, x))
        for d in (2, 1, 3, 0):
            for a in range(2):
                p, _q = place[a]

                @pl.loop(0, 4)
                def _(u):
                    x0_send[a, d, u] = total(a, (p + d) % 4, u, other)

                x0_copy(a, d).start()

        def own(a, d, u):
            return total(a, (place[a][0] + d) % 4, u, core) + x0_recv[a, d, u]

        def r1_copy(a, kind):
            return remote(r1_send.at[a, kind], r1_recv.at[it, a, kind], a_send.at[a, kind],
                          a_recv.at[it, a, kind], on_ring(a, 1 if kind % 2 == 0 else 3))

        for a in range(2):
            x0_copy(a, 2).wait_recv()
            for kind, d, u0 in ((0, 2, 0), (1, 2, 2)):
                write_block(r1_send.at[a, kind], 2, lambda i: own(a, d, u0 + i))
                r1_copy(a, kind).start()
        for a in range(2):
            for kind, d, u0 in ((2, 1, 2), (3, 3, 0)):
                x0_copy(a, d).wait_recv()
                write_block(r1_send.at[a, kind], 2, lambda i: own(a, d, u0 + i))
                r1_copy(a, kind).start()
        for a in range(2):
            for kind, d, u0 in ((4, 1, 0), (5, 3, 2)):
                r1_copy(a, kind - 4).wait_recv()
                got = r1_recv.at[it, a, kind - 4]
                write_block(r1_send.at[a, kind], 2,
                            lambda i: own(a, d, u0 + i) + read_block(got, 2, measures, i))
                r1_copy(a, kind).start()
        for a in range(2):
            x0_copy(a, 0).wait_recv()
            r1_copy(a, 2).wait_recv()
            r1_copy(a, 3).wait_recv()

            @pl.loop(0, 2)
            def _(i):
                part[a, i] = own(a, 0, i) + read_block(r1_recv.at[it, a, 3], 2, measures, i)
                part[a, 2 + i] = own(a, 0, 2 + i) + read_block(
                    r1_recv.at[it, a, 2], 2, measures, i)

            r1_copy(a, 4).wait_recv()
            r1_copy(a, 5).wait_recv()

            @pl.loop(0, 2)
            def _(i):
                part[a, i] += read_block(r1_recv.at[it, a, 4], 2, measures, i)
                part[a, 2 + i] += read_block(r1_recv.at[it, a, 5], 2, measures, i)

        def r2_copy(a, kind):
            return remote(r2_send.at[a, kind], r2_recv.at[it, a, kind], b_send.at[a, kind],
                          b_recv.at[it, a, kind], on_ring(1 - a, 1 if kind % 2 == 0 else 3))

        lower, upper = slice(0, half), slice(half, measures)
        for a in range(2):
            q = place[a][1]
            for kind, d, side in ((0, 2, lower), (1, 2, upper), (2, 1, upper), (3, 3, lower)):
                write_block(r2_send.at[a, kind], 1, lambda i: part[a, (q + d) % 4, side])
                r2_copy(a, kind).start()
        for a in range(2):
            q = place[a][1]
            for kind, d, side in ((4, 1, lower), (5, 3, upper)):
                r2_copy(a, kind - 4).wait_recv()
                got = r2_recv.at[it, a, kind - 4]
                write_block(r2_send.at[a, kind], 1,
                            lambda i: part[a, (q + d) % 4, side] + read_block(got, 1, half, 0))
                r2_copy(a, kind).start()

        def spot(a, g, u):
            return ((core * 2 + a) * 4 + g) * 4 + u

        def q_copy(a, kind):
            p, q = place[a]
            u = (q, q, (q + 3) % 4, (q + 1) % 4)[kind]
            rows = (slice(0, measures), slice(0, measures), lower, upper)[kind]
            ref = t_band.at[it, spot(a, p, u), rows]
            return remote(ref, ref, q_send.at[a, kind], q_recv.at[it, a, kind],
                          on_ring(1 - a, 1 if kind % 2 == 0 else 3))

        def q_got(a, kind):
            p, q = place[a]
            u = ((q + 3) % 4, (q + 1) % 4, (q + 2) % 4, (q + 2) % 4)[kind]
            rows = (slice(0, measures), slice(0, measures), lower, upper)[kind]
            ref = t_band.at[it, spot(a, p, u), rows]
            return remote(ref, ref, q_send.at[a, kind], q_recv.at[it, a, kind], sibling)

        def g_copy(a, du, kind):
            p, q = place[a]
            relay_up = du < 2
            g = p if kind < 2 else ((p + 3) % 4 if relay_up else (p + 1) % 4)
            ref = t_band.at[it, spot(a, g, (q + du) % 4)]
            up = kind == 0 or (kind == 2 and relay_up)
            return remote(ref, ref, g_send.at[a, du, kind], g_recv.at[it, a, du, kind],
                          on_ring(a, 1 if up else 3))

        def g_got(a, du, kind):
            p, q = place[a]
            g = ((p + 3) % 4, (p + 1) % 4, (p + 2) % 4)[kind]
            ref = t_band.at[it, spot(a, g, (q + du) % 4)]
            return remote(ref, ref, g_send.at[a, du, kind], g_recv.at[it, a, du, kind], sibling)

        def c_copy(a, dg):
            ref = t_band.at[it, pl.ds(spot(a, (place[a][0] + dg) % 4, 0), 4)]
            return remote(ref, ref, c_send.at[a, dg], c_recv.at[it, a, dg], sibling)

        def c_got(a, dg):
            base = ((other * 2 + a) * 4 + (place[a][0] + dg) % 4) * 4
            ref = t_band.at[it, pl.ds(base, 4)]
            return remote(ref, ref, c_send.at[a, dg], c_recv.at[it, a, dg], sibling)

        for a in range(2):
            p, q = place[a]
            r2_copy(a, 2).wait_recv()
            r2_copy(a, 3).wait_recv()
            r2_copy(a, 4).wait_recv()
            r2_copy(a, 5).wait_recv()
            got = [read_block(r2_recv.at[it, a, kind], 1, half, 0) for kind in (3, 4, 2, 5)]
            part[a, q, lower] += got[0] + got[1]
            part[a, q, upper] += got[2] + got[3]
            mass = tm_in[a * tile:(a + 1) * tile, :].T
            dual = mass / part[a, q]
            t_band[it, spot(a, p, q)] = dual.astype(BF16)
            q_copy(a, 0).start()
            q_copy(a, 1).start()
            g_copy(a, 0, 0).start()
            g_copy(a, 0, 1).start()

            @pl.when(it == ITERS - 1)
            def _():
                td_own[a * tile:(a + 1) * tile, :] = dual.T

        for a in range(2):
            q_got(a, 0).wait_recv()
            q_copy(a, 2).start()
            g_copy(a, 3, 0).start()
            g_copy(a, 3, 1).start()
            q_got(a, 1).wait_recv()
            q_copy(a, 3).start()
            g_copy(a, 1, 0).start()
            g_copy(a, 1, 1).start()
        for a in range(2):
            g_got(a, 0, 0).wait_recv()
            g_copy(a, 0, 2).start()
            g_got(a, 0, 1).wait_recv()
            q_got(a, 2).wait_recv()
            q_got(a, 3).wait_recv()
            g_copy(a, 2, 0).start()
            g_copy(a, 2, 1).start()
            c_copy(a, 0).start()
        for a in range(2):
            g_got(a, 3, 1).wait_recv()
            g_copy(a, 3, 2).start()
            g_got(a, 1, 0).wait_recv()
            g_copy(a, 1, 2).start()
            g_got(a, 3, 0).wait_recv()
            g_got(a, 1, 1).wait_recv()
            g_got(a, 2, 1).wait_recv()
            g_copy(a, 2, 2).start()
            g_got(a, 2, 0).wait_recv()
            c_copy(a, 3).start()
            c_copy(a, 1).start()
        for a in range(2):
            for du in range(4):
                g_got(a, du, 2).wait_recv()
            c_copy(a, 2).start()
        for dg in (0, 3, 1, 2):
            for a in range(2):
                c_got(a, dg).wait_recv()

        out_copy = remote(td_own, td_out, o_send, o_recv, partner)

        @pl.when(it == ITERS - 1)
        def _():
            @pl.when(swapped)
            def _():
                out_copy.start()

            @pl.when(own_role)
            def _():
                td_out[...] = td_own[...]

        @pl.loop(0, slots // 2)
        def _(pair):
            products = [
                lax.dot_general(t_band[it, meta[6, 2 * pair + m]], kt[2 * pair + m],
                                (((1,), (1,)), ((), ())), preferred_element_type=F32)
                for m in range(2)
            ]
            for m in range(2):
                acc[2 * pair + m] = products[m] + acc[meta[3, 2 * pair + m]]

        def z_copy(r):
            return remote(z_send.at[r], z_recv.at[it, z], w_send.at[r], w_recv.at[it, z],
                          device(x, y, core * 2 + r // 2, r % 2))

        for r in range(4):
            write_block(z_send.at[r], 2, lambda i: acc[meta[5, 2 * r + i]])

            @pl.when(jnp.logical_or(swapped, row != r))
            def _():
                z_copy(r).start()

            @pl.when(jnp.logical_and(own_role, row == r))
            def _():
                z_recv[it, z] = z_send[r]

        for from_z in range(4):
            @pl.when(jnp.logical_or(swapped, z != from_z))
            def _():
                remote(z_send.at[0], z_recv.at[it, from_z], w_send.at[0],
                       w_recv.at[it, from_z], sibling).wait_recv()

        for k in range(2):
            sums = read_block(z_recv.at[it, 0], 2, measures, k)
            for from_z in range(1, 4):
                sums = sums + read_block(z_recv.at[it, from_z], 2, measures, k)
            dual = sm[k * tile:(k + 1) * tile, :].T / sums

            @pl.when(it < ITERS - 1)
            def _():
                src_own[1, k] = dual.astype(BF16)

            @pl.when(it == ITERS - 1)
            def _():
                so_out[k * tile:(k + 1) * tile, :] = dual.T

        source_sent(it)

        @pl.when(it < ITERS - 1)
        def _():
            source_send(1)

        for a in range(2):
            for d in range(4):
                x0_copy(a, d).wait_send()
            for kind in range(6):
                r1_copy(a, kind).wait_send()
                r2_copy(a, kind).wait_send()
            for kind in range(4):
                q_copy(a, kind).wait_send()
            for du in range(4):
                for kind in range(3):
                    g_copy(a, du, kind).wait_send()
                c_copy(a, du).wait_send()
        for r in range(4):
            @pl.when(jnp.logical_or(swapped, row != r))
            def _():
                z_copy(r).wait_send()
        return 0

    lax.fori_loop(0, ITERS, iteration, 0)

    @pl.when(own_role)
    def _():
        points_out.wait_send()

    @pl.when(swapped)
    def _():
        out_copy = remote(td_own, td_out, o_send, o_recv, partner)
        out_copy.wait()
        meta_copy.wait_send()
        sp_copy.wait_send()
        tm_copy.wait_send()


def local(target_points, source_points, target_mass, source_mass, start_dual,
          tile_row, tile_column, tile_count):
    slots = tile_row.shape[0]
    rows, measures = target_mass.shape
    tile = rows // 2
    half = measures // 2
    dma = pltpu.SemaphoreType.DMA
    vmem = pltpu.VMEM
    whole = pl.BlockSpec(memory_space=pltpu.VMEM)
    long_block, short_block = 2 * measures + 16, half + 16
    return pl.pallas_call(
        functools.partial(kernel, slots),
        out_shape=(
            jax.ShapeDtypeStruct((rows, measures), F32),
            jax.ShapeDtypeStruct((rows, measures), F32),
        ),
        in_specs=[whole] * 7 + [pl.BlockSpec(memory_space=pltpu.SMEM)],
        out_specs=(whole, whole),
        scratch_shapes=[
            vmem((8, 128), I32),
            vmem((8, 128), I32),
            pltpu.SMEM((8, 128), I32),
            vmem(target_points.shape, F32),
            vmem(source_points.shape, F32),
            vmem((rows, measures), F32),
            vmem((64, 8, tile), F32),
            vmem((8, 3, tile, 128), F32),
            vmem((slots, tile, tile), BF16),
            vmem((slots + 1, measures, tile), F32),
            vmem((ITERS, 2, measures, tile), BF16),
            vmem((ITERS, 8, measures, tile), BF16),
            vmem((2, 4, 4, measures, tile), F32),
            vmem((2, 4, 4, measures, tile), F32),
            vmem((2, 6, long_block, tile), I16),
            vmem((ITERS, 2, 6, long_block, tile), I16),
            vmem((2, 6, short_block, tile), I16),
            vmem((ITERS, 2, 6, short_block, tile), I16),
            vmem((2, 4, measures, tile), F32),
            vmem((ITERS, 64, measures, tile), BF16),
            vmem((4, long_block, tile), I16),
            vmem((ITERS, 4, long_block, tile), I16),
            vmem((rows, measures), F32),
            dma((4,)), dma((4,)),
            dma((4,)), dma((ITERS, 4)),
            dma((2, 4)), dma((ITERS, 2, 4)),
            dma((2, 6)), dma((ITERS, 2, 6)),
            dma((2, 6)), dma((ITERS, 2, 6)),
            dma((2, 4)), dma((ITERS, 2, 4)),
            dma((2, 4, 3)), dma((ITERS, 2, 4, 3)),
            dma((2, 4)), dma((ITERS, 2, 4)),
            dma((4,)), dma((ITERS, 4)),
            dma, dma, dma,
        ],
        compiler_params=pltpu.CompilerParams(
            collective_id=0, has_side_effects=True, vmem_limit_bytes=60 * 1024 * 1024
        ),
    )(target_points, source_points, target_mass, source_mass, start_dual,
      tile_row.reshape(1, slots), tile_column.reshape(1, slots), tile_count)


def solution(mesh):
    return jax.shard_map(
        local,
        mesh=mesh,
        in_specs=(
            P(None, "row"),
            P(None, "col"),
            P(("row", "col"), None),
            P(("col", "row"), None),
            P(("col", "row"), None),
            P(("row", "col")),
            P(("row", "col")),
            P(("row", "col")),
        ),
        out_specs=(P(("row", "col"), None), P(("col", "row"), None)),
        check_vma=False,
    )
```

```python
import functools

import jax
import jax.numpy as jnp
from jax import lax
from jax.experimental import pallas as pl
from jax.experimental.pallas import tpu as pltpu
from jax.sharding import PartitionSpec as P

MESH = pl.DeviceIdType.MESH
ITERS = 2
CHAINS = 2
LAG = 5.0
GROUP = 4
FINE = 2896.0
COARSE = 256.0
F32 = jnp.float32
BF16 = jnp.bfloat16
I16 = jnp.int16
I32 = jnp.int32


def encode(x):
    level = jnp.log(jnp.maximum(x, 1e-37))
    ref = (level[0:1] * COARSE + 32768.5).astype(I32) - 32768
    fine = (level - ref.astype(F32) * (1.0 / COARSE)) * FINE + 32768.5
    code = jnp.clip(fine, 0.5, 65535.0).astype(I32) - 32768
    return code.astype(I16), ref


def decode(code, ref):
    return jnp.exp(
        code.astype(I32).astype(F32) * (1.0 / FINE) + ref.astype(F32) * (1.0 / COARSE)
    )


def kernel(
    slots,
    tp, sp, tm, sm, sd, tr, tc, tn,
    td_out, so_out,
    meta_own, meta_in, meta, tp_in, sp_in, tm_in, tt, sb, kt, acc,
    src_own, s_band, x0_send, x0_recv, r1_send, r1_recv, r2_send, r2_recv, part,
    t_band, z_send, z_recv, td_own, t_mass, s_mass, t_all, s_all,
    p_send, p_recv, s_send, s_recv, x_send, x_recv, a_send, a_recv, b_send, b_recv,
    q_send, q_recv, g_send, g_recv, c_send, c_recv, w_send, w_recv, o_send, o_recv, m_sem,
):
    tile = kt.shape[1]
    mh = acc.shape[2]
    row = lax.axis_index("row")
    col = lax.axis_index("col")
    z_lo, core = row // 2, row % 2
    x, z_hi, y = col // 8, (col // 4) % 2, col % 4
    z = z_hi * 2 + z_lo
    other = 1 - core
    own_role = core == z_hi
    swapped = core != z_hi

    def device(x_, y_, z_, core_):
        return ((z_ % 2) * 2 + core_, x_ * 8 + (z_ // 2) * 4 + y_)

    sibling = device(x, y, z, other)
    partner = device(x, y, core * 2 + z_lo, z_hi)

    def on_ring(axis, step):
        if axis == 0:
            return device((x + step) % 4, y, z, core)
        return device(x, (y + step) % 4, z, core)

    def remote(src, dst, send, recv, target):
        return pltpu.make_async_remote_copy(
            src_ref=src, dst_ref=dst, send_sem=send, recv_sem=recv,
            device_id=target, device_id_type=MESH,
        )

    barrier = pltpu.get_barrier_semaphore()
    friends = [device(x, y, (z + dz) % 4, (core + dk) % 2)
               for dz in range(4) for dk in range(2) if dz or dk]
    friends += [on_ring(axis, step) for axis in (0, 1) for step in (1, 3)]
    for friend in friends:
        pl.semaphore_signal(barrier, inc=1, device_id=friend, device_id_type=MESH)

    meta_own[...] = jnp.zeros_like(meta_own)
    meta_own[0:1, 0:slots] = jnp.clip(tr[...], 0, 63)
    meta_own[1:2, 0:slots] = jnp.clip(tc[...], 0, 7)
    lane = lax.broadcasted_iota(I32, (128, 128), 1)
    sub = lax.broadcasted_iota(I32, (128, 128), 0)
    alive = sub < tn[0]
    for k in range(2):
        across = jnp.broadcast_to(meta_own[k:k + 1, :], (128, 128))
        down = across.T
        same = (down == across) & (sub < lane) & alive
        found = jnp.max(jnp.where(same, sub, -1), axis=0, keepdims=True)
        meta_own[2 + k:3 + k, :] = jnp.where(found < 0, slots, found)
        same = (down == lane) & alive
        found = jnp.max(jnp.where(same, sub, -1), axis=0, keepdims=True)
        meta_own[4 + k:5 + k, :] = jnp.where(found < 0, slots, found)
    index = meta_own[0:1, :]
    share = index // 2
    sx, sh, sy = share // 8, (share // 4) % 2, share % 4
    even = ((sh * 2 + 0) * 4 + sx) * 4 + sy
    odd = ((sh * 2 + 1) * 4 + sy) * 4 + sx
    meta_own[6:7, :] = jnp.where(index % 2 == 0, even, odd)

    pl.semaphore_wait(barrier, len(friends))

    points_out = remote(tp, tp_in, p_send.at[0], p_recv.at[0], sibling)
    sp_copy = remote(sp, sp_in, p_send.at[1], p_recv.at[1], partner)
    meta_copy = remote(meta_own, meta_in, p_send.at[2], p_recv.at[2], partner)
    tm_copy = remote(tm, tm_in, p_send.at[3], p_recv.at[3], partner)

    @pl.when(own_role)
    def _():
        points_out.start()
        sp_in[...] = sp[...]
        tp_in[...] = tp[...]
        tm_in[...] = tm[...]
        meta_in[...] = meta_own[...]

    @pl.when(swapped)
    def _():
        meta_copy.start()
        sp_copy.start()

    def source_copy(it, h, step):
        return remote(
            src_own.at[it, h], s_band[h].at[it, pl.ds(2 * row, 2)],
            s_send.at[h, step], s_recv.at[it, h, row], device(x, y, (z + step) % 4, z_hi),
        )

    def source_send(it, h):
        for step in (1, 2, 3):
            source_copy(it, h, step).start()

        @pl.when(swapped)
        def _():
            source_copy(it, h, 0).start()

        @pl.when(own_role)
        def _():
            s_band[h][it, pl.ds(2 * row, 2)] = src_own[it, h]

    def source_sent(it, h):
        for step in (1, 2, 3):
            source_copy(it, h, step).wait_send()

        @pl.when(swapped)
        def _():
            source_copy(it, h, 0).wait_send()

    def source_arrived(it, h):
        for r in range(4):
            @pl.when(jnp.logical_or(swapped, row != r))
            def _():
                remote(src_own.at[it, h], s_band[h].at[it, 2 * r:2 * r + 2], s_send.at[h, 0],
                       s_recv.at[it, h, r], sibling).wait_recv()

    for k in range(2):
        start_tile = sd[k * tile:(k + 1) * tile, :].astype(F32).T.astype(BF16)
        for h in range(CHAINS):
            src_own[0, h, k] = start_tile[h * mh:(h + 1) * mh]
    for h in range(CHAINS):
        source_send(0, h)

    @pl.when(swapped)
    def _():
        tm_copy.start()
        meta_copy.wait_recv()
        sp_copy.wait_recv()
        points_out.wait_recv()

    to_scalar = pltpu.make_async_copy(meta_in, meta, m_sem)
    to_scalar.start()

    @pl.loop(0, 8)
    def _(c):
        start = pl.multiple_of(c * tile, tile)
        for k in range(3):
            line = sp_in[k:k + 1, pl.ds(start, tile)]
            sb[c, k] = jnp.broadcast_to(line, (128, tile)).T

    @pl.loop(0, 64)
    def _(r):
        tt[r, 0:3] = tp_in[:, pl.ds(pl.multiple_of(r * tile, tile), tile)]

    to_scalar.wait()

    @pl.loop(0, slots)
    def _(s):
        r, c = meta[0, s], meta[1, s]
        for part_at in range(tile // 128):
            lanes = slice(part_at * 128, (part_at + 1) * 128)
            distance = (sb[c, 0] - tt[r, 0:1, lanes]) ** 2
            distance = distance + (sb[c, 1] - tt[r, 1:2, lanes]) ** 2
            distance = distance + (sb[c, 2] - tt[r, 2:3, lanes]) ** 2
            weight = jnp.exp(distance * -5.0) * (1.0 / 256.0)
            kt[s, :, part_at * 128:(part_at + 1) * 128] = weight.astype(BF16)

    for h in range(CHAINS):
        acc[h, slots] = jnp.zeros((mh, tile), F32)

    @pl.when(swapped)
    def _():
        tm_copy.wait_recv()

    for k in range(2):
        t_mass[k] = tm_in[k * tile:(k + 1) * tile, :].T
        s_mass[k] = sm[k * tile:(k + 1) * tile, :].T

    def write_block(ref, value):
        line = lax.broadcasted_iota(I32, (16, tile), 0)

        def piece(i, refs):
            code, ref_row = encode(value(i))
            ref[pl.ds(pl.multiple_of(i * mh, 16), mh), :] = code
            return jnp.where(line == i, ref_row, refs)

        refs = lax.fori_loop(0, 2, piece, jnp.zeros((16, tile), I32))
        ref[2 * mh:2 * mh + 16, :] = refs.astype(I16)

    def read_block(ref, i):
        refs = ref[2 * mh:2 * mh + 16, :].astype(I32)
        line = lax.broadcasted_iota(I32, (16, tile), 0)
        ref_row = jnp.sum(jnp.where(line == i, refs, 0), axis=0, keepdims=True)
        return decode(ref[pl.ds(pl.multiple_of(i * mh, 16), mh), :], ref_row)

    place = ((x, y), (y, x))
    half = mh // 2
    lower, upper, full = slice(0, half), slice(half, mh), slice(0, mh)
    out_copy = remote(td_own, td_out, o_send, o_recv, partner)

    class Chain:
        def __init__(self, h, it):
            self.h, self.it = h, it

        def x0_copy(self, a, d):
            h = self.h
            return remote(x0_send.at[h, a, d], x0_recv.at[h, a, d], x_send.at[h, a, d],
                          x_recv.at[self.it, h, a, d], sibling)

        def r1_copy(self, a, kind):
            h, it = self.h, self.it
            return remote(r1_send.at[h, a, kind], r1_recv.at[it, h, a, kind],
                          a_send.at[h, a, kind], a_recv.at[it, h, a, kind],
                          on_ring(a, 1 if kind % 2 == 0 else 3))

        def r2_copy(self, a, kind):
            h, it = self.h, self.it
            return remote(r2_send.at[h, a, kind], r2_recv.at[it, h, a, kind],
                          b_send.at[h, a, kind], b_recv.at[it, h, a, kind],
                          on_ring(1 - a, 1 if kind % 2 == 0 else 3))

        def spot(self, a, g, u):
            return ((core * 2 + a) * 4 + g) * 4 + u

        def q_copy(self, a, kind):
            p, q = place[a]
            u = (q, q, (q + 3) % 4, (q + 1) % 4)[kind]
            rows = (full, full, lower, upper)[kind]
            ref = t_band[self.h].at[self.it, self.spot(a, p, u), rows]
            return remote(ref, ref, q_send.at[self.h, a, kind],
                          q_recv.at[self.it, self.h, a, kind],
                          on_ring(1 - a, 1 if kind % 2 == 0 else 3))

        def q_got(self, a, kind):
            p, q = place[a]
            u = ((q + 3) % 4, (q + 1) % 4, (q + 2) % 4, (q + 2) % 4)[kind]
            rows = (full, full, lower, upper)[kind]
            ref = t_band[self.h].at[self.it, self.spot(a, p, u), rows]
            remote(ref, ref, q_send.at[self.h, a, kind],
                   q_recv.at[self.it, self.h, a, kind], sibling).wait_recv()

        def g_copy(self, a, du, kind):
            p, q = place[a]
            relay_up = du < 2
            g = p if kind < 2 else ((p + 3) % 4 if relay_up else (p + 1) % 4)
            ref = t_band[self.h].at[self.it, self.spot(a, g, (q + du) % 4)]
            up = kind == 0 or (kind == 2 and relay_up)
            return remote(ref, ref, g_send.at[self.h, a, du, kind],
                          g_recv.at[self.it, self.h, a, du, kind], on_ring(a, 1 if up else 3))

        def g_got(self, a, du, kind):
            p, q = place[a]
            g = ((p + 3) % 4, (p + 1) % 4, (p + 2) % 4)[kind]
            ref = t_band[self.h].at[self.it, self.spot(a, g, (q + du) % 4)]
            remote(ref, ref, g_send.at[self.h, a, du, kind],
                   g_recv.at[self.it, self.h, a, du, kind], sibling).wait_recv()

        def c_copy(self, a, dg):
            base = self.spot(a, (place[a][0] + dg) % 4, 0)
            ref = t_band[self.h].at[self.it, pl.ds(base, 4)]
            return remote(ref, ref, c_send.at[self.h, a, dg],
                          c_recv.at[self.it, self.h, a, dg], sibling)

        def c_got(self, a, dg):
            base = ((other * 2 + a) * 4 + (place[a][0] + dg) % 4) * 4
            ref = t_band[self.h].at[self.it, pl.ds(base, 4)]
            remote(ref, ref, c_send.at[self.h, a, dg],
                   c_recv.at[self.it, self.h, a, dg], sibling).wait_recv()

        def z_copy(self, r):
            return remote(z_send.at[self.h, r], z_recv.at[self.it, self.h, z],
                          w_send.at[self.h, r], w_recv.at[self.it, self.h, z],
                          device(x, y, core * 2 + r // 2, r % 2))

        def total(self, a, d, u, side):
            g = (place[a][0] + d) % 4
            gx, gy = (g, u) if a == 0 else (u, g)
            return acc[self.h, meta[4, 2 * (gx * 8 + side * 4 + gy) + a]]

        def own(self, a, d, u):
            return self.total(a, d, u, core) + x0_recv[self.h, a, d, u]

        def rows_product(self, begin, end):
            h, it = self.h, self.it

            @pl.loop(begin // GROUP, end // GROUP)
            def _(group):
                at = [group * GROUP + m for m in range(GROUP)]
                products = [jnp.dot(s_band[h][it, meta[1, s]], kt[s],
                                    preferred_element_type=F32) for s in at]
                for s, product in zip(at, products):
                    acc[h, s] = product + acc[h, meta[2, s]]

        def columns_product(self, begin, end):
            h, it = self.h, self.it

            @pl.loop(begin // GROUP, end // GROUP)
            def _(group):
                at = [group * GROUP + m for m in range(GROUP)]
                products = [lax.dot_general(t_band[h][it, meta[6, s]], kt[s],
                                            (((1,), (1,)), ((), ())),
                                            preferred_element_type=F32) for s in at]
                for s, product in zip(at, products):
                    acc[h, s] = product + acc[h, meta[3, s]]

        def rows_first(self):
            source_arrived(self.it, self.h)
            self.rows_product(0, slots // 2)

        def rows_second(self):
            self.rows_product(slots // 2, slots)

        def to_sibling(self):
            for d in (2, 1, 3, 0):
                for a in range(2):
                    @pl.loop(0, 4)
                    def _(u):
                        x0_send[self.h, a, d, u] = self.total(a, d, u, other)

                    self.x0_copy(a, d).start()

        def ring_far(self):
            for a in range(2):
                self.x0_copy(a, 2).wait_recv()
                for kind, d, u0 in ((0, 2, 0), (1, 2, 2)):
                    write_block(r1_send.at[self.h, a, kind], lambda i: self.own(a, d, u0 + i))
                    self.r1_copy(a, kind).start()

        def ring_near(self):
            for a in range(2):
                for kind, d, u0 in ((2, 1, 2), (3, 3, 0)):
                    self.x0_copy(a, d).wait_recv()
                    write_block(r1_send.at[self.h, a, kind], lambda i: self.own(a, d, u0 + i))
                    self.r1_copy(a, kind).start()

        def ring_relay(self):
            for a in range(2):
                for kind, d, u0 in ((4, 1, 0), (5, 3, 2)):
                    self.r1_copy(a, kind - 4).wait_recv()
                    got = r1_recv.at[self.it, self.h, a, kind - 4]
                    write_block(r1_send.at[self.h, a, kind],
                                lambda i: self.own(a, d, u0 + i) + read_block(got, i))
                    self.r1_copy(a, kind).start()

        def ring_sum(self):
            h, it = self.h, self.it
            for a in range(2):
                self.x0_copy(a, 0).wait_recv()
                self.r1_copy(a, 2).wait_recv()
                self.r1_copy(a, 3).wait_recv()

                @pl.loop(0, 2)
                def _(i):
                    part[h, a, i] = self.own(a, 0, i) + read_block(r1_recv.at[it, h, a, 3], i)
                    part[h, a, 2 + i] = self.own(a, 0, 2 + i) + read_block(
                        r1_recv.at[it, h, a, 2], i)

        def ring_total(self):
            h, it = self.h, self.it
            for a in range(2):
                q = place[a][1]
                self.r1_copy(a, 4).wait_recv()
                self.r1_copy(a, 5).wait_recv()

                @pl.loop(0, 2)
                def _(i):
                    part[h, a, i] += read_block(r1_recv.at[it, h, a, 4], i)
                    part[h, a, 2 + i] += read_block(r1_recv.at[it, h, a, 5], i)

                for kind, d, side in ((0, 2, lower), (1, 2, upper), (2, 1, upper), (3, 3, lower)):
                    r2_send[h, a, kind] = part[h, a, (q + d) % 4, side]
                    self.r2_copy(a, kind).start()

        def short_relay(self):
            h, it = self.h, self.it
            for a in range(2):
                q = place[a][1]
                for kind, d, side in ((4, 1, lower), (5, 3, upper)):
                    self.r2_copy(a, kind - 4).wait_recv()
                    r2_send[h, a, kind] = (part[h, a, (q + d) % 4, side]
                                           + r2_recv[it, h, a, kind - 4])
                    self.r2_copy(a, kind).start()

        def target(self):
            h, it = self.h, self.it
            for a in range(2):
                p, q = place[a]
                for kind in (2, 3, 4, 5):
                    self.r2_copy(a, kind).wait_recv()
                sums = part[h, a, q] + jnp.concatenate(
                    [r2_recv[it, h, a, 3] + r2_recv[it, h, a, 4],
                     r2_recv[it, h, a, 2] + r2_recv[it, h, a, 5]], axis=0)
                dual = t_mass[a, h * mh:(h + 1) * mh] / sums
                t_band[h][it, self.spot(a, p, q)] = dual.astype(BF16)
                self.q_copy(a, 0).start()
                self.q_copy(a, 1).start()
                self.g_copy(a, 0, 0).start()
                self.g_copy(a, 0, 1).start()
                t_all[a, h * mh:(h + 1) * mh] = dual

        def gather_near(self):
            for a in range(2):
                self.q_got(a, 0)
                self.q_copy(a, 2).start()
                self.g_copy(a, 3, 0).start()
                self.g_copy(a, 3, 1).start()
                self.q_got(a, 1)
                self.q_copy(a, 3).start()
                self.g_copy(a, 1, 0).start()
                self.g_copy(a, 1, 1).start()

        def gather_far(self):
            for a in range(2):
                self.g_got(a, 0, 0)
                self.g_copy(a, 0, 2).start()
                self.g_got(a, 0, 1)
                self.q_got(a, 2)
                self.q_got(a, 3)
                self.g_copy(a, 2, 0).start()
                self.g_copy(a, 2, 1).start()
                self.c_copy(a, 0).start()

        def gather_relay(self):
            for a in range(2):
                self.g_got(a, 3, 1)
                self.g_copy(a, 3, 2).start()
                self.g_got(a, 1, 0)
                self.g_copy(a, 1, 2).start()
                self.g_got(a, 3, 0)
                self.g_got(a, 1, 1)
                self.g_got(a, 2, 1)
                self.g_copy(a, 2, 2).start()
                self.g_got(a, 2, 0)
                self.c_copy(a, 3).start()
                self.c_copy(a, 1).start()

        def gather_last(self):
            for a in range(2):
                for du in range(4):
                    self.g_got(a, du, 2)
                self.c_copy(a, 2).start()

        def columns_first(self):
            for dg in (0, 3, 1, 2):
                for a in range(2):
                    self.c_got(a, dg)
            self.columns_product(0, slots // 2)

        def columns_second(self):
            self.columns_product(slots // 2, slots)

        def to_owner(self):
            h, it = self.h, self.it
            for r in range(4):
                write_block(z_send.at[h, r], lambda i: acc[h, meta[5, 2 * r + i]])

                @pl.when(jnp.logical_or(swapped, row != r))
                def _():
                    self.z_copy(r).start()

                @pl.when(jnp.logical_and(own_role, row == r))
                def _():
                    z_recv[it, h, z] = z_send[h, r]

        def source(self):
            h, it = self.h, self.it
            for from_z in range(4):
                @pl.when(jnp.logical_or(swapped, z != from_z))
                def _():
                    remote(z_send.at[h, 0], z_recv.at[it, h, from_z], w_send.at[h, 0],
                           w_recv.at[it, h, from_z], sibling).wait_recv()

            for k in range(2):
                sums = read_block(z_recv.at[it, h, 0], k)
                for from_z in range(1, 4):
                    sums = sums + read_block(z_recv.at[it, h, from_z], k)
                dual = s_mass[k, h * mh:(h + 1) * mh] / sums
                s_all[k, h * mh:(h + 1) * mh] = dual

                @pl.when(it < ITERS - 1)
                def _():
                    src_own[1, h, k] = dual.astype(BF16)

            source_sent(it, h)

            @pl.when(it < ITERS - 1)
            def _():
                source_send(1, h)

        def sent(self):
            h = self.h
            for a in range(2):
                for d in range(4):
                    self.x0_copy(a, d).wait_send()
                for kind in range(6):
                    self.r1_copy(a, kind).wait_send()
                    self.r2_copy(a, kind).wait_send()
                for kind in range(4):
                    self.q_copy(a, kind).wait_send()
                for du in range(4):
                    for kind in range(3):
                        self.g_copy(a, du, kind).wait_send()
                    self.c_copy(a, du).wait_send()
            for r in range(4):
                @pl.when(jnp.logical_or(swapped, row != r))
                def _():
                    self.z_copy(r).wait_send()

    moments = (
        (0.0, "rows_first"), (1.7, "rows_second"), (3.4, "to_sibling"), (5.5, "ring_far"),
        (6.2, "ring_near"), (8.3, "ring_relay"), (9.0, "ring_sum"), (11.0, "ring_total"),
        (13.0, "short_relay"), (14.5, "target"), (16.0, "gather_near"), (17.3, "gather_far"),
        (20.0, "gather_relay"), (22.0, "gather_last"), (23.5, "columns_first"),
        (25.0, "columns_second"), (26.7, "to_owner"), (32.0, "source"),
    )
    plan = sorted((moment + LAG * h, h, name) for moment, name in moments for h in range(CHAINS))

    def iteration(it, _):
        chains = [Chain(h, it) for h in range(CHAINS)]
        targets = 0
        for _moment, h, name in plan:
            getattr(chains[h], name)()
            if name == "target":
                targets += 1
                if targets == CHAINS:
                    @pl.when(it == ITERS - 1)
                    def _():
                        for a in range(2):
                            td_own[a * tile:(a + 1) * tile, :] = t_all[a].T

                        @pl.when(swapped)
                        def _():
                            out_copy.start()

                        @pl.when(own_role)
                        def _():
                            td_out[...] = td_own[...]

        for chain in chains:
            chain.sent()
        return 0

    lax.fori_loop(0, ITERS, iteration, 0)
    for k in range(2):
        so_out[k * tile:(k + 1) * tile, :] = s_all[k].T

    @pl.when(own_role)
    def _():
        points_out.wait_send()

    @pl.when(swapped)
    def _():
        out_copy.wait()
        meta_copy.wait_send()
        sp_copy.wait_send()
        tm_copy.wait_send()


def local(target_points, source_points, target_mass, source_mass, start_dual,
          tile_row, tile_column, tile_count):
    slots = tile_row.shape[0]
    rows, measures = target_mass.shape
    tile = rows // 2
    mh = measures // CHAINS
    dma = pltpu.SemaphoreType.DMA
    vmem = pltpu.VMEM
    whole = pl.BlockSpec(memory_space=pltpu.VMEM)
    block = 2 * mh + 16
    return pl.pallas_call(
        functools.partial(kernel, slots),
        out_shape=(
            jax.ShapeDtypeStruct((rows, measures), F32),
            jax.ShapeDtypeStruct((rows, measures), F32),
        ),
        in_specs=[whole] * 7 + [pl.BlockSpec(memory_space=pltpu.SMEM)],
        out_specs=(whole, whole),
        scratch_shapes=[
            vmem((8, 128), I32),
            vmem((8, 128), I32),
            pltpu.SMEM((8, 128), I32),
            vmem(target_points.shape, F32),
            vmem(source_points.shape, F32),
            vmem((rows, measures), F32),
            vmem((64, 8, tile), F32),
            vmem((8, 3, tile, 128), F32),
            vmem((slots, tile, tile), BF16),
            vmem((CHAINS, slots + 1, mh, tile), F32),
            vmem((ITERS, CHAINS, 2, mh, tile), BF16),
            [vmem((ITERS, 8, mh, tile), BF16)] * CHAINS,
            vmem((CHAINS, 2, 4, 4, mh, tile), F32),
            vmem((CHAINS, 2, 4, 4, mh, tile), F32),
            vmem((CHAINS, 2, 6, block, tile), I16),
            vmem((ITERS, CHAINS, 2, 6, block, tile), I16),
            vmem((CHAINS, 2, 6, mh // 2, tile), F32),
            vmem((ITERS, CHAINS, 2, 6, mh // 2, tile), F32),
            vmem((CHAINS, 2, 4, mh, tile), F32),
            [vmem((ITERS, 64, mh, tile), BF16)] * CHAINS,
            vmem((CHAINS, 4, block, tile), I16),
            vmem((ITERS, CHAINS, 4, block, tile), I16),
            vmem((rows, measures), F32),
            vmem((2, measures, tile), F32),
            vmem((2, measures, tile), F32),
            vmem((2, measures, tile), F32),
            vmem((2, measures, tile), F32),
            dma((4,)), dma((4,)),
            dma((CHAINS, 4)), dma((ITERS, CHAINS, 4)),
            dma((CHAINS, 2, 4)), dma((ITERS, CHAINS, 2, 4)),
            dma((CHAINS, 2, 6)), dma((ITERS, CHAINS, 2, 6)),
            dma((CHAINS, 2, 6)), dma((ITERS, CHAINS, 2, 6)),
            dma((CHAINS, 2, 4)), dma((ITERS, CHAINS, 2, 4)),
            dma((CHAINS, 2, 4, 3)), dma((ITERS, CHAINS, 2, 4, 3)),
            dma((CHAINS, 2, 4)), dma((ITERS, CHAINS, 2, 4)),
            dma((CHAINS, 4)), dma((ITERS, CHAINS, 4)),
            dma, dma, dma,
        ],
        compiler_params=pltpu.CompilerParams(
            collective_id=0, has_side_effects=True, vmem_limit_bytes=60 * 1024 * 1024
        ),
    )(target_points, source_points, target_mass, source_mass, start_dual,
      tile_row.reshape(1, slots), tile_column.reshape(1, slots), tile_count)


def solution(mesh):
    return jax.shard_map(
        local,
        mesh=mesh,
        in_specs=(
            P(None, "row"),
            P(None, "col"),
            P(("row", "col"), None),
            P(("col", "row"), None),
            P(("col", "row"), None),
            P(("row", "col")),
            P(("row", "col")),
            P(("row", "col")),
        ),
        out_specs=(P(("row", "col"), None), P(("col", "row"), None)),
        check_vma=False,
    )
```

```python
import functools

import jax
import jax.numpy as jnp
from jax import lax
from jax.experimental import pallas as pl
from jax.experimental.pallas import tpu as pltpu
from jax.sharding import PartitionSpec as P

MESH = pl.DeviceIdType.MESH
ITERS = 2
CHAINS = 1
LAG = 5.0
GROUP = 8
FINE = 2896.0
COARSE = 256.0
F32 = jnp.float32
BF16 = jnp.bfloat16
I16 = jnp.int16
I32 = jnp.int32


def encode(x):
    level = jnp.log(jnp.maximum(x, 1e-37))
    ref = (level[0:1] * COARSE + 32768.5).astype(I32) - 32768
    fine = (level - ref.astype(F32) * (1.0 / COARSE)) * FINE + 32768.5
    code = jnp.clip(fine, 0.5, 65535.0).astype(I32) - 32768
    return code.astype(I16), ref


def decode(code, ref):
    return jnp.exp(
        code.astype(I32).astype(F32) * (1.0 / FINE) + ref.astype(F32) * (1.0 / COARSE)
    )


def kernel(
    slots,
    tp, sp, tm, sm, sd, tr, tc, tn,
    td_out, so_out,
    meta_own, meta_in, meta, tp_in, sp_in, tm_in, tt, sb, kt, acc,
    src_own, s_band, x0_send, x0_recv, r1_send, r1_recv, r2_send, r2_recv, part,
    t_band, z_send, z_recv, td_own, t_mass, s_mass, t_all, s_all,
    p_send, p_recv, s_send, s_recv, x_send, x_recv, a_send, a_recv, b_send, b_recv,
    q_send, q_recv, g_send, g_recv, c_send, c_recv, w_send, w_recv, o_send, o_recv, m_sem,
):
    tile = kt.shape[1]
    mh = acc.shape[2]
    row = lax.axis_index("row")
    col = lax.axis_index("col")
    z_lo, core = row // 2, row % 2
    x, z_hi, y = col // 8, (col // 4) % 2, col % 4
    z = z_hi * 2 + z_lo
    other = 1 - core
    own_role = core == z_hi
    swapped = core != z_hi

    def device(x_, y_, z_, core_):
        return ((z_ % 2) * 2 + core_, x_ * 8 + (z_ // 2) * 4 + y_)

    sibling = device(x, y, z, other)
    partner = device(x, y, core * 2 + z_lo, z_hi)

    ring = {(0, step): device((x + step) % 4, y, z, core) for step in (1, 3)}
    ring.update({(1, step): device(x, (y + step) % 4, z, core) for step in (1, 3)})

    def on_ring(axis, step):
        return ring[axis, step]

    delta = (z + 4 - 2 * core) % 4

    def by_delta(*values):
        return jnp.where(delta < 2, jnp.where(delta == 0, values[0], values[1]),
                         jnp.where(delta == 2, values[2], values[3]))

    relayed, single = by_delta(2, 0, 3, 1), by_delta(3, 1, 2, 0)
    up_band = device(x, y, (z + 1) % 4, z_hi)
    down_band = device(x, y, (z + 3) % 4, z_hi)
    up_core = device(x, y, (z + 1) % 4, core)
    down_core = device(x, y, (z + 3) % 4, core)
    relay_step = by_delta(3, 1, 1, 3)
    relay_on = device(x, y, (z + relay_step) % 4, core)

    def owner(r):
        return device(x, y, core * 2 + r // 2, r % 2)

    def remote(src, dst, send, recv, target):
        return pltpu.make_async_remote_copy(
            src_ref=src, dst_ref=dst, send_sem=send, recv_sem=recv,
            device_id=target, device_id_type=MESH,
        )

    barrier = pltpu.get_barrier_semaphore()
    friends = [device(x, y, (z + dz) % 4, (core + dk) % 2)
               for dz in range(4) for dk in range(2) if dz or dk]
    friends += [on_ring(axis, step) for axis in (0, 1) for step in (1, 3)]
    for friend in friends:
        pl.semaphore_signal(barrier, inc=1, device_id=friend, device_id_type=MESH)

    meta_own[...] = jnp.zeros_like(meta_own)
    meta_own[0:1, 0:slots] = jnp.clip(tr[...], 0, 63)
    meta_own[1:2, 0:slots] = jnp.clip(tc[...], 0, 7)
    lane = lax.broadcasted_iota(I32, (128, 128), 1)
    sub = lax.broadcasted_iota(I32, (128, 128), 0)
    alive = sub < tn[0]
    for k in range(2):
        across = jnp.broadcast_to(meta_own[k:k + 1, :], (128, 128))
        down = across.T
        same = (down == across) & (sub < lane) & alive
        found = jnp.max(jnp.where(same, sub, -1), axis=0, keepdims=True)
        meta_own[2 + k:3 + k, :] = jnp.where(found < 0, slots, found)
        same = (down == lane) & alive
        found = jnp.max(jnp.where(same, sub, -1), axis=0, keepdims=True)
        meta_own[4 + k:5 + k, :] = jnp.where(found < 0, slots, found)
    index = meta_own[0:1, :]
    share = index // 2
    sx, sh, sy = share // 8, (share // 4) % 2, share % 4
    even = ((sh * 2 + 0) * 4 + sx) * 4 + sy
    odd = ((sh * 2 + 1) * 4 + sy) * 4 + sx
    meta_own[6:7, :] = jnp.where(index % 2 == 0, even, odd)

    pl.semaphore_wait(barrier, len(friends))

    points_out = remote(tp, tp_in, p_send.at[0], p_recv.at[0], sibling)
    sp_copy = remote(sp, sp_in, p_send.at[1], p_recv.at[1], partner)
    meta_copy = remote(meta_own, meta_in, p_send.at[2], p_recv.at[2], partner)
    tm_copy = remote(tm, tm_in, p_send.at[3], p_recv.at[3], partner)

    @pl.when(own_role)
    def _():
        points_out.start()
        sp_in[...] = sp[...]
        tp_in[...] = tp[...]
        tm_in[...] = tm[...]
        meta_in[...] = meta_own[...]

    @pl.when(swapped)
    def _():
        meta_copy.start()
        sp_copy.start()

    def source_copy(it, h, step):
        target = (sibling, up_band, None, down_band)[step]
        return remote(
            src_own.at[it, h], s_band[h].at[it, pl.ds(2 * row, 2)],
            s_send.at[h, step], s_recv.at[it, h, row], target,
        )

    def source_relay(it, h):
        ref = s_band[h].at[it, pl.ds(2 * relayed, 2)]
        return remote(ref, ref, s_send.at[h, 2], s_recv.at[it, h, relayed], relay_on)

    def source_send(it, h):
        source_copy(it, h, 1).start()
        source_copy(it, h, 3).start()

        @pl.when(swapped)
        def _():
            source_copy(it, h, 0).start()

        @pl.when(own_role)
        def _():
            s_band[h][it, pl.ds(2 * row, 2)] = src_own[it, h]

    def source_sent(it, h):
        source_copy(it, h, 1).wait_send()
        source_copy(it, h, 3).wait_send()
        source_relay(it, h).wait_send()

        @pl.when(swapped)
        def _():
            source_copy(it, h, 0).wait_send()

    def source_pass_on(it, h):
        source_relay(it, h).wait_recv()
        source_relay(it, h).start()

    def source_arrived(it, h):
        for r in range(4):
            @pl.when(jnp.logical_and(jnp.logical_or(swapped, row != r), relayed != r))
            def _():
                remote(src_own.at[it, h], s_band[h].at[it, 2 * r:2 * r + 2], s_send.at[h, 0],
                       s_recv.at[it, h, r], sibling).wait_recv()

    for k in range(2):
        start_tile = sd[k * tile:(k + 1) * tile, :].astype(F32).T.astype(BF16)
        for h in range(CHAINS):
            src_own[0, h, k] = start_tile[h * mh:(h + 1) * mh]
    for h in range(CHAINS):
        source_send(0, h)

    for h in range(CHAINS):
        source_pass_on(0, h)

    @pl.when(swapped)
    def _():
        tm_copy.start()
        meta_copy.wait_recv()
        sp_copy.wait_recv()
        points_out.wait_recv()

    to_scalar = pltpu.make_async_copy(meta_in, meta, m_sem)
    to_scalar.start()

    @pl.loop(0, 8)
    def _(c):
        start = pl.multiple_of(c * tile, tile)
        for k in range(3):
            line = sp_in[k:k + 1, pl.ds(start, tile)]
            sb[c, k] = jnp.broadcast_to(line, (128, tile)).T

    @pl.loop(0, 64)
    def _(r):
        tt[r, 0:3] = tp_in[:, pl.ds(pl.multiple_of(r * tile, tile), tile)]

    to_scalar.wait()

    @pl.loop(0, slots)
    def _(s):
        r, c = meta[0, s], meta[1, s]
        for part_at in range(tile // 128):
            lanes = slice(part_at * 128, (part_at + 1) * 128)
            distance = (sb[c, 0] - tt[r, 0:1, lanes]) ** 2
            distance = distance + (sb[c, 1] - tt[r, 1:2, lanes]) ** 2
            distance = distance + (sb[c, 2] - tt[r, 2:3, lanes]) ** 2
            weight = jnp.exp(distance * -5.0) * (1.0 / 256.0)
            kt[s, :, part_at * 128:(part_at + 1) * 128] = weight.astype(BF16)

    for h in range(CHAINS):
        acc[h, slots] = jnp.zeros((mh, tile), F32)

    @pl.when(swapped)
    def _():
        tm_copy.wait_recv()

    for k in range(2):
        t_mass[k] = tm_in[k * tile:(k + 1) * tile, :].T
        s_mass[k] = sm[k * tile:(k + 1) * tile, :].T

    def write_block(ref, value):
        line = lax.broadcasted_iota(I32, (16, tile), 0)

        def piece(i, refs):
            code, ref_row = encode(value(i))
            ref[pl.ds(pl.multiple_of(i * mh, 16), mh), :] = code
            return jnp.where(line == i, ref_row, refs)

        refs = lax.fori_loop(0, 2, piece, jnp.zeros((16, tile), I32))
        ref[2 * mh:2 * mh + 16, :] = refs.astype(I16)

    def read_block(ref, i):
        refs = ref[2 * mh:2 * mh + 16, :].astype(I32)
        line = lax.broadcasted_iota(I32, (16, tile), 0)
        ref_row = jnp.sum(jnp.where(line == i, refs, 0), axis=0, keepdims=True)
        return decode(ref[pl.ds(pl.multiple_of(i * mh, 16), mh), :], ref_row)

    place = ((x, y), (y, x))
    half = mh // 2
    lower, upper, full = slice(0, half), slice(half, mh), slice(0, mh)
    out_copy = remote(td_own, td_out, o_send, o_recv, partner)

    class Chain:
        def __init__(self, h, it):
            self.h, self.it = h, it

        def x0_copy(self, a, d):
            h = self.h
            return remote(x0_send.at[h, a, d], x0_recv.at[h, a, d], x_send.at[h, a, d],
                          x_recv.at[self.it, h, a, d], sibling)

        def r1_copy(self, a, kind):
            h, it = self.h, self.it
            return remote(r1_send.at[h, a, kind], r1_recv.at[it, h, a, kind],
                          a_send.at[h, a, kind], a_recv.at[it, h, a, kind],
                          on_ring(a, 1 if kind % 2 == 0 else 3))

        def r2_copy(self, a, kind):
            h, it = self.h, self.it
            return remote(r2_send.at[h, a, kind], r2_recv.at[it, h, a, kind],
                          b_send.at[h, a, kind], b_recv.at[it, h, a, kind],
                          on_ring(1 - a, 1 if kind % 2 == 0 else 3))

        def spot(self, a, g, u):
            return ((core * 2 + a) * 4 + g) * 4 + u

        def q_copy(self, a, kind):
            p, q = place[a]
            u = (q, q, (q + 3) % 4, (q + 1) % 4)[kind]
            rows = (full, full, lower, upper)[kind]
            ref = t_band[self.h].at[self.it, self.spot(a, p, u), rows]
            return remote(ref, ref, q_send.at[self.h, a, kind],
                          q_recv.at[self.it, self.h, a, kind],
                          on_ring(1 - a, 1 if kind % 2 == 0 else 3))

        def q_got(self, a, kind):
            p, q = place[a]
            u = ((q + 3) % 4, (q + 1) % 4, (q + 2) % 4, (q + 2) % 4)[kind]
            rows = (full, full, lower, upper)[kind]
            ref = t_band[self.h].at[self.it, self.spot(a, p, u), rows]
            remote(ref, ref, q_send.at[self.h, a, kind],
                   q_recv.at[self.it, self.h, a, kind], sibling).wait_recv()

        def g_copy(self, a, du, kind):
            p, q = place[a]
            relay_up = du < 2
            g = p if kind < 2 else ((p + 3) % 4 if relay_up else (p + 1) % 4)
            ref = t_band[self.h].at[self.it, self.spot(a, g, (q + du) % 4)]
            up = kind == 0 or (kind == 2 and relay_up)
            return remote(ref, ref, g_send.at[self.h, a, du, kind],
                          g_recv.at[self.it, self.h, a, du, kind], on_ring(a, 1 if up else 3))

        def g_got(self, a, du, kind):
            p, q = place[a]
            g = ((p + 3) % 4, (p + 1) % 4, (p + 2) % 4)[kind]
            ref = t_band[self.h].at[self.it, self.spot(a, g, (q + du) % 4)]
            remote(ref, ref, g_send.at[self.h, a, du, kind],
                   g_recv.at[self.it, self.h, a, du, kind], sibling).wait_recv()

        def c_copy(self, a, dg):
            base = self.spot(a, (place[a][0] + dg) % 4, 0)
            ref = t_band[self.h].at[self.it, pl.ds(base, 4)]
            return remote(ref, ref, c_send.at[self.h, a, dg],
                          c_recv.at[self.it, self.h, a, dg], sibling)

        def c_got(self, a, dg):
            base = ((other * 2 + a) * 4 + (place[a][0] + dg) % 4) * 4
            ref = t_band[self.h].at[self.it, pl.ds(base, 4)]
            remote(ref, ref, c_send.at[self.h, a, dg],
                   c_recv.at[self.it, self.h, a, dg], sibling).wait_recv()

        def z_copy(self, kind, r):
            h, it = self.h, self.it
            return remote(z_send.at[h, r], z_recv.at[it, h, kind], w_send.at[h, r],
                          w_recv.at[it, h, kind], owner(r))

        def z_far(self, r, target):
            h, it = self.h, self.it
            return remote(z_send.at[h, r], z_recv.at[it, h, 3], w_send.at[h, r],
                          w_recv.at[it, h, 3], target)

        def to_next(self, r, fn):
            below = (core * 2 + r // 2 + 3) % 4 == z

            @pl.when(below)
            def _():
                fn(self.z_copy(1, r))

            @pl.when(jnp.logical_not(below))
            def _():
                fn(self.z_copy(2, r))

        def total(self, a, d, u, side):
            g = (place[a][0] + d) % 4
            gx, gy = (g, u) if a == 0 else (u, g)
            return acc[self.h, meta[4, 2 * (gx * 8 + side * 4 + gy) + a]]

        def own(self, a, d, u):
            return self.total(a, d, u, core) + x0_recv[self.h, a, d, u]

        def products(self, begin, end, one, link):
            h = self.h

            @pl.loop(begin // GROUP, end // GROUP)
            def _(group):
                for m in range(GROUP):
                    acc[h, group * GROUP + m] = one(group * GROUP + m)

            @pl.loop(begin // 4, end // 4)
            def _(group):
                for m in range(4):
                    s = group * 4 + m
                    acc[h, s] = acc[h, s] + acc[h, meta[link, s]]

        def rows_product(self, begin, end):
            h, it = self.h, self.it
            self.products(begin, end, lambda s: jnp.dot(
                s_band[h][it, meta[1, s]], kt[s], preferred_element_type=F32), 2)

        def columns_product(self, begin, end):
            h, it = self.h, self.it
            self.products(begin, end, lambda s: lax.dot_general(
                t_band[h][it, meta[6, s]], kt[s], (((1,), (1,)), ((), ())),
                preferred_element_type=F32), 3)

        def rows_first(self):
            source_arrived(self.it, self.h)
            self.rows_product(0, slots)

        def to_sibling(self):
            for d in (2, 1, 3, 0):
                for a in range(2):
                    @pl.loop(0, 4)
                    def _(u):
                        x0_send[self.h, a, d, u] = self.total(a, d, u, other)

                    self.x0_copy(a, d).start()

        def ring_far(self):
            for a in range(2):
                self.x0_copy(a, 2).wait_recv()
                for kind, d, u0 in ((0, 2, 0), (1, 2, 2)):
                    write_block(r1_send.at[self.h, a, kind], lambda i: self.own(a, d, u0 + i))
                    self.r1_copy(a, kind).start()

        def ring_near(self):
            for a in range(2):
                for kind, d, u0 in ((2, 1, 2), (3, 3, 0)):
                    self.x0_copy(a, d).wait_recv()
                    write_block(r1_send.at[self.h, a, kind], lambda i: self.own(a, d, u0 + i))
                    self.r1_copy(a, kind).start()

        def ring_relay(self):
            for a in range(2):
                for kind, d, u0 in ((4, 1, 0), (5, 3, 2)):
                    self.r1_copy(a, kind - 4).wait_recv()
                    got = r1_recv.at[self.it, self.h, a, kind - 4]
                    write_block(r1_send.at[self.h, a, kind],
                                lambda i: self.own(a, d, u0 + i) + read_block(got, i))
                    self.r1_copy(a, kind).start()

        def ring_sum(self):
            h, it = self.h, self.it
            for a in range(2):
                self.x0_copy(a, 0).wait_recv()
                self.r1_copy(a, 2).wait_recv()
                self.r1_copy(a, 3).wait_recv()

                @pl.loop(0, 2)
                def _(i):
                    part[h, a, i] = self.own(a, 0, i) + read_block(r1_recv.at[it, h, a, 3], i)
                    part[h, a, 2 + i] = self.own(a, 0, 2 + i) + read_block(
                        r1_recv.at[it, h, a, 2], i)

        def ring_total(self):
            h, it = self.h, self.it
            for a in range(2):
                q = place[a][1]
                self.r1_copy(a, 4).wait_recv()
                self.r1_copy(a, 5).wait_recv()

                @pl.loop(0, 2)
                def _(i):
                    part[h, a, i] += read_block(r1_recv.at[it, h, a, 4], i)
                    part[h, a, 2 + i] += read_block(r1_recv.at[it, h, a, 5], i)

                for kind, d, side in ((0, 2, lower), (1, 2, upper), (2, 1, upper), (3, 3, lower)):
                    r2_send[h, a, kind] = part[h, a, (q + d) % 4, side]
                    self.r2_copy(a, kind).start()

        def short_relay(self):
            h, it = self.h, self.it
            for a in range(2):
                q = place[a][1]
                for kind, d, side in ((4, 1, lower), (5, 3, upper)):
                    self.r2_copy(a, kind - 4).wait_recv()
                    r2_send[h, a, kind] = (part[h, a, (q + d) % 4, side]
                                           + r2_recv[it, h, a, kind - 4])
                    self.r2_copy(a, kind).start()

        def target(self):
            h, it = self.h, self.it
            for a in range(2):
                p, q = place[a]
                for kind in (2, 3, 4, 5):
                    self.r2_copy(a, kind).wait_recv()
                sums = part[h, a, q] + jnp.concatenate(
                    [r2_recv[it, h, a, 3] + r2_recv[it, h, a, 4],
                     r2_recv[it, h, a, 2] + r2_recv[it, h, a, 5]], axis=0)
                dual = t_mass[a, h * mh:(h + 1) * mh] / sums
                t_band[h][it, self.spot(a, p, q)] = dual.astype(BF16)
                self.q_copy(a, 0).start()
                self.q_copy(a, 1).start()
                self.g_copy(a, 0, 0).start()
                self.g_copy(a, 0, 1).start()
                t_all[a, h * mh:(h + 1) * mh] = dual

        def gather_near(self):
            for a in range(2):
                self.q_got(a, 0)
                self.q_copy(a, 2).start()
                self.g_copy(a, 3, 0).start()
                self.g_copy(a, 3, 1).start()
                self.q_got(a, 1)
                self.q_copy(a, 3).start()
                self.g_copy(a, 1, 0).start()
                self.g_copy(a, 1, 1).start()

        def gather_far(self):
            for a in range(2):
                self.g_got(a, 0, 0)
                self.g_copy(a, 0, 2).start()
                self.g_got(a, 0, 1)
                self.q_got(a, 2)
                self.q_got(a, 3)
                self.g_copy(a, 2, 0).start()
                self.g_copy(a, 2, 1).start()
                self.c_copy(a, 0).start()

        def gather_relay(self):
            for a in range(2):
                self.g_got(a, 3, 1)
                self.g_copy(a, 3, 2).start()
                self.g_got(a, 1, 0)
                self.g_copy(a, 1, 2).start()
                self.g_got(a, 3, 0)
                self.g_got(a, 1, 1)
                self.g_got(a, 2, 1)
                self.g_copy(a, 2, 2).start()
                self.g_got(a, 2, 0)
                self.c_copy(a, 3).start()
                self.c_copy(a, 1).start()

        def gather_last(self):
            for a in range(2):
                for du in range(4):
                    self.g_got(a, du, 2)
                self.c_copy(a, 2).start()

        def columns_first(self):
            for dg in (0, 3, 1, 2):
                for a in range(2):
                    self.c_got(a, dg)
            self.columns_product(0, slots)

        def to_owner(self):
            h, it = self.h, self.it
            first = 2 * (delta % 2)
            for at in range(2):
                r = first + at
                write_block(z_send.at[h, r], lambda i: acc[h, meta[5, 2 * r + i]])

                @pl.when(swapped)
                def _():
                    self.z_far(r, device(
                        x, y, (z + jnp.where((delta == 2) == (at == 0), 3, 1)) % 4, core)).start()

                @pl.when(jnp.logical_and(own_role, core != at))
                def _():
                    self.z_copy(0, r).start()

                @pl.when(jnp.logical_and(own_role, core == at))
                def _():
                    z_recv[it, h, 0] = z_send[h, r]

            write_block(z_send.at[h, single], lambda i: acc[h, meta[5, 2 * single + i]])
            self.to_next(single, lambda copy: copy.start())
            self.z_far(0, sibling).wait_recv()
            got = z_recv.at[it, h, 3]
            write_block(z_send.at[h, relayed],
                        lambda i: acc[h, meta[5, 2 * relayed + i]] + read_block(got, i))
            self.to_next(relayed, lambda copy: copy.start())

        def source(self):
            h, it = self.h, self.it
            for kind in range(3):
                @pl.when(jnp.logical_or(swapped, kind != 0))
                def _():
                    self.z_copy(kind, 0).wait_recv()

            for k in range(2):
                sums = read_block(z_recv.at[it, h, 0], k)
                for kind in (1, 2):
                    sums = sums + read_block(z_recv.at[it, h, kind], k)
                dual = s_mass[k, h * mh:(h + 1) * mh] / sums
                s_all[k, h * mh:(h + 1) * mh] = dual

                @pl.when(it < ITERS - 1)
                def _():
                    src_own[1, h, k] = dual.astype(BF16)

            source_sent(it, h)

            @pl.when(it < ITERS - 1)
            def _():
                source_send(1, h)
                source_pass_on(1, h)

        def sent(self):
            h = self.h
            for a in range(2):
                for d in range(4):
                    self.x0_copy(a, d).wait_send()
                for kind in range(6):
                    self.r1_copy(a, kind).wait_send()
                    self.r2_copy(a, kind).wait_send()
                for kind in range(4):
                    self.q_copy(a, kind).wait_send()
                for du in range(4):
                    for kind in range(3):
                        self.g_copy(a, du, kind).wait_send()
                    self.c_copy(a, du).wait_send()
            first = 2 * (delta % 2)
            for at in range(2):
                @pl.when(jnp.logical_or(swapped, core != at))
                def _():
                    self.z_far(first + at, sibling).wait_send()
            for r in (single, relayed):
                self.z_copy(1, r).wait_send()

    moments = (
        (0.0, "rows_first"), (3.4, "to_sibling"), (5.5, "ring_far"),
        (6.2, "ring_near"), (8.3, "ring_relay"), (9.0, "ring_sum"), (11.0, "ring_total"),
        (13.0, "short_relay"), (14.5, "target"), (16.0, "gather_near"), (17.3, "gather_far"),
        (20.0, "gather_relay"), (22.0, "gather_last"), (23.5, "columns_first"),
        (26.7, "to_owner"), (32.0, "source"),
    )
    plan = sorted((moment + LAG * h, h, name) for moment, name in moments for h in range(CHAINS))

    def iteration(it, _):
        chains = [Chain(h, it) for h in range(CHAINS)]
        targets = 0
        for _moment, h, name in plan:
            getattr(chains[h], name)()
            if name == "target":
                targets += 1
                if targets == CHAINS:
                    @pl.when(it == ITERS - 1)
                    def _():
                        for a in range(2):
                            td_own[a * tile:(a + 1) * tile, :] = t_all[a].T

                        @pl.when(swapped)
                        def _():
                            out_copy.start()

                        @pl.when(own_role)
                        def _():
                            td_out[...] = td_own[...]

        for chain in chains:
            chain.sent()
        return 0

    lax.fori_loop(0, ITERS, iteration, 0)
    for k in range(2):
        so_out[k * tile:(k + 1) * tile, :] = s_all[k].T

    @pl.when(own_role)
    def _():
        points_out.wait_send()

    @pl.when(swapped)
    def _():
        out_copy.wait()
        meta_copy.wait_send()
        sp_copy.wait_send()
        tm_copy.wait_send()


def local(target_points, source_points, target_mass, source_mass, start_dual,
          tile_row, tile_column, tile_count):
    slots = tile_row.shape[0]
    rows, measures = target_mass.shape
    tile = rows // 2
    mh = measures // CHAINS
    dma = pltpu.SemaphoreType.DMA
    vmem = pltpu.VMEM
    whole = pl.BlockSpec(memory_space=pltpu.VMEM)
    block = 2 * mh + 16
    return pl.pallas_call(
        functools.partial(kernel, slots),
        out_shape=(
            jax.ShapeDtypeStruct((rows, measures), F32),
            jax.ShapeDtypeStruct((rows, measures), F32),
        ),
        in_specs=[whole] * 7 + [pl.BlockSpec(memory_space=pltpu.SMEM)],
        out_specs=(whole, whole),
        scratch_shapes=[
            vmem((8, 128), I32),
            vmem((8, 128), I32),
            pltpu.SMEM((8, 128), I32),
            vmem(target_points.shape, F32),
            vmem(source_points.shape, F32),
            vmem((rows, measures), F32),
            vmem((64, 8, tile), F32),
            vmem((8, 3, tile, 128), F32),
            vmem((slots, tile, tile), BF16),
            vmem((CHAINS, slots + 1, mh, tile), F32),
            vmem((ITERS, CHAINS, 2, mh, tile), BF16),
            [vmem((ITERS, 8, mh, tile), BF16)] * CHAINS,
            vmem((CHAINS, 2, 4, 4, mh, tile), F32),
            vmem((CHAINS, 2, 4, 4, mh, tile), F32),
            vmem((CHAINS, 2, 6, block, tile), I16),
            vmem((ITERS, CHAINS, 2, 6, block, tile), I16),
            vmem((CHAINS, 2, 6, mh // 2, tile), F32),
            vmem((ITERS, CHAINS, 2, 6, mh // 2, tile), F32),
            vmem((CHAINS, 2, 4, mh, tile), F32),
            [vmem((ITERS, 64, mh, tile), BF16)] * CHAINS,
            vmem((CHAINS, 4, block, tile), I16),
            vmem((ITERS, CHAINS, 4, block, tile), I16),
            vmem((rows, measures), F32),
            vmem((2, measures, tile), F32),
            vmem((2, measures, tile), F32),
            vmem((2, measures, tile), F32),
            vmem((2, measures, tile), F32),
            dma((4,)), dma((4,)),
            dma((CHAINS, 4)), dma((ITERS, CHAINS, 4)),
            dma((CHAINS, 2, 4)), dma((ITERS, CHAINS, 2, 4)),
            dma((CHAINS, 2, 6)), dma((ITERS, CHAINS, 2, 6)),
            dma((CHAINS, 2, 6)), dma((ITERS, CHAINS, 2, 6)),
            dma((CHAINS, 2, 4)), dma((ITERS, CHAINS, 2, 4)),
            dma((CHAINS, 2, 4, 3)), dma((ITERS, CHAINS, 2, 4, 3)),
            dma((CHAINS, 2, 4)), dma((ITERS, CHAINS, 2, 4)),
            dma((CHAINS, 4)), dma((ITERS, CHAINS, 4)),
            dma, dma, dma,
        ],
        compiler_params=pltpu.CompilerParams(
            collective_id=0, has_side_effects=True, vmem_limit_bytes=60 * 1024 * 1024
        ),
    )(target_points, source_points, target_mass, source_mass, start_dual,
      tile_row.reshape(1, slots), tile_column.reshape(1, slots), tile_count)


def solution(mesh):
    return jax.shard_map(
        local,
        mesh=mesh,
        in_specs=(
            P(None, "row"),
            P(None, "col"),
            P(("row", "col"), None),
            P(("col", "row"), None),
            P(("col", "row"), None),
            P(("row", "col")),
            P(("row", "col")),
            P(("row", "col")),
        ),
        out_specs=(P(("row", "col"), None), P(("col", "row"), None)),
        check_vma=False,
    )
```

```python
import functools

import jax
import jax.numpy as jnp
from jax import lax
from jax.experimental import pallas as pl
from jax.experimental.pallas import tpu as pltpu
from jax.sharding import PartitionSpec as P

MESH = pl.DeviceIdType.MESH
ITERS = 2
CHAINS = 2
GROUP = 8
SCALE = 2.6857913
FINE = 2896.0
COARSE = 256.0
F32 = jnp.float32
BF16 = jnp.bfloat16
I16 = jnp.int16
I32 = jnp.int32


def encode(x):
    level = jnp.log(jnp.maximum(x, 1e-37))
    ref = (level[0:1] * COARSE + 32768.5).astype(I32) - 32768
    fine = (level - ref.astype(F32) * (1.0 / COARSE)) * FINE + 32768.5
    code = jnp.clip(fine, 0.5, 65535.0).astype(I32) - 32768
    return code.astype(I16), ref


def decode(code, ref):
    return jnp.exp(
        code.astype(I32).astype(F32) * (1.0 / FINE) + ref.astype(F32) * (1.0 / COARSE)
    )


def kernel(
    slots,
    tp, sp, tm, sm, sd, tr, tc, tn,
    td_out, so_out,
    meta_own, meta_in, meta, tp_in, sp_in, tm_in, tt, sb, kt, acc,
    src_own, s_band, x0_send, x0_recv, r1_send, r1_recv, r2_send, r2_recv, part,
    t_band, z_send, z_recv, td_own, t_mass, s_mass, t_all, s_all,
    p_send, p_recv, s_send, s_recv, x_send, x_recv, a_send, a_recv, b_send, b_recv,
    q_send, q_recv, g_send, g_recv, c_send, c_recv, w_send, w_recv, o_send, o_recv, m_sem,
):
    tile = kt.shape[1]
    measures = acc.shape[1]
    mh = measures // CHAINS
    row = lax.axis_index("row")
    col = lax.axis_index("col")
    z_lo, core = row // 2, row % 2
    x, z_hi, y = col // 8, (col // 4) % 2, col % 4
    z = z_hi * 2 + z_lo
    other = 1 - core
    own_role = core == z_hi
    swapped = core != z_hi

    def device(x_, y_, z_, core_):
        return ((z_ % 2) * 2 + core_, x_ * 8 + (z_ // 2) * 4 + y_)

    sibling = device(x, y, z, other)
    partner = device(x, y, core * 2 + z_lo, z_hi)

    ring = {(0, step): device((x + step) % 4, y, z, core) for step in (1, 3)}
    ring.update({(1, step): device(x, (y + step) % 4, z, core) for step in (1, 3)})

    def on_ring(axis, step):
        return ring[axis, step]

    delta = (z + 4 - 2 * core) % 4

    def by_delta(*values):
        return jnp.where(delta < 2, jnp.where(delta == 0, values[0], values[1]),
                         jnp.where(delta == 2, values[2], values[3]))

    relayed, single = by_delta(2, 0, 3, 1), by_delta(3, 1, 2, 0)
    up_band = device(x, y, (z + 1) % 4, z_hi)
    down_band = device(x, y, (z + 3) % 4, z_hi)
    up_core = device(x, y, (z + 1) % 4, core)
    down_core = device(x, y, (z + 3) % 4, core)
    relay_step = by_delta(3, 1, 1, 3)
    relay_on = device(x, y, (z + relay_step) % 4, core)

    def owner(r):
        return device(x, y, core * 2 + r // 2, r % 2)

    def remote(src, dst, send, recv, target):
        return pltpu.make_async_remote_copy(
            src_ref=src, dst_ref=dst, send_sem=send, recv_sem=recv,
            device_id=target, device_id_type=MESH,
        )

    barrier = pltpu.get_barrier_semaphore()
    friends = [device(x, y, (z + dz) % 4, (core + dk) % 2)
               for dz in range(4) for dk in range(2) if dz or dk]
    friends += [on_ring(axis, step) for axis in (0, 1) for step in (1, 3)]
    for friend in friends:
        pl.semaphore_signal(barrier, inc=1, device_id=friend, device_id_type=MESH)

    meta_own[...] = jnp.zeros_like(meta_own)
    meta_own[0:1, 0:slots] = jnp.clip(tr[...], 0, 63)
    meta_own[1:2, 0:slots] = jnp.clip(tc[...], 0, 7)
    lane = lax.broadcasted_iota(I32, (128, 128), 1)
    sub = lax.broadcasted_iota(I32, (128, 128), 0)
    alive = sub < tn[0]
    for k in range(2):
        across = jnp.broadcast_to(meta_own[k:k + 1, :], (128, 128))
        down = across.T
        same = (down == across) & (sub < lane) & alive
        found = jnp.max(jnp.where(same, sub, -1), axis=0, keepdims=True)
        meta_own[2 + k:3 + k, :] = jnp.where(found < 0, slots, found)
        same = (down == lane) & alive
        found = jnp.max(jnp.where(same, sub, -1), axis=0, keepdims=True)
        meta_own[4 + k:5 + k, :] = jnp.where(found < 0, slots, found)
    index = meta_own[0:1, :]
    share = index // 2
    sx, sh, sy = share // 8, (share // 4) % 2, share % 4
    even = ((sh * 2 + 0) * 4 + sx) * 4 + sy
    odd = ((sh * 2 + 1) * 4 + sy) * 4 + sx
    meta_own[6:7, :] = jnp.where(index % 2 == 0, even, odd)

    pl.semaphore_wait(barrier, len(friends))

    points_out = remote(tp, tp_in, p_send.at[0], p_recv.at[0], sibling)
    sp_copy = remote(sp, sp_in, p_send.at[1], p_recv.at[1], partner)
    meta_copy = remote(meta_own, meta_in, p_send.at[2], p_recv.at[2], partner)
    tm_copy = remote(tm, tm_in, p_send.at[3], p_recv.at[3], partner)

    @pl.when(own_role)
    def _():
        points_out.start()
        sp_in[...] = sp[...]
        tp_in[...] = tp[...]
        tm_in[...] = tm[...]
        meta_in[...] = meta_own[...]

    @pl.when(swapped)
    def _():
        meta_copy.start()
        sp_copy.start()

    def rows_of(h):
        return slice(h * mh, (h + 1) * mh)

    def source_copy(it, h, step):
        target = (sibling, up_band, None, down_band)[step]
        return remote(
            src_own.at[it, :, rows_of(h)], s_band.at[it, pl.ds(2 * row, 2), rows_of(h)],
            s_send.at[h, step], s_recv.at[it, h, row], target,
        )

    def source_relay(it, h):
        ref = s_band.at[it, pl.ds(2 * relayed, 2), rows_of(h)]
        return remote(ref, ref, s_send.at[h, 2], s_recv.at[it, h, relayed], relay_on)

    def source_send(it, h):
        source_copy(it, h, 1).start()
        source_copy(it, h, 3).start()

        @pl.when(swapped)
        def _():
            source_copy(it, h, 0).start()

        @pl.when(own_role)
        def _():
            s_band[it, pl.ds(2 * row, 2), rows_of(h)] = src_own[it, :, rows_of(h)]

    def source_sent(it, h):
        source_copy(it, h, 1).wait_send()
        source_copy(it, h, 3).wait_send()
        source_relay(it, h).wait_send()

        @pl.when(swapped)
        def _():
            source_copy(it, h, 0).wait_send()

    def source_pass_on(it, h):
        source_relay(it, h).wait_recv()
        source_relay(it, h).start()

    def source_arrived(it, h):
        for r in range(4):
            @pl.when(jnp.logical_and(jnp.logical_or(swapped, row != r), relayed != r))
            def _():
                remote(src_own.at[it, :, rows_of(h)],
                       s_band.at[it, 2 * r:2 * r + 2, rows_of(h)], s_send.at[h, 0],
                       s_recv.at[it, h, r], sibling).wait_recv()

    for k in range(2):
        src_own[0, k] = sd[k * tile:(k + 1) * tile, :].astype(F32).T.astype(BF16)
    for h in range(CHAINS):
        source_send(0, h)

    for h in range(CHAINS):
        source_pass_on(0, h)

    @pl.when(swapped)
    def _():
        tm_copy.start()
        meta_copy.wait_recv()
        sp_copy.wait_recv()
        points_out.wait_recv()

    to_scalar = pltpu.make_async_copy(meta_in, meta, m_sem)
    to_scalar.start()

    @pl.loop(0, 8)
    def _(c):
        start = pl.multiple_of(c * tile, tile)
        for k in range(3):
            line = sp_in[k:k + 1, pl.ds(start, tile)] * SCALE
            sb[c, k] = jnp.broadcast_to(line, (128, tile)).T

    @pl.loop(0, 64)
    def _(r):
        tt[r, 0:3] = tp_in[:, pl.ds(pl.multiple_of(r * tile, tile), tile)] * SCALE

    to_scalar.wait()

    @pl.loop(0, slots)
    def _(s):
        r, c = meta[0, s], meta[1, s]
        for part_at in range(tile // 128):
            lanes = slice(part_at * 128, (part_at + 1) * 128)
            distance = (sb[c, 0] - tt[r, 0:1, lanes]) ** 2
            distance = distance + (sb[c, 1] - tt[r, 1:2, lanes]) ** 2
            distance = distance + (sb[c, 2] - tt[r, 2:3, lanes]) ** 2
            weight = jnp.exp2(-8.0 - distance)
            kt[s, :, part_at * 128:(part_at + 1) * 128] = weight.astype(BF16)

    acc[slots] = jnp.zeros((measures, tile), F32)

    @pl.when(swapped)
    def _():
        tm_copy.wait_recv()

    for k in range(2):
        t_mass[k] = tm_in[k * tile:(k + 1) * tile, :].T
        s_mass[k] = sm[k * tile:(k + 1) * tile, :].T

    def write_block(ref, value):
        line = lax.broadcasted_iota(I32, (16, tile), 0)

        def piece(i, refs):
            code, ref_row = encode(value(i))
            ref[pl.ds(pl.multiple_of(i * mh, 16), mh), :] = code
            return jnp.where(line == i, ref_row, refs)

        refs = lax.fori_loop(0, 2, piece, jnp.zeros((16, tile), I32))
        ref[2 * mh:2 * mh + 16, :] = refs.astype(I16)

    def read_block(ref, i):
        refs = ref[2 * mh:2 * mh + 16, :].astype(I32)
        line = lax.broadcasted_iota(I32, (16, tile), 0)
        ref_row = jnp.sum(jnp.where(line == i, refs, 0), axis=0, keepdims=True)
        return decode(ref[pl.ds(pl.multiple_of(i * mh, 16), mh), :], ref_row)

    place = ((x, y), (y, x))
    half = mh // 2
    lower, upper, full = slice(0, half), slice(half, mh), slice(0, mh)
    out_copy = remote(td_own, td_out, o_send, o_recv, partner)

    def total(a, d, u, side):
        g = (place[a][0] + d) % 4
        gx, gy = (g, u) if a == 0 else (u, g)
        return meta[4, 2 * (gx * 8 + side * 4 + gy) + a]

    def products(one, link):
        @pl.loop(0, slots // GROUP)
        def _(group):
            for m in range(GROUP):
                s = group * GROUP + m
                acc[s] = one(s) + acc[meta[link, s]]

    class Chain:
        def __init__(self, h, it):
            self.h, self.it, self.rows = h, it, rows_of(h)

        def x0_copy(self, d):
            h = self.h
            return remote(x0_send.at[h, d], x0_recv.at[h, d], x_send.at[h, d],
                          x_recv.at[self.it, h, d], sibling)

        def r1_copy(self, a, kind):
            h, it = self.h, self.it
            return remote(r1_send.at[h, a, kind], r1_recv.at[it, h, a, kind],
                          a_send.at[h, a, kind], a_recv.at[it, h, a, kind],
                          on_ring(a, 1 if kind % 2 == 0 else 3))

        def r2_copy(self, a, kind):
            h, it = self.h, self.it
            return remote(r2_send.at[h, a, kind], r2_recv.at[it, h, a, kind],
                          b_send.at[h, a, kind], b_recv.at[it, h, a, kind],
                          on_ring(1 - a, 1 if kind % 2 == 0 else 3))

        def spot(self, a, g, u, side=None):
            return (((core if side is None else side) * 2 + a) * 4 + g) * 4 + u

        def some(self, kind):
            begin = self.h * mh
            return (self.rows, self.rows, slice(begin, begin + half),
                    slice(begin + half, begin + mh))[kind]

        def q_copy(self, a, kind):
            p, q = place[a]
            u = (q, q, (q + 3) % 4, (q + 1) % 4)[kind]
            ref = t_band.at[self.it, self.spot(a, p, u), self.some(kind)]
            return remote(ref, ref, q_send.at[self.h, a, kind],
                          q_recv.at[self.it, self.h, a, kind],
                          on_ring(1 - a, 1 if kind % 2 == 0 else 3))

        def q_got(self, a, kind):
            p, q = place[a]
            u = ((q + 3) % 4, (q + 1) % 4, (q + 2) % 4, (q + 2) % 4)[kind]
            ref = t_band.at[self.it, self.spot(a, p, u), self.some(kind)]
            remote(ref, ref, q_send.at[self.h, a, kind],
                   q_recv.at[self.it, self.h, a, kind], sibling).wait_recv()

        def pair(self, a, g, part_at):
            return t_band.at[self.it, pl.ds(self.spot(a, g, 2 * part_at), 2), self.rows]

        def g_copy(self, a, kind):
            p = place[a][0]
            g = (p, p, p, p, (p + 3) % 4, (p + 1) % 4)[kind]
            ref = self.pair(a, g, (0, 1, 0, 1, 0, 1)[kind])
            return remote(ref, ref, g_send.at[self.h, a, kind], g_recv.at[self.it, self.h, a, kind],
                          on_ring(a, (1, 1, 3, 3, 1, 3)[kind]))

        def g_got(self, a, kind):
            p = place[a][0]
            g = ((p + 3) % 4, (p + 3) % 4, (p + 1) % 4, (p + 1) % 4,
                 (p + 2) % 4, (p + 2) % 4)[kind]
            ref = self.pair(a, g, (0, 1, 0, 1, 0, 1)[kind])
            remote(ref, ref, g_send.at[self.h, a, kind], g_recv.at[self.it, self.h, a, kind],
                   sibling).wait_recv()

        def c_copy(self, a, dg):
            base = self.spot(a, (place[a][0] + dg) % 4, 0)
            ref = t_band.at[self.it, pl.ds(base, 4), self.rows]
            return remote(ref, ref, c_send.at[self.h, a, dg],
                          c_recv.at[self.it, self.h, a, dg], sibling)

        def c_got(self, a, dg):
            base = self.spot(a, (place[a][0] + dg) % 4, 0, other)
            ref = t_band.at[self.it, pl.ds(base, 4), self.rows]
            remote(ref, ref, c_send.at[self.h, a, dg],
                   c_recv.at[self.it, self.h, a, dg], sibling).wait_recv()

        def z_copy(self, kind, r):
            h, it = self.h, self.it
            return remote(z_send.at[h, r], z_recv.at[it, h, kind], w_send.at[h, r],
                          w_recv.at[it, h, kind], owner(r))

        def z_far(self, r, target):
            h, it = self.h, self.it
            return remote(z_send.at[h, r], z_recv.at[it, h, 3], w_send.at[h, r],
                          w_recv.at[it, h, 3], target)

        def to_next(self, r, fn):
            below = (core * 2 + r // 2 + 3) % 4 == z

            @pl.when(below)
            def _():
                fn(self.z_copy(1, r))

            @pl.when(jnp.logical_not(below))
            def _():
                fn(self.z_copy(2, r))

        def own(self, a, d, u):
            return acc[total(a, d, u, core), self.rows] + x0_recv[self.h, d, a, u]

        def stage(self, d):
            for a in range(2):
                @pl.loop(0, 4)
                def _(u):
                    x0_send[self.h, d, a, u] = acc[total(a, d, u, other), self.rows]

            self.x0_copy(d).start()

        def ring_far(self):
            self.x0_copy(2).wait_recv()
            for a in range(2):
                for kind, d, u0 in ((0, 2, 0), (1, 2, 2)):
                    write_block(r1_send.at[self.h, a, kind], lambda i: self.own(a, d, u0 + i))
                    self.r1_copy(a, kind).start()

        def ring_near(self):
            for kind, d, u0 in ((2, 1, 2), (3, 3, 0)):
                self.x0_copy(d).wait_recv()
                for a in range(2):
                    write_block(r1_send.at[self.h, a, kind], lambda i: self.own(a, d, u0 + i))
                    self.r1_copy(a, kind).start()

        def ring_relay(self):
            for a in range(2):
                for kind, d, u0 in ((4, 1, 0), (5, 3, 2)):
                    self.r1_copy(a, kind - 4).wait_recv()
                    got = r1_recv.at[self.it, self.h, a, kind - 4]
                    write_block(r1_send.at[self.h, a, kind],
                                lambda i: self.own(a, d, u0 + i) + read_block(got, i))
                    self.r1_copy(a, kind).start()

        def ring_sum(self):
            h, it = self.h, self.it
            self.x0_copy(0).wait_recv()
            for a in range(2):
                self.r1_copy(a, 2).wait_recv()
                self.r1_copy(a, 3).wait_recv()

                @pl.loop(0, 2)
                def _(i):
                    part[h, a, i] = self.own(a, 0, i) + read_block(r1_recv.at[it, h, a, 3], i)
                    part[h, a, 2 + i] = self.own(a, 0, 2 + i) + read_block(
                        r1_recv.at[it, h, a, 2], i)

        def ring_total(self):
            h, it = self.h, self.it
            for a in range(2):
                q = place[a][1]
                self.r1_copy(a, 4).wait_recv()
                self.r1_copy(a, 5).wait_recv()

                @pl.loop(0, 2)
                def _(i):
                    part[h, a, i] += read_block(r1_recv.at[it, h, a, 4], i)
                    part[h, a, 2 + i] += read_block(r1_recv.at[it, h, a, 5], i)

                for kind, d, side in ((0, 2, lower), (1, 2, upper), (2, 1, upper), (3, 3, lower)):
                    r2_send[h, a, kind] = part[h, a, (q + d) % 4, side]
                    self.r2_copy(a, kind).start()

        def short_relay(self):
            h, it = self.h, self.it
            for a in range(2):
                q = place[a][1]
                for kind, d, side in ((4, 1, lower), (5, 3, upper)):
                    self.r2_copy(a, kind - 4).wait_recv()
                    r2_send[h, a, kind] = (part[h, a, (q + d) % 4, side]
                                           + r2_recv[it, h, a, kind - 4])
                    self.r2_copy(a, kind).start()

        def target(self):
            h, it = self.h, self.it
            for a in range(2):
                p, q = place[a]
                for kind in (2, 3, 4, 5):
                    self.r2_copy(a, kind).wait_recv()
                sums = part[h, a, q] + jnp.concatenate(
                    [r2_recv[it, h, a, 3] + r2_recv[it, h, a, 4],
                     r2_recv[it, h, a, 2] + r2_recv[it, h, a, 5]], axis=0)
                dual = t_mass[a, self.rows] / sums
                t_band[it, self.spot(a, p, q), self.rows] = dual.astype(BF16)
                self.q_copy(a, 0).start()
                self.q_copy(a, 1).start()
                t_all[a, self.rows] = dual

        def gather_near(self):
            for a in range(2):
                self.q_got(a, 0)
                self.q_copy(a, 2).start()
                self.q_got(a, 1)
                self.q_copy(a, 3).start()

        def gather_block(self):
            for a in range(2):
                self.q_got(a, 2)
                self.q_got(a, 3)
                for kind in (0, 3, 1, 2):
                    self.g_copy(a, kind).start()
            for a in range(2):
                self.c_copy(a, 0).start()

        def gather_relay(self):
            for a in range(2):
                self.g_got(a, 0)
                self.g_copy(a, 4).start()
                self.g_got(a, 3)
                self.g_copy(a, 5).start()
            for a in range(2):
                self.g_got(a, 1)
                self.c_copy(a, 3).start()
                self.g_got(a, 2)
                self.c_copy(a, 1).start()

        def gather_last(self):
            for a in range(2):
                self.g_got(a, 4)
                self.g_got(a, 5)
                self.c_copy(a, 2).start()

        def gathered(self):
            for dg in (0, 3, 1, 2):
                for a in range(2):
                    self.c_got(a, dg)

        def to_owner(self):
            h, it = self.h, self.it
            first = 2 * (delta % 2)
            for at in range(2):
                r = first + at
                write_block(z_send.at[h, r], lambda i: acc[meta[5, 2 * r + i], self.rows])

                @pl.when(swapped)
                def _():
                    self.z_far(r, device(
                        x, y, (z + jnp.where((delta == 2) == (at == 0), 3, 1)) % 4, core)).start()

                @pl.when(jnp.logical_and(own_role, core != at))
                def _():
                    self.z_copy(0, r).start()

                @pl.when(jnp.logical_and(own_role, core == at))
                def _():
                    z_recv[it, h, 0] = z_send[h, r]

            write_block(z_send.at[h, single], lambda i: acc[meta[5, 2 * single + i], self.rows])
            self.to_next(single, lambda copy: copy.start())

        def to_owner_relay(self):
            h, it = self.h, self.it
            self.z_far(0, sibling).wait_recv()
            got = z_recv.at[it, h, 3]
            write_block(z_send.at[h, relayed],
                        lambda i: acc[meta[5, 2 * relayed + i], self.rows] + read_block(got, i))
            self.to_next(relayed, lambda copy: copy.start())

        def source(self):
            h, it = self.h, self.it
            for kind in range(3):
                @pl.when(jnp.logical_or(swapped, kind != 0))
                def _():
                    self.z_copy(kind, 0).wait_recv()

            for k in range(2):
                sums = read_block(z_recv.at[it, h, 0], k)
                for kind in (1, 2):
                    sums = sums + read_block(z_recv.at[it, h, kind], k)
                dual = s_mass[k, self.rows] / sums
                s_all[k, self.rows] = dual

                @pl.when(it < ITERS - 1)
                def _():
                    src_own[1, k, self.rows] = dual.astype(BF16)

            source_sent(it, h)

            @pl.when(it < ITERS - 1)
            def _():
                source_send(1, h)

        def sent(self):
            h = self.h
            for d in range(4):
                self.x0_copy(d).wait_send()
            for a in range(2):
                for kind in range(6):
                    self.r1_copy(a, kind).wait_send()
                    self.r2_copy(a, kind).wait_send()
                    self.g_copy(a, kind).wait_send()
                for kind in range(4):
                    self.q_copy(a, kind).wait_send()
                    self.c_copy(a, kind).wait_send()
            first = 2 * (delta % 2)
            for at in range(2):
                @pl.when(jnp.logical_or(swapped, core != at))
                def _():
                    self.z_far(first + at, sibling).wait_send()
            for r in (single, relayed):
                self.z_copy(1, r).wait_send()

    def iteration(it, _):
        chains = [Chain(h, it) for h in range(CHAINS)]
        for h in range(CHAINS):
            source_arrived(it, h)
        products(lambda s: jnp.dot(s_band[it, meta[1, s]], kt[s],
                                   preferred_element_type=F32), 2)
        for d in (2, 1, 3, 0):
            for chain in chains:
                chain.stage(d)
        for name in ("ring_far", "ring_near", "ring_relay", "ring_sum", "ring_total",
                     "short_relay", "target", "gather_near", "gather_block", "gather_relay",
                     "gather_last"):
            for chain in chains:
                getattr(chain, name)()

        @pl.when(it == ITERS - 1)
        def _():
            for a in range(2):
                td_own[a * tile:(a + 1) * tile, :] = t_all[a].T

            @pl.when(swapped)
            def _():
                out_copy.start()

            @pl.when(own_role)
            def _():
                td_out[...] = td_own[...]

        for chain in chains:
            chain.gathered()
        products(lambda s: lax.dot_general(t_band[it, meta[6, s]], kt[s],
                                           (((1,), (1,)), ((), ())),
                                           preferred_element_type=F32), 3)
        for name in ("to_owner", "to_owner_relay", "source"):
            for chain in chains:
                getattr(chain, name)()

        @pl.when(it < ITERS - 1)
        def _():
            for h in range(CHAINS):
                source_pass_on(1, h)

        for chain in chains:
            chain.sent()
        return 0

    lax.fori_loop(0, ITERS, iteration, 0)
    for k in range(2):
        so_out[k * tile:(k + 1) * tile, :] = s_all[k].T

    @pl.when(own_role)
    def _():
        points_out.wait_send()

    @pl.when(swapped)
    def _():
        out_copy.wait()
        meta_copy.wait_send()
        sp_copy.wait_send()
        tm_copy.wait_send()


def local(target_points, source_points, target_mass, source_mass, start_dual,
          tile_row, tile_column, tile_count):
    slots = tile_row.shape[0]
    rows, measures = target_mass.shape
    tile = rows // 2
    mh = measures // CHAINS
    dma = pltpu.SemaphoreType.DMA
    vmem = pltpu.VMEM
    whole = pl.BlockSpec(memory_space=pltpu.VMEM)
    block = 2 * mh + 16
    return pl.pallas_call(
        functools.partial(kernel, slots),
        out_shape=(
            jax.ShapeDtypeStruct((rows, measures), F32),
            jax.ShapeDtypeStruct((rows, measures), F32),
        ),
        in_specs=[whole] * 7 + [pl.BlockSpec(memory_space=pltpu.SMEM)],
        out_specs=(whole, whole),
        scratch_shapes=[
            vmem((8, 128), I32),
            vmem((8, 128), I32),
            pltpu.SMEM((8, 128), I32),
            vmem(target_points.shape, F32),
            vmem(source_points.shape, F32),
            vmem((rows, measures), F32),
            vmem((64, 8, tile), F32),
            vmem((8, 3, tile, 128), F32),
            vmem((slots, tile, tile), BF16),
            vmem((slots + 1, measures, tile), F32),
            vmem((ITERS, 2, measures, tile), BF16),
            vmem((ITERS, 8, measures, tile), BF16),
            vmem((CHAINS, 4, 2, 4, mh, tile), F32),
            vmem((CHAINS, 4, 2, 4, mh, tile), F32),
            vmem((CHAINS, 2, 6, block, tile), I16),
            vmem((ITERS, CHAINS, 2, 6, block, tile), I16),
            vmem((CHAINS, 2, 6, mh // 2, tile), F32),
            vmem((ITERS, CHAINS, 2, 6, mh // 2, tile), F32),
            vmem((CHAINS, 2, 4, mh, tile), F32),
            vmem((ITERS, 64, measures, tile), BF16),
            vmem((CHAINS, 4, block, tile), I16),
            vmem((ITERS, CHAINS, 4, block, tile), I16),
            vmem((rows, measures), F32),
            vmem((2, measures, tile), F32),
            vmem((2, measures, tile), F32),
            vmem((2, measures, tile), F32),
            vmem((2, measures, tile), F32),
            dma((4,)), dma((4,)),
            dma((CHAINS, 4)), dma((ITERS, CHAINS, 4)),
            dma((CHAINS, 4)), dma((ITERS, CHAINS, 4)),
            dma((CHAINS, 2, 6)), dma((ITERS, CHAINS, 2, 6)),
            dma((CHAINS, 2, 6)), dma((ITERS, CHAINS, 2, 6)),
            dma((CHAINS, 2, 4)), dma((ITERS, CHAINS, 2, 4)),
            dma((CHAINS, 2, 6)), dma((ITERS, CHAINS, 2, 6)),
            dma((CHAINS, 2, 4)), dma((ITERS, CHAINS, 2, 4)),
            dma((CHAINS, 4)), dma((ITERS, CHAINS, 4)),
            dma, dma, dma,
        ],
        compiler_params=pltpu.CompilerParams(
            collective_id=0, has_side_effects=True, vmem_limit_bytes=60 * 1024 * 1024
        ),
    )(target_points, source_points, target_mass, source_mass, start_dual,
      tile_row.reshape(1, slots), tile_column.reshape(1, slots), tile_count)


def solution(mesh):
    return jax.shard_map(
        local,
        mesh=mesh,
        in_specs=(
            P(None, "row"),
            P(None, "col"),
            P(("row", "col"), None),
            P(("col", "row"), None),
            P(("col", "row"), None),
            P(("row", "col")),
            P(("row", "col")),
            P(("row", "col")),
        ),
        out_specs=(P(("row", "col"), None), P(("col", "row"), None)),
        check_vma=False,
    )
```

```python
import functools

import jax
import jax.numpy as jnp
from jax import lax
from jax.experimental import pallas as pl
from jax.experimental.pallas import tpu as pltpu
from jax.sharding import PartitionSpec as P

MESH = pl.DeviceIdType.MESH
ITERS = 2
CHAINS = 2
GROUP = 16
SCALE = 2.6857913
FINE = 2896.0
COARSE = 256.0
F32 = jnp.float32
BF16 = jnp.bfloat16
I16 = jnp.int16
I32 = jnp.int32


def encode(x):
    level = jnp.log(jnp.maximum(x, 1e-37))
    ref = (level[0:1] * COARSE + 32768.5).astype(I32) - 32768
    fine = (level - ref.astype(F32) * (1.0 / COARSE)) * FINE + 32768.5
    code = jnp.clip(fine, 0.5, 65535.0).astype(I32) - 32768
    return code.astype(I16), ref


def decode(code, ref):
    return jnp.exp(
        code.astype(I32).astype(F32) * (1.0 / FINE) + ref.astype(F32) * (1.0 / COARSE)
    )


def kernel(
    slots,
    tp, sp, tm, sm, sd, tr, tc, tn,
    td_out, so_out,
    meta_own, meta_in, meta, tp_in, sp_in, tm_in, tt, sb, kt, acc,
    src_own, s_band, x0_send, x0_recv, r1_send, r1_recv, r2_send, r2_recv, part,
    t_band, z_send, z_recv, td_own, t_mass, s_mass, t_all, s_all,
    p_send, p_recv, s_send, s_recv, x_send, x_recv, a_send, a_recv, b_send, b_recv,
    q_send, q_recv, g_send, g_recv, c_send, c_recv, w_send, w_recv, o_send, o_recv, m_sem,
):
    tile = kt.shape[1]
    measures = acc.shape[1]
    mh = measures // CHAINS
    row = lax.axis_index("row")
    col = lax.axis_index("col")
    z_lo, core = row // 2, row % 2
    x, z_hi, y = col // 8, (col // 4) % 2, col % 4
    z = z_hi * 2 + z_lo
    other = 1 - core
    own_role = core == z_hi
    swapped = core != z_hi

    def device(x_, y_, z_, core_):
        return ((z_ % 2) * 2 + core_, x_ * 8 + (z_ // 2) * 4 + y_)

    sibling = device(x, y, z, other)
    partner = device(x, y, core * 2 + z_lo, z_hi)

    ring = {(0, step): device((x + step) % 4, y, z, core) for step in (1, 3)}
    ring.update({(1, step): device(x, (y + step) % 4, z, core) for step in (1, 3)})

    def on_ring(axis, step):
        return ring[axis, step]

    delta = (z + 4 - 2 * core) % 4

    def by_delta(*values):
        return jnp.where(delta < 2, jnp.where(delta == 0, values[0], values[1]),
                         jnp.where(delta == 2, values[2], values[3]))

    relayed, single = by_delta(2, 0, 3, 1), by_delta(3, 1, 2, 0)
    up_band = device(x, y, (z + 1) % 4, z_hi)
    down_band = device(x, y, (z + 3) % 4, z_hi)
    up_core = device(x, y, (z + 1) % 4, core)
    down_core = device(x, y, (z + 3) % 4, core)
    relay_step = by_delta(3, 1, 1, 3)
    relay_on = device(x, y, (z + relay_step) % 4, core)

    def owner(r):
        return device(x, y, core * 2 + r // 2, r % 2)

    def remote(src, dst, send, recv, target):
        return pltpu.make_async_remote_copy(
            src_ref=src, dst_ref=dst, send_sem=send, recv_sem=recv,
            device_id=target, device_id_type=MESH,
        )

    barrier = pltpu.get_barrier_semaphore()
    friends = [device(x, y, (z + dz) % 4, (core + dk) % 2)
               for dz in range(4) for dk in range(2) if dz or dk]
    friends += [on_ring(axis, step) for axis in (0, 1) for step in (1, 3)]
    for friend in friends:
        pl.semaphore_signal(barrier, inc=1, device_id=friend, device_id_type=MESH)

    meta_own[...] = jnp.zeros_like(meta_own)
    meta_own[0:1, 0:slots] = jnp.clip(tr[...], 0, 63)
    meta_own[1:2, 0:slots] = jnp.clip(tc[...], 0, 7)
    lane = lax.broadcasted_iota(I32, (128, 128), 1)
    sub = lax.broadcasted_iota(I32, (128, 128), 0)
    alive = sub < tn[0]
    for k in range(2):
        across = jnp.broadcast_to(meta_own[k:k + 1, :], (128, 128))
        down = across.T
        same = (down == across) & (sub < lane) & alive
        found = jnp.max(jnp.where(same, sub, -1), axis=0, keepdims=True)
        meta_own[2 + k:3 + k, :] = jnp.where(found < 0, slots, found)
        same = (down == lane) & alive
        found = jnp.max(jnp.where(same, sub, -1), axis=0, keepdims=True)
        meta_own[4 + k:5 + k, :] = jnp.where(found < 0, slots, found)
    index = meta_own[0:1, :]
    share = index // 2
    sx, sh, sy = share // 8, (share // 4) % 2, share % 4
    even = ((sh * 2 + 0) * 4 + sx) * 4 + sy
    odd = ((sh * 2 + 1) * 4 + sy) * 4 + sx
    meta_own[6:7, :] = jnp.where(index % 2 == 0, even, odd)

    for k in range(2):
        src_own[0, k] = sd[k * tile:(k + 1) * tile, :].astype(F32).T.astype(BF16)
        s_mass[k] = sm[k * tile:(k + 1) * tile, :].T

    pl.semaphore_wait(barrier, len(friends))

    points_out = remote(tp, tp_in, p_send.at[0], p_recv.at[0], sibling)
    sp_copy = remote(sp, sp_in, p_send.at[1], p_recv.at[1], partner)
    meta_copy = remote(meta_own, meta_in, p_send.at[2], p_recv.at[2], partner)
    tm_copy = remote(tm, tm_in, p_send.at[3], p_recv.at[3], partner)

    @pl.when(own_role)
    def _():
        points_out.start()
        sp_in[...] = sp[...]
        tp_in[...] = tp[...]
        tm_in[...] = tm[...]
        meta_in[...] = meta_own[...]

    @pl.when(swapped)
    def _():
        meta_copy.start()
        sp_copy.start()

    def rows_of(h):
        return slice(h * mh, (h + 1) * mh)

    def source_copy(it, h, step):
        target = (sibling, up_band, None, down_band)[step]
        return remote(
            src_own.at[it, :, rows_of(h)], s_band.at[it, pl.ds(2 * row, 2), rows_of(h)],
            s_send.at[h, step], s_recv.at[it, h, row], target,
        )

    def source_relay(it, h):
        ref = s_band.at[it, pl.ds(2 * relayed, 2), rows_of(h)]
        return remote(ref, ref, s_send.at[h, 2], s_recv.at[it, h, relayed], relay_on)

    def source_send(it, h):
        source_copy(it, h, 1).start()
        source_copy(it, h, 3).start()

        @pl.when(swapped)
        def _():
            source_copy(it, h, 0).start()

        @pl.when(own_role)
        def _():
            s_band[it, pl.ds(2 * row, 2), rows_of(h)] = src_own[it, :, rows_of(h)]

    def source_sent(it, h):
        source_copy(it, h, 1).wait_send()
        source_copy(it, h, 3).wait_send()
        source_relay(it, h).wait_send()

        @pl.when(swapped)
        def _():
            source_copy(it, h, 0).wait_send()

    def source_pass_on(it, h):
        source_relay(it, h).wait_recv()
        source_relay(it, h).start()

    def source_arrived(it, h):
        for r in range(4):
            @pl.when(jnp.logical_and(jnp.logical_or(swapped, row != r), relayed != r))
            def _():
                remote(src_own.at[it, :, rows_of(h)],
                       s_band.at[it, 2 * r:2 * r + 2, rows_of(h)], s_send.at[h, 0],
                       s_recv.at[it, h, r], sibling).wait_recv()

    for h in range(CHAINS):
        source_send(0, h)

    @pl.when(swapped)
    def _():
        meta_copy.wait_recv()
        sp_copy.wait_recv()
        points_out.wait_recv()

    to_scalar = pltpu.make_async_copy(meta_in, meta, m_sem)
    to_scalar.start()

    @pl.loop(0, 8)
    def _(c):
        start = pl.multiple_of(c * tile, tile)
        for k in range(3):
            line = sp_in[k:k + 1, pl.ds(start, tile)] * SCALE
            sb[c, k] = jnp.broadcast_to(line, (128, tile)).T

    @pl.loop(0, 64)
    def _(r):
        tt[r, 0:3] = tp_in[:, pl.ds(pl.multiple_of(r * tile, tile), tile)] * SCALE

    to_scalar.wait()

    acc[slots] = jnp.zeros((measures, tile), F32)

    def make_tile(s):
        r, c = meta[0, s], meta[1, s]
        for part_at in range(tile // 128):
            lanes = slice(part_at * 128, (part_at + 1) * 128)
            distance = (sb[c, 0] - tt[r, 0:1, lanes]) ** 2
            distance = distance + (sb[c, 1] - tt[r, 1:2, lanes]) ** 2
            distance = distance + (sb[c, 2] - tt[r, 2:3, lanes]) ** 2
            kt[s, :, lanes] = jnp.exp2(-8.0 - distance).astype(BF16)

    def row_product(it, s):
        acc[s] = acc[meta[2, s]] + jnp.dot(s_band[it, meta[1, s]], kt[s],
                                           preferred_element_type=F32)

    steps = 14
    first_tiles = slots - 2 * steps

    @pl.loop(0, first_tiles // 2)
    def _(pair):
        make_tile(2 * pair)
        make_tile(2 * pair + 1)

    for h in range(CHAINS):
        source_pass_on(0, h)

    @pl.when(swapped)
    def _():
        tm_copy.start()

    for h in range(CHAINS):
        source_arrived(0, h)

    @pl.loop(0, steps)
    def _(step):
        for m in range(3):
            row_product(0, 3 * step + m)
        for m in range(2):
            make_tile(first_tiles + 2 * step + m)

    for s in range(3 * steps, slots):
        row_product(0, s)

    def write_block(ref, value):
        line = lax.broadcasted_iota(I32, (16, tile), 0)

        def piece(i, refs):
            code, ref_row = encode(value(i))
            ref[pl.ds(pl.multiple_of(i * mh, 16), mh), :] = code
            return jnp.where(line == i, ref_row, refs)

        refs = lax.fori_loop(0, 2, piece, jnp.zeros((16, tile), I32))
        ref[2 * mh:2 * mh + 16, :] = refs.astype(I16)

    def read_block(ref, i):
        refs = ref[2 * mh:2 * mh + 16, :].astype(I32)
        line = lax.broadcasted_iota(I32, (16, tile), 0)
        ref_row = jnp.sum(jnp.where(line == i, refs, 0), axis=0, keepdims=True)
        return decode(ref[pl.ds(pl.multiple_of(i * mh, 16), mh), :], ref_row)

    place = ((x, y), (y, x))
    half = mh // 2
    lower, upper, full = slice(0, half), slice(half, mh), slice(0, mh)
    out_copy = remote(td_own, td_out, o_send, o_recv, partner)

    def total(a, d, u, side):
        g = (place[a][0] + d) % 4
        gx, gy = (g, u) if a == 0 else (u, g)
        return meta[4, 2 * (gx * 8 + side * 4 + gy) + a]

    class Chain:
        def __init__(self, h, it):
            self.h, self.it, self.rows = h, it, rows_of(h)

        def x0_copy(self, d):
            h = self.h
            return remote(x0_send.at[h, d], x0_recv.at[h, d], x_send.at[h, d],
                          x_recv.at[self.it, h, d], sibling)

        def r1_copy(self, a, kind):
            h, it = self.h, self.it
            return remote(r1_send.at[h, a, kind], r1_recv.at[it, h, a, kind],
                          a_send.at[h, a, kind], a_recv.at[it, h, a, kind],
                          on_ring(a, 1 if kind % 2 == 0 else 3))

        def r2_copy(self, a, kind):
            h, it = self.h, self.it
            return remote(r2_send.at[h, a, kind], r2_recv.at[it, h, a, kind],
                          b_send.at[h, a, kind], b_recv.at[it, h, a, kind],
                          on_ring(1 - a, 1 if kind % 2 == 0 else 3))

        def spot(self, a, g, u, side=None):
            return (((core if side is None else side) * 2 + a) * 4 + g) * 4 + u

        def some(self, kind):
            begin = self.h * mh
            return (self.rows, self.rows, slice(begin, begin + half),
                    slice(begin + half, begin + mh))[kind]

        def q_copy(self, a, kind):
            p, q = place[a]
            u = (q, q, (q + 3) % 4, (q + 1) % 4)[kind]
            ref = t_band.at[self.it, self.spot(a, p, u), self.some(kind)]
            return remote(ref, ref, q_send.at[self.h, a, kind],
                          q_recv.at[self.it, self.h, a, kind],
                          on_ring(1 - a, 1 if kind % 2 == 0 else 3))

        def q_got(self, a, kind):
            p, q = place[a]
            u = ((q + 3) % 4, (q + 1) % 4, (q + 2) % 4, (q + 2) % 4)[kind]
            ref = t_band.at[self.it, self.spot(a, p, u), self.some(kind)]
            remote(ref, ref, q_send.at[self.h, a, kind],
                   q_recv.at[self.it, self.h, a, kind], sibling).wait_recv()

        def pair(self, a, g, far):
            q = place[a][1]
            begin = 2 * (1 - q // 2) if far else 2 * (q // 2)
            return t_band.at[self.it, pl.ds(self.spot(a, g, begin), 2), self.rows]

        def g_copy(self, a, kind):
            p = place[a][0]
            g = (p, p, p, p, (p + 3) % 4, (p + 1) % 4)[kind]
            ref = self.pair(a, g, kind % 2 == 1)
            return remote(ref, ref, g_send.at[self.h, a, kind], g_recv.at[self.it, self.h, a, kind],
                          on_ring(a, (1, 1, 3, 3, 1, 3)[kind]))

        def g_got(self, a, kind):
            p = place[a][0]
            g = ((p + 3) % 4, (p + 3) % 4, (p + 1) % 4, (p + 1) % 4,
                 (p + 2) % 4, (p + 2) % 4)[kind]
            ref = self.pair(a, g, kind % 2 == 1)
            remote(ref, ref, g_send.at[self.h, a, kind], g_recv.at[self.it, self.h, a, kind],
                   sibling).wait_recv()

        def c_copy(self, a, dg):
            base = self.spot(a, (place[a][0] + dg) % 4, 0)
            ref = t_band.at[self.it, pl.ds(base, 4), self.rows]
            return remote(ref, ref, c_send.at[self.h, a, dg],
                          c_recv.at[self.it, self.h, a, dg], sibling)

        def c_got(self, a, dg):
            base = self.spot(a, (place[a][0] + dg) % 4, 0, other)
            ref = t_band.at[self.it, pl.ds(base, 4), self.rows]
            remote(ref, ref, c_send.at[self.h, a, dg],
                   c_recv.at[self.it, self.h, a, dg], sibling).wait_recv()

        def z_copy(self, kind, r):
            h, it = self.h, self.it
            return remote(z_send.at[h, r], z_recv.at[it, h, kind], w_send.at[h, r],
                          w_recv.at[it, h, kind], owner(r))

        def z_far(self, r, target):
            h, it = self.h, self.it
            return remote(z_send.at[h, r], z_recv.at[it, h, 3], w_send.at[h, r],
                          w_recv.at[it, h, 3], target)

        def to_next(self, r, fn):
            below = (core * 2 + r // 2 + 3) % 4 == z

            @pl.when(below)
            def _():
                fn(self.z_copy(1, r))

            @pl.when(jnp.logical_not(below))
            def _():
                fn(self.z_copy(2, r))

        def own(self, a, d, u):
            return acc[total(a, d, u, core), self.rows] + x0_recv[self.h, d, a, u]

        def stage(self, d):
            for a in range(2):
                @pl.loop(0, 4)
                def _(u):
                    x0_send[self.h, d, a, u] = acc[total(a, d, u, other), self.rows]

            self.x0_copy(d).start()

        def ring_far(self):
            self.x0_copy(2).wait_recv()
            for a in range(2):
                for kind, d, u0 in ((0, 2, 0), (1, 2, 2)):
                    write_block(r1_send.at[self.h, a, kind], lambda i: self.own(a, d, u0 + i))
                    self.r1_copy(a, kind).start()

        def ring_near(self):
            for kind, d, u0 in ((2, 1, 2), (3, 3, 0)):
                self.x0_copy(d).wait_recv()
                for a in range(2):
                    write_block(r1_send.at[self.h, a, kind], lambda i: self.own(a, d, u0 + i))
                    self.r1_copy(a, kind).start()

        def ring_relay(self):
            for a in range(2):
                for kind, d, u0 in ((4, 1, 0), (5, 3, 2)):
                    self.r1_copy(a, kind - 4).wait_recv()
                    got = r1_recv.at[self.it, self.h, a, kind - 4]
                    write_block(r1_send.at[self.h, a, kind],
                                lambda i: self.own(a, d, u0 + i) + read_block(got, i))
                    self.r1_copy(a, kind).start()

        def ring_sum(self):
            h, it = self.h, self.it
            self.x0_copy(0).wait_recv()
            for a in range(2):
                self.r1_copy(a, 2).wait_recv()
                self.r1_copy(a, 3).wait_recv()

                @pl.loop(0, 2)
                def _(i):
                    part[h, a, i] = self.own(a, 0, i) + read_block(r1_recv.at[it, h, a, 3], i)
                    part[h, a, 2 + i] = self.own(a, 0, 2 + i) + read_block(
                        r1_recv.at[it, h, a, 2], i)

        def ring_total(self):
            h, it = self.h, self.it
            for a in range(2):
                q = place[a][1]
                self.r1_copy(a, 4).wait_recv()
                self.r1_copy(a, 5).wait_recv()

                @pl.loop(0, 2)
                def _(i):
                    part[h, a, i] += read_block(r1_recv.at[it, h, a, 4], i)
                    part[h, a, 2 + i] += read_block(r1_recv.at[it, h, a, 5], i)

                for kind, d, side in ((0, 2, lower), (1, 2, upper), (2, 1, upper), (3, 3, lower)):
                    r2_send[h, a, kind] = part[h, a, (q + d) % 4, side]
                    self.r2_copy(a, kind).start()

        def short_relay(self):
            h, it = self.h, self.it
            for a in range(2):
                q = place[a][1]
                for kind, d, side in ((4, 1, lower), (5, 3, upper)):
                    self.r2_copy(a, kind - 4).wait_recv()
                    r2_send[h, a, kind] = (part[h, a, (q + d) % 4, side]
                                           + r2_recv[it, h, a, kind - 4])
                    self.r2_copy(a, kind).start()

        def target(self):
            h, it = self.h, self.it
            for a in range(2):
                p, q = place[a]
                for kind in (2, 3, 4, 5):
                    self.r2_copy(a, kind).wait_recv()
                sums = part[h, a, q] + jnp.concatenate(
                    [r2_recv[it, h, a, 3] + r2_recv[it, h, a, 4],
                     r2_recv[it, h, a, 2] + r2_recv[it, h, a, 5]], axis=0)
                dual = t_mass[a, self.rows] / sums
                t_band[it, self.spot(a, p, q), self.rows] = dual.astype(BF16)
                self.q_copy(a, 0).start()
                self.q_copy(a, 1).start()
                t_all[a, self.rows] = dual

        def gather_near(self):
            for a in range(2):
                self.q_got(a, 0)
                self.q_copy(a, 2).start()
                self.q_got(a, 1)
                self.q_copy(a, 3).start()
                self.g_copy(a, 0).start()
                self.g_copy(a, 2).start()

        def gather_block(self):
            for a in range(2):
                self.q_got(a, 2)
                self.q_got(a, 3)
                self.g_copy(a, 3).start()
                self.g_copy(a, 1).start()
                self.g_got(a, 0)
                self.g_copy(a, 4).start()
            for a in range(2):
                self.c_copy(a, 0).start()

        def gather_relay(self):
            for a in range(2):
                self.g_got(a, 3)
                self.g_copy(a, 5).start()
            for a in range(2):
                self.g_got(a, 1)
                self.c_copy(a, 3).start()
                self.g_got(a, 2)
                self.c_copy(a, 1).start()

        def gather_last(self):
            for a in range(2):
                self.g_got(a, 4)
                self.g_got(a, 5)
                self.c_copy(a, 2).start()

        def gathered(self):
            for dg in (0, 3, 1, 2):
                for a in range(2):
                    self.c_got(a, dg)

        def to_owner(self):
            h, it = self.h, self.it
            first = 2 * (delta % 2)
            for at in range(2):
                r = first + at
                write_block(z_send.at[h, r], lambda i: acc[meta[5, 2 * r + i], self.rows])

                @pl.when(swapped)
                def _():
                    self.z_far(r, device(
                        x, y, (z + jnp.where((delta == 2) == (at == 0), 3, 1)) % 4, core)).start()

                @pl.when(jnp.logical_and(own_role, core != at))
                def _():
                    self.z_copy(0, r).start()

                @pl.when(jnp.logical_and(own_role, core == at))
                def _():
                    z_recv[it, h, 0] = z_send[h, r]

            write_block(z_send.at[h, single], lambda i: acc[meta[5, 2 * single + i], self.rows])
            self.to_next(single, lambda copy: copy.start())

        def to_owner_relay(self):
            h, it = self.h, self.it
            self.z_far(0, sibling).wait_recv()
            got = z_recv.at[it, h, 3]
            write_block(z_send.at[h, relayed],
                        lambda i: acc[meta[5, 2 * relayed + i], self.rows] + read_block(got, i))
            self.to_next(relayed, lambda copy: copy.start())

        def source(self):
            h, it = self.h, self.it
            for kind in range(3):
                @pl.when(jnp.logical_or(swapped, kind != 0))
                def _():
                    self.z_copy(kind, 0).wait_recv()

            for k in range(2):
                sums = read_block(z_recv.at[it, h, 0], k)
                for kind in (1, 2):
                    sums = sums + read_block(z_recv.at[it, h, kind], k)
                dual = s_mass[k, self.rows] / sums
                s_all[k, self.rows] = dual

                @pl.when(it < ITERS - 1)
                def _():
                    src_own[1, k, self.rows] = dual.astype(BF16)

            source_sent(it, h)

            @pl.when(it < ITERS - 1)
            def _():
                source_send(1, h)

        def sent(self):
            h = self.h
            for d in range(4):
                self.x0_copy(d).wait_send()
            for a in range(2):
                for kind in range(6):
                    self.r1_copy(a, kind).wait_send()
                    self.r2_copy(a, kind).wait_send()
                    self.g_copy(a, kind).wait_send()
                for kind in range(4):
                    self.q_copy(a, kind).wait_send()
                    self.c_copy(a, kind).wait_send()
            first = 2 * (delta % 2)
            for at in range(2):
                @pl.when(jnp.logical_or(swapped, core != at))
                def _():
                    self.z_far(first + at, sibling).wait_send()
            for r in (single, relayed):
                self.z_copy(1, r).wait_send()

    def iteration(it, _):
        chains = [Chain(h, it) for h in range(CHAINS)]

        @pl.when(it > 0)
        def _():
            for h in range(CHAINS):
                source_arrived(1, h)

            @pl.loop(0, slots // GROUP)
            def _(group):
                for m in range(GROUP):
                    row_product(1, group * GROUP + m)

        for d in (2, 1, 3, 0):
            for chain in chains:
                chain.stage(d)
        for name in ("ring_far", "ring_near", "ring_relay", "ring_sum", "ring_total",
                     "short_relay", "target", "gather_near", "gather_block", "gather_relay",
                     "gather_last"):
            for chain in chains:
                getattr(chain, name)()
            if name == "ring_near":
                @pl.when(it == 0)
                def _():
                    @pl.when(swapped)
                    def _():
                        tm_copy.wait_recv()

                    for k in range(2):
                        t_mass[k] = tm_in[k * tile:(k + 1) * tile, :].T

        @pl.when(it == ITERS - 1)
        def _():
            for a in range(2):
                td_own[a * tile:(a + 1) * tile, :] = t_all[a].T

            @pl.when(swapped)
            def _():
                out_copy.start()

            @pl.when(own_role)
            def _():
                td_out[...] = td_own[...]

        for chain in chains:
            chain.gathered()

        @pl.loop(0, slots // GROUP)
        def _(group):
            for m in range(GROUP):
                s = group * GROUP + m
                acc[s] = acc[meta[3, s]] + lax.dot_general(
                    t_band[it, meta[6, s]], kt[s], (((1,), (1,)), ((), ())),
                    preferred_element_type=F32)

        for name in ("to_owner", "to_owner_relay", "source"):
            for chain in chains:
                getattr(chain, name)()

        @pl.when(it < ITERS - 1)
        def _():
            for h in range(CHAINS):
                source_pass_on(1, h)

        for chain in chains:
            chain.sent()
        return 0

    lax.fori_loop(0, ITERS, iteration, 0)
    for k in range(2):
        so_out[k * tile:(k + 1) * tile, :] = s_all[k].T

    @pl.when(own_role)
    def _():
        points_out.wait_send()

    @pl.when(swapped)
    def _():
        out_copy.wait()
        meta_copy.wait_send()
        sp_copy.wait_send()
        tm_copy.wait_send()


def local(target_points, source_points, target_mass, source_mass, start_dual,
          tile_row, tile_column, tile_count):
    slots = tile_row.shape[0]
    rows, measures = target_mass.shape
    tile = rows // 2
    mh = measures // CHAINS
    dma = pltpu.SemaphoreType.DMA
    vmem = pltpu.VMEM
    whole = pl.BlockSpec(memory_space=pltpu.VMEM)
    block = 2 * mh + 16
    return pl.pallas_call(
        functools.partial(kernel, slots),
        out_shape=(
            jax.ShapeDtypeStruct((rows, measures), F32),
            jax.ShapeDtypeStruct((rows, measures), F32),
        ),
        in_specs=[whole] * 7 + [pl.BlockSpec(memory_space=pltpu.SMEM)],
        out_specs=(whole, whole),
        scratch_shapes=[
            vmem((8, 128), I32),
            vmem((8, 128), I32),
            pltpu.SMEM((8, 128), I32),
            vmem(target_points.shape, F32),
            vmem(source_points.shape, F32),
            vmem((rows, measures), F32),
            vmem((64, 8, tile), F32),
            vmem((8, 3, tile, 128), F32),
            vmem((slots, tile, tile), BF16),
            vmem((slots + 1, measures, tile), F32),
            vmem((ITERS, 2, measures, tile), BF16),
            vmem((ITERS, 8, measures, tile), BF16),
            vmem((CHAINS, 4, 2, 4, mh, tile), F32),
            vmem((CHAINS, 4, 2, 4, mh, tile), F32),
            vmem((CHAINS, 2, 6, block, tile), I16),
            vmem((ITERS, CHAINS, 2, 6, block, tile), I16),
            vmem((CHAINS, 2, 6, mh // 2, tile), F32),
            vmem((ITERS, CHAINS, 2, 6, mh // 2, tile), F32),
            vmem((CHAINS, 2, 4, mh, tile), F32),
            vmem((ITERS, 64, measures, tile), BF16),
            vmem((CHAINS, 4, block, tile), I16),
            vmem((ITERS, CHAINS, 4, block, tile), I16),
            vmem((rows, measures), F32),
            vmem((2, measures, tile), F32),
            vmem((2, measures, tile), F32),
            vmem((2, measures, tile), F32),
            vmem((2, measures, tile), F32),
            dma((4,)), dma((4,)),
            dma((CHAINS, 4)), dma((ITERS, CHAINS, 4)),
            dma((CHAINS, 4)), dma((ITERS, CHAINS, 4)),
            dma((CHAINS, 2, 6)), dma((ITERS, CHAINS, 2, 6)),
            dma((CHAINS, 2, 6)), dma((ITERS, CHAINS, 2, 6)),
            dma((CHAINS, 2, 4)), dma((ITERS, CHAINS, 2, 4)),
            dma((CHAINS, 2, 6)), dma((ITERS, CHAINS, 2, 6)),
            dma((CHAINS, 2, 4)), dma((ITERS, CHAINS, 2, 4)),
            dma((CHAINS, 4)), dma((ITERS, CHAINS, 4)),
            dma, dma, dma,
        ],
        compiler_params=pltpu.CompilerParams(
            collective_id=0, has_side_effects=True, vmem_limit_bytes=60 * 1024 * 1024
        ),
    )(target_points, source_points, target_mass, source_mass, start_dual,
      tile_row.reshape(1, slots), tile_column.reshape(1, slots), tile_count)


def solution(mesh):
    return jax.shard_map(
        local,
        mesh=mesh,
        in_specs=(
            P(None, "row"),
            P(None, "col"),
            P(("row", "col"), None),
            P(("col", "row"), None),
            P(("col", "row"), None),
            P(("row", "col")),
            P(("row", "col")),
            P(("row", "col")),
        ),
        out_specs=(P(("row", "col"), None), P(("col", "row"), None)),
        check_vma=False,
    )
```

```python
import functools

import jax
import jax.numpy as jnp
from jax import lax
from jax.experimental import pallas as pl
from jax.experimental.pallas import tpu as pltpu
from jax.sharding import PartitionSpec as P

MESH = pl.DeviceIdType.MESH
ITERS = 2
CHAINS = 2
GROUP = 16
SCALE = 2.6857913
FINE = 2896.0
COARSE = 256.0
F32 = jnp.float32
BF16 = jnp.bfloat16
I16 = jnp.int16
I32 = jnp.int32


def encode(x):
    level = jnp.log(jnp.maximum(x, 1e-37))
    ref = (level[0:1] * COARSE + 32768.5).astype(I32) - 32768
    fine = level * FINE + (32768.5 - ref.astype(F32) * (FINE / COARSE))
    return (fine.astype(I32) - 32768).astype(I16), ref


def decode(code, ref):
    return jnp.exp(
        code.astype(I32).astype(F32) * (1.0 / FINE) + ref.astype(F32) * (1.0 / COARSE)
    )


def kernel(
    slots,
    tp, sp, tm, sm, sd, tr, tc, tn,
    td_out, so_out,
    meta_own, meta_in, meta, tp_in, sp_in, tm_in, tt, sb, kt, acc,
    src_own, s_band, x0_send, x0_recv, r1_send, r1_recv, r2_recv, part,
    t_band, z_send, z_recv, td_own, t_mass, s_mass, t_all, s_all,
    p_send, p_recv, s_send, s_recv, x_send, x_recv, a_send, a_recv, b_send, b_recv,
    q_send, q_recv, g_send, g_recv, c_send, c_recv, w_send, w_recv, o_send, o_recv, m_sem,
):
    tile = kt.shape[1]
    measures = acc.shape[1]
    mh = measures // CHAINS
    row = lax.axis_index("row")
    col = lax.axis_index("col")
    z_lo, core = row // 2, row % 2
    x, z_hi, y = col // 8, (col // 4) % 2, col % 4
    z = z_hi * 2 + z_lo
    other = 1 - core
    own_role = core == z_hi
    swapped = core != z_hi

    def device(x_, y_, z_, core_):
        return ((z_ % 2) * 2 + core_, x_ * 8 + (z_ // 2) * 4 + y_)

    sibling = device(x, y, z, other)
    partner = device(x, y, core * 2 + z_lo, z_hi)

    ring = {(0, step): device((x + step) % 4, y, z, core) for step in (1, 2, 3)}
    ring.update({(1, step): device(x, (y + step) % 4, z, core) for step in (1, 2, 3)})

    def on_ring(axis, step):
        return ring[axis, step]

    delta = (z + 4 - 2 * core) % 4

    def by_delta(*values):
        return jnp.where(delta < 2, jnp.where(delta == 0, values[0], values[1]),
                         jnp.where(delta == 2, values[2], values[3]))

    relayed, single = by_delta(2, 0, 3, 1), by_delta(3, 1, 2, 0)
    up_band = device(x, y, (z + 1) % 4, z_hi)
    down_band = device(x, y, (z + 3) % 4, z_hi)
    up_core = device(x, y, (z + 1) % 4, core)
    down_core = device(x, y, (z + 3) % 4, core)
    relay_step = by_delta(3, 1, 1, 3)
    relay_on = device(x, y, (z + relay_step) % 4, core)

    def owner(r):
        return device(x, y, core * 2 + r // 2, r % 2)

    def remote(src, dst, send, recv, target):
        return pltpu.make_async_remote_copy(
            src_ref=src, dst_ref=dst, send_sem=send, recv_sem=recv,
            device_id=target, device_id_type=MESH,
        )

    barrier = pltpu.get_barrier_semaphore()
    friends = [device(x, y, (z + dz) % 4, (core + dk) % 2)
               for dz in range(4) for dk in range(2) if dz or dk]
    friends += [on_ring(axis, step) for axis in (0, 1) for step in (1, 2, 3)]
    for friend in friends:
        pl.semaphore_signal(barrier, inc=1, device_id=friend, device_id_type=MESH)

    meta_own[...] = jnp.zeros_like(meta_own)
    meta_own[0:1, 0:slots] = jnp.clip(tr[...], 0, 63)
    meta_own[1:2, 0:slots] = jnp.clip(tc[...], 0, 7)
    lane = lax.broadcasted_iota(I32, (128, 128), 1)
    sub = lax.broadcasted_iota(I32, (128, 128), 0)
    alive = sub < tn[0]
    for k in range(2):
        across = jnp.broadcast_to(meta_own[k:k + 1, :], (128, 128))
        down = across.T
        same = (down == across) & (sub < lane) & alive
        found = jnp.max(jnp.where(same, sub, -1), axis=0, keepdims=True)
        meta_own[2 + k:3 + k, :] = jnp.where(found < 0, slots, found)
        same = (down == lane) & alive
        found = jnp.max(jnp.where(same, sub, -1), axis=0, keepdims=True)
        meta_own[4 + k:5 + k, :] = jnp.where(found < 0, slots, found)
    index = meta_own[0:1, :]
    share = index // 2
    sx, sh, sy = share // 8, (share // 4) % 2, share % 4
    even = ((sh * 2 + 0) * 4 + sx) * 4 + sy
    odd = ((sh * 2 + 1) * 4 + sy) * 4 + sx
    meta_own[6:7, :] = jnp.where(index % 2 == 0, even, odd)

    for k in range(2):
        src_own[0, k] = sd[k * tile:(k + 1) * tile, :].astype(F32).T.astype(BF16)
        s_mass[k] = sm[k * tile:(k + 1) * tile, :].T

    pl.semaphore_wait(barrier, len(friends))

    points_out = remote(tp, tp_in, p_send.at[0], p_recv.at[0], sibling)
    sp_copy = remote(sp, sp_in, p_send.at[1], p_recv.at[1], partner)
    meta_copy = remote(meta_own, meta_in, p_send.at[2], p_recv.at[2], partner)
    tm_copy = remote(tm, tm_in, p_send.at[3], p_recv.at[3], partner)

    @pl.when(own_role)
    def _():
        points_out.start()
        sp_in[...] = sp[...]
        tp_in[...] = tp[...]
        tm_in[...] = tm[...]
        meta_in[...] = meta_own[...]

    @pl.when(swapped)
    def _():
        meta_copy.start()
        sp_copy.start()

    def rows_of(h):
        return slice(h * mh, (h + 1) * mh)

    def source_copy(it, h, step):
        target = (sibling, up_band, None, down_band)[step]
        return remote(
            src_own.at[it, :, rows_of(h)], s_band.at[it, pl.ds(2 * row, 2), rows_of(h)],
            s_send.at[h, step], s_recv.at[it, h, row], target,
        )

    def source_relay(it, h):
        ref = s_band.at[it, pl.ds(2 * relayed, 2), rows_of(h)]
        return remote(ref, ref, s_send.at[h, 2], s_recv.at[it, h, relayed], relay_on)

    def source_send(it, h):
        source_copy(it, h, 1).start()
        source_copy(it, h, 3).start()

        @pl.when(swapped)
        def _():
            source_copy(it, h, 0).start()

        @pl.when(own_role)
        def _():
            s_band[it, pl.ds(2 * row, 2), rows_of(h)] = src_own[it, :, rows_of(h)]

    def source_sent(it, h):
        source_copy(it, h, 1).wait_send()
        source_copy(it, h, 3).wait_send()
        source_relay(it, h).wait_send()

        @pl.when(swapped)
        def _():
            source_copy(it, h, 0).wait_send()

    def source_pass_on(it, h):
        source_relay(it, h).wait_recv()
        source_relay(it, h).start()

    def source_arrived(it, h):
        for r in range(4):
            @pl.when(jnp.logical_and(jnp.logical_or(swapped, row != r), relayed != r))
            def _():
                remote(src_own.at[it, :, rows_of(h)],
                       s_band.at[it, 2 * r:2 * r + 2, rows_of(h)], s_send.at[h, 0],
                       s_recv.at[it, h, r], sibling).wait_recv()

    for h in range(CHAINS):
        source_send(0, h)

    @pl.when(swapped)
    def _():
        meta_copy.wait_recv()
        sp_copy.wait_recv()
        points_out.wait_recv()

    to_scalar = pltpu.make_async_copy(meta_in, meta, m_sem)
    to_scalar.start()

    @pl.loop(0, 8)
    def _(c):
        start = pl.multiple_of(c * tile, tile)
        for k in range(3):
            line = sp_in[k:k + 1, pl.ds(start, tile)] * SCALE
            sb[c, k] = jnp.broadcast_to(line, (128, tile)).T

    @pl.loop(0, 64)
    def _(r):
        tt[r, 0:3] = tp_in[:, pl.ds(pl.multiple_of(r * tile, tile), tile)] * SCALE

    to_scalar.wait()

    acc[slots] = jnp.zeros((measures, tile), F32)

    def make_tile(s):
        r, c = meta[0, s], meta[1, s]
        for part_at in range(tile // 128):
            lanes = slice(part_at * 128, (part_at + 1) * 128)
            distance = (sb[c, 0] - tt[r, 0:1, lanes]) ** 2
            distance = distance + (sb[c, 1] - tt[r, 1:2, lanes]) ** 2
            distance = distance + (sb[c, 2] - tt[r, 2:3, lanes]) ** 2
            kt[s, :, lanes] = jnp.exp2(-8.0 - distance).astype(BF16)

    def row_product(it, s):
        acc[s] = acc[meta[2, s]] + jnp.dot(s_band[it, meta[1, s]], kt[s],
                                           preferred_element_type=F32)

    steps = 14
    first_tiles = slots - 2 * steps

    @pl.loop(0, first_tiles // 2)
    def _(pair):
        make_tile(2 * pair)
        make_tile(2 * pair + 1)

    for h in range(CHAINS):
        source_pass_on(0, h)

    @pl.when(swapped)
    def _():
        tm_copy.start()

    for h in range(CHAINS):
        source_arrived(0, h)

    @pl.loop(0, steps)
    def _(step):
        for m in range(3):
            row_product(0, 3 * step + m)
        for m in range(2):
            make_tile(first_tiles + 2 * step + m)

    for s in range(3 * steps, slots):
        row_product(0, s)

    def write_block(ref, value):
        coded = [encode(value(i)) for i in range(2)]
        for i in range(2):
            ref[i * mh:(i + 1) * mh, :] = coded[i][0]
        line = lax.broadcasted_iota(I32, (16, tile), 0)
        ref[2 * mh:2 * mh + 16, :] = jnp.where(line == 0, coded[0][1], coded[1][1]).astype(I16)

    def read_block(ref, i):
        refs = ref[2 * mh:2 * mh + 16, :].astype(I32)
        return decode(ref[i * mh:(i + 1) * mh, :], refs[i:i + 1])

    place = ((x, y), (y, x))
    out_copy = remote(td_own, td_out, o_send, o_recv, partner)

    def total(a, d, u, side):
        g = (place[a][0] + d) % 4
        gx, gy = (g, u) if a == 0 else (u, g)
        return meta[4, 2 * (gx * 8 + side * 4 + gy) + a]

    class Chain:
        def __init__(self, h, it):
            self.h, self.it, self.rows = h, it, rows_of(h)

        def x0_copy(self, d):
            h = self.h
            return remote(x0_send.at[h, d], x0_recv.at[h, d], x_send.at[h, d],
                          x_recv.at[self.it, h, d], sibling)

        def r1_copy(self, a, kind):
            h, it = self.h, self.it
            return remote(r1_send.at[h, a, kind], r1_recv.at[it, h, a, kind],
                          a_send.at[h, a, kind], a_recv.at[it, h, a, kind],
                          on_ring(a, 1 if kind % 2 == 0 else 3))

        def r2_copy(self, a, kind):
            h, it, step = self.h, self.it, (1, 3, 2)[kind]
            return remote(part.at[h, a, (place[a][1] + step) % 4], r2_recv.at[it, h, a, kind],
                          b_send.at[h, a, kind], b_recv.at[it, h, a, kind], on_ring(1 - a, step))

        def spot(self, a, g, u, side=None):
            return (((core if side is None else side) * 2 + a) * 4 + g) * 4 + u

        def q_copy(self, a, kind):
            p, q = place[a]
            ref = t_band.at[self.it, self.spot(a, p, q), self.rows]
            return remote(ref, ref, q_send.at[self.h, a, kind],
                          q_recv.at[self.it, self.h, a, kind], on_ring(1 - a, (1, 3, 2)[kind]))

        def q_got(self, a, kind):
            p, q = place[a]
            ref = t_band.at[self.it, self.spot(a, p, (q + (3, 1, 2)[kind]) % 4), self.rows]
            remote(ref, ref, q_send.at[self.h, a, kind],
                   q_recv.at[self.it, self.h, a, kind], sibling).wait_recv()

        def pair(self, a, g, far):
            q = place[a][1]
            begin = 2 * (1 - q // 2) if far else 2 * (q // 2)
            return t_band.at[self.it, pl.ds(self.spot(a, g, begin), 2), self.rows]

        def g_copy(self, a, kind):
            p = place[a][0]
            g = (p, p, p, p, (p + 3) % 4, (p + 1) % 4)[kind]
            ref = self.pair(a, g, kind % 2 == 1)
            return remote(ref, ref, g_send.at[self.h, a, kind], g_recv.at[self.it, self.h, a, kind],
                          on_ring(a, (1, 1, 3, 3, 1, 3)[kind]))

        def g_got(self, a, kind):
            p = place[a][0]
            g = ((p + 3) % 4, (p + 3) % 4, (p + 1) % 4, (p + 1) % 4,
                 (p + 2) % 4, (p + 2) % 4)[kind]
            ref = self.pair(a, g, kind % 2 == 1)
            remote(ref, ref, g_send.at[self.h, a, kind], g_recv.at[self.it, self.h, a, kind],
                   sibling).wait_recv()

        def c_copy(self, a, dg):
            base = self.spot(a, (place[a][0] + dg) % 4, 0)
            ref = t_band.at[self.it, pl.ds(base, 4), self.rows]
            return remote(ref, ref, c_send.at[self.h, a, dg],
                          c_recv.at[self.it, self.h, a, dg], sibling)

        def c_got(self, a, dg):
            base = self.spot(a, (place[a][0] + dg) % 4, 0, other)
            ref = t_band.at[self.it, pl.ds(base, 4), self.rows]
            remote(ref, ref, c_send.at[self.h, a, dg],
                   c_recv.at[self.it, self.h, a, dg], sibling).wait_recv()

        def z_copy(self, kind, r):
            h, it = self.h, self.it
            return remote(z_send.at[h, r], z_recv.at[it, h, kind], w_send.at[h, r],
                          w_recv.at[it, h, kind], owner(r))

        def z_far(self, r, target):
            h, it = self.h, self.it
            return remote(z_send.at[h, r], z_recv.at[it, h, 3], w_send.at[h, r],
                          w_recv.at[it, h, 3], target)

        def to_next(self, r, fn):
            below = (core * 2 + r // 2 + 3) % 4 == z

            @pl.when(below)
            def _():
                fn(self.z_copy(1, r))

            @pl.when(jnp.logical_not(below))
            def _():
                fn(self.z_copy(2, r))

        def own(self, a, d, u):
            return acc[total(a, d, u, core), self.rows] + x0_recv[self.h, d, a, u]

        def stage(self, d):
            for a in range(2):
                @pl.loop(0, 4)
                def _(u):
                    x0_send[self.h, d, a, u] = acc[total(a, d, u, other), self.rows]

            self.x0_copy(d).start()

        def ring_far(self):
            self.x0_copy(2).wait_recv()
            for a in range(2):
                for kind, d, u0 in ((0, 2, 0), (1, 2, 2)):
                    write_block(r1_send.at[self.h, a, kind], lambda i: self.own(a, d, u0 + i))
                    self.r1_copy(a, kind).start()

        def ring_near(self):
            for kind, d, u0 in ((2, 1, 2), (3, 3, 0)):
                self.x0_copy(d).wait_recv()
                for a in range(2):
                    write_block(r1_send.at[self.h, a, kind], lambda i: self.own(a, d, u0 + i))
                    self.r1_copy(a, kind).start()

        def ring_relay(self):
            for a in range(2):
                for kind, d, u0 in ((4, 1, 0), (5, 3, 2)):
                    self.r1_copy(a, kind - 4).wait_recv()
                    got = r1_recv.at[self.it, self.h, a, kind - 4]
                    write_block(r1_send.at[self.h, a, kind],
                                lambda i: self.own(a, d, u0 + i) + read_block(got, i))
                    self.r1_copy(a, kind).start()

        def ring_sum(self):
            h, it = self.h, self.it
            self.x0_copy(0).wait_recv()
            for a in range(2):
                self.r1_copy(a, 2).wait_recv()
                self.r1_copy(a, 3).wait_recv()

                for i in range(2):
                    part[h, a, i] = self.own(a, 0, i) + read_block(r1_recv.at[it, h, a, 3], i)
                    part[h, a, 2 + i] = self.own(a, 0, 2 + i) + read_block(
                        r1_recv.at[it, h, a, 2], i)

        def ring_total(self):
            h, it = self.h, self.it
            for a in range(2):
                self.r1_copy(a, 4).wait_recv()
                self.r1_copy(a, 5).wait_recv()
                for i in range(2):
                    part[h, a, i] += read_block(r1_recv.at[it, h, a, 4], i)
                    part[h, a, 2 + i] += read_block(r1_recv.at[it, h, a, 5], i)
                for kind in (2, 0, 1):
                    self.r2_copy(a, kind).start()

        def target(self):
            h, it = self.h, self.it
            for a in range(2):
                p, q = place[a]
                for kind in range(3):
                    self.r2_copy(a, kind).wait_recv()
                sums = (part[h, a, q] + r2_recv[it, h, a, 0]) + (
                    r2_recv[it, h, a, 1] + r2_recv[it, h, a, 2])
                dual = t_mass[a, self.rows] / sums
                t_band[it, self.spot(a, p, q), self.rows] = dual.astype(BF16)
                for kind in (2, 0, 1):
                    self.q_copy(a, kind).start()
                t_all[a, self.rows] = dual

        def gather_near(self):
            for a in range(2):
                self.q_got(a, 0)
                self.q_got(a, 1)
                self.g_copy(a, 0).start()
                self.g_copy(a, 2).start()

        def gather_block(self):
            for a in range(2):
                self.q_got(a, 2)
                self.g_copy(a, 3).start()
                self.g_copy(a, 1).start()
                self.g_got(a, 0)
                self.g_copy(a, 4).start()
            for a in range(2):
                self.c_copy(a, 0).start()

        def gather_relay(self):
            for a in range(2):
                self.g_got(a, 3)
                self.g_copy(a, 5).start()
            for a in range(2):
                self.g_got(a, 1)
                self.c_copy(a, 3).start()
                self.g_got(a, 2)
                self.c_copy(a, 1).start()

        def gather_last(self):
            for a in range(2):
                self.g_got(a, 4)
                self.g_got(a, 5)
                self.c_copy(a, 2).start()

        def gathered(self):
            for dg in (0, 3, 1, 2):
                for a in range(2):
                    self.c_got(a, dg)

        def to_owner(self):
            h, it = self.h, self.it
            first = 2 * (delta % 2)
            for at in range(2):
                r = first + at
                write_block(z_send.at[h, r], lambda i: acc[meta[5, 2 * r + i], self.rows])

                @pl.when(swapped)
                def _():
                    self.z_far(r, device(
                        x, y, (z + jnp.where((delta == 2) == (at == 0), 3, 1)) % 4, core)).start()

                @pl.when(jnp.logical_and(own_role, core != at))
                def _():
                    self.z_copy(0, r).start()

                @pl.when(jnp.logical_and(own_role, core == at))
                def _():
                    z_recv[it, h, 0] = z_send[h, r]

            write_block(z_send.at[h, single], lambda i: acc[meta[5, 2 * single + i], self.rows])
            self.to_next(single, lambda copy: copy.start())

        def to_owner_relay(self):
            h, it = self.h, self.it
            self.z_far(0, sibling).wait_recv()
            got = z_recv.at[it, h, 3]
            write_block(z_send.at[h, relayed],
                        lambda i: acc[meta[5, 2 * relayed + i], self.rows] + read_block(got, i))
            self.to_next(relayed, lambda copy: copy.start())

        def source(self):
            h, it = self.h, self.it
            for kind in range(3):
                @pl.when(jnp.logical_or(swapped, kind != 0))
                def _():
                    self.z_copy(kind, 0).wait_recv()

            for k in range(2):
                sums = read_block(z_recv.at[it, h, 0], k)
                for kind in (1, 2):
                    sums = sums + read_block(z_recv.at[it, h, kind], k)
                dual = s_mass[k, self.rows] / sums
                s_all[k, self.rows] = dual

                @pl.when(it < ITERS - 1)
                def _():
                    src_own[1, k, self.rows] = dual.astype(BF16)

            source_sent(it, h)

            @pl.when(it < ITERS - 1)
            def _():
                source_send(1, h)

        def sent(self):
            h = self.h
            for d in range(4):
                self.x0_copy(d).wait_send()
            for a in range(2):
                for kind in range(6):
                    self.r1_copy(a, kind).wait_send()
                    self.g_copy(a, kind).wait_send()
                for kind in range(3):
                    self.r2_copy(a, kind).wait_send()
                    self.q_copy(a, kind).wait_send()
                for kind in range(4):
                    self.c_copy(a, kind).wait_send()
            first = 2 * (delta % 2)
            for at in range(2):
                @pl.when(jnp.logical_or(swapped, core != at))
                def _():
                    self.z_far(first + at, sibling).wait_send()
            for r in (single, relayed):
                self.z_copy(1, r).wait_send()

    def iteration(it, _):
        chains = [Chain(h, it) for h in range(CHAINS)]

        @pl.when(it > 0)
        def _():
            for h in range(CHAINS):
                source_arrived(1, h)

            @pl.loop(0, slots // GROUP)
            def _(group):
                for m in range(GROUP):
                    row_product(1, group * GROUP + m)

        for d in (2, 1, 3, 0):
            for chain in chains:
                chain.stage(d)
        for name in ("ring_far", "ring_near", "ring_relay", "ring_sum", "ring_total",
                     "target", "gather_near", "gather_block", "gather_relay",
                     "gather_last"):
            for chain in chains:
                getattr(chain, name)()
            if name == "ring_near":
                @pl.when(it == 0)
                def _():
                    @pl.when(swapped)
                    def _():
                        tm_copy.wait_recv()

                    for k in range(2):
                        t_mass[k] = tm_in[k * tile:(k + 1) * tile, :].T

        @pl.when(it == ITERS - 1)
        def _():
            for a in range(2):
                td_own[a * tile:(a + 1) * tile, :] = t_all[a].T

            @pl.when(swapped)
            def _():
                out_copy.start()

            @pl.when(own_role)
            def _():
                td_out[...] = td_own[...]

        for chain in chains:
            chain.gathered()

        @pl.loop(0, slots // GROUP)
        def _(group):
            for m in range(GROUP):
                s = group * GROUP + m
                acc[s] = acc[meta[3, s]] + lax.dot_general(
                    t_band[it, meta[6, s]], kt[s], (((1,), (1,)), ((), ())),
                    preferred_element_type=F32)

        for name in ("to_owner", "to_owner_relay", "source"):
            for chain in chains:
                getattr(chain, name)()

        @pl.when(it < ITERS - 1)
        def _():
            for h in range(CHAINS):
                source_pass_on(1, h)

        for chain in chains:
            chain.sent()
        return 0

    lax.fori_loop(0, ITERS, iteration, 0)
    for k in range(2):
        so_out[k * tile:(k + 1) * tile, :] = s_all[k].T

    @pl.when(own_role)
    def _():
        points_out.wait_send()

    @pl.when(swapped)
    def _():
        out_copy.wait()
        meta_copy.wait_send()
        sp_copy.wait_send()
        tm_copy.wait_send()


def local(target_points, source_points, target_mass, source_mass, start_dual,
          tile_row, tile_column, tile_count):
    slots = tile_row.shape[0]
    rows, measures = target_mass.shape
    tile = rows // 2
    mh = measures // CHAINS
    dma = pltpu.SemaphoreType.DMA
    vmem = pltpu.VMEM
    whole = pl.BlockSpec(memory_space=pltpu.VMEM)
    block = 2 * mh + 16
    return pl.pallas_call(
        functools.partial(kernel, slots),
        out_shape=(
            jax.ShapeDtypeStruct((rows, measures), F32),
            jax.ShapeDtypeStruct((rows, measures), F32),
        ),
        in_specs=[whole] * 7 + [pl.BlockSpec(memory_space=pltpu.SMEM)],
        out_specs=(whole, whole),
        scratch_shapes=[
            vmem((8, 128), I32),
            vmem((8, 128), I32),
            pltpu.SMEM((8, 128), I32),
            vmem(target_points.shape, F32),
            vmem(source_points.shape, F32),
            vmem((rows, measures), F32),
            vmem((64, 8, tile), F32),
            vmem((8, 3, tile, 128), F32),
            vmem((slots, tile, tile), BF16),
            vmem((slots + 1, measures, tile), F32),
            vmem((ITERS, 2, measures, tile), BF16),
            vmem((ITERS, 8, measures, tile), BF16),
            vmem((CHAINS, 4, 2, 4, mh, tile), F32),
            vmem((CHAINS, 4, 2, 4, mh, tile), F32),
            vmem((CHAINS, 2, 6, block, tile), I16),
            vmem((ITERS, CHAINS, 2, 6, block, tile), I16),
            vmem((ITERS, CHAINS, 2, 3, mh, tile), F32),
            vmem((CHAINS, 2, 4, mh, tile), F32),
            vmem((ITERS, 64, measures, tile), BF16),
            vmem((CHAINS, 4, block, tile), I16),
            vmem((ITERS, CHAINS, 4, block, tile), I16),
            vmem((rows, measures), F32),
            vmem((2, measures, tile), F32),
            vmem((2, measures, tile), F32),
            vmem((2, measures, tile), F32),
            vmem((2, measures, tile), F32),
            dma((4,)), dma((4,)),
            dma((CHAINS, 4)), dma((ITERS, CHAINS, 4)),
            dma((CHAINS, 4)), dma((ITERS, CHAINS, 4)),
            dma((CHAINS, 2, 6)), dma((ITERS, CHAINS, 2, 6)),
            dma((CHAINS, 2, 3)), dma((ITERS, CHAINS, 2, 3)),
            dma((CHAINS, 2, 3)), dma((ITERS, CHAINS, 2, 3)),
            dma((CHAINS, 2, 6)), dma((ITERS, CHAINS, 2, 6)),
            dma((CHAINS, 2, 4)), dma((ITERS, CHAINS, 2, 4)),
            dma((CHAINS, 4)), dma((ITERS, CHAINS, 4)),
            dma, dma, dma,
        ],
        compiler_params=pltpu.CompilerParams(
            collective_id=0, has_side_effects=True, vmem_limit_bytes=60 * 1024 * 1024
        ),
    )(target_points, source_points, target_mass, source_mass, start_dual,
      tile_row.reshape(1, slots), tile_column.reshape(1, slots), tile_count)


def solution(mesh):
    return jax.shard_map(
        local,
        mesh=mesh,
        in_specs=(
            P(None, "row"),
            P(None, "col"),
            P(("row", "col"), None),
            P(("col", "row"), None),
            P(("col", "row"), None),
            P(("row", "col")),
            P(("row", "col")),
            P(("row", "col")),
        ),
        out_specs=(P(("row", "col"), None), P(("col", "row"), None)),
        check_vma=False,
    )
```

```python
import functools

import jax
import jax.numpy as jnp
from jax import lax
from jax.experimental import pallas as pl
from jax.experimental.pallas import tpu as pltpu
from jax.sharding import PartitionSpec as P

MESH = pl.DeviceIdType.MESH
ITERS = 2
CHAINS = 2
GROUP = 16
SCALE = 2.6857913
FINE = 2896.0
COARSE = 256.0
F32 = jnp.float32
BF16 = jnp.bfloat16
I16 = jnp.int16
I32 = jnp.int32


def encode(x):
    level = jnp.log(jnp.maximum(x, 1e-37))
    ref = (level[0:1] * COARSE + 32768.5).astype(I32) - 32768
    fine = level * FINE + (32768.5 - ref.astype(F32) * (FINE / COARSE))
    return (fine.astype(I32) - 32768).astype(I16), ref


def decode(code, ref):
    return jnp.exp(
        code.astype(I32).astype(F32) * (1.0 / FINE) + ref.astype(F32) * (1.0 / COARSE)
    )


def kernel(
    slots,
    tp, sp, tm, sm, sd, tr, tc, tn,
    td_out, so_out,
    meta_own, meta_in, meta, tp_in, sp_in, tm_in, tt, sb, kt, acc,
    src_own, s_band, x0_send, x0_recv, r1_send, r1_recv, r2_recv, part,
    t_band, z_send, z_recv, td_own, t_mass, s_mass, t_all, s_all,
    p_send, p_recv, s_send, s_recv, x_send, x_recv, a_send, a_recv, b_send, b_recv,
    q_send, q_recv, g_send, g_recv, c_send, c_recv, w_send, w_recv, o_send, o_recv, m_sem,
):
    tile = kt.shape[1]
    measures = acc.shape[1]
    mh = measures // CHAINS
    row = lax.axis_index("row")
    col = lax.axis_index("col")
    z_lo, core = row // 2, row % 2
    x, z_hi, y = col // 8, (col // 4) % 2, col % 4
    z = z_hi * 2 + z_lo
    other = 1 - core
    own_role = core == z_hi
    swapped = core != z_hi

    def device(x_, y_, z_, core_):
        return ((z_ % 2) * 2 + core_, x_ * 8 + (z_ // 2) * 4 + y_)

    sibling = device(x, y, z, other)
    partner = device(x, y, core * 2 + z_lo, z_hi)

    ring = {(0, step): device((x + step) % 4, y, z, core) for step in (1, 2, 3)}
    ring.update({(1, step): device(x, (y + step) % 4, z, core) for step in (1, 2, 3)})

    def on_ring(axis, step):
        return ring[axis, step]

    delta = (z + 4 - 2 * core) % 4

    def by_delta(*values):
        return jnp.where(delta < 2, jnp.where(delta == 0, values[0], values[1]),
                         jnp.where(delta == 2, values[2], values[3]))

    relayed, single = by_delta(2, 0, 3, 1), by_delta(3, 1, 2, 0)
    up_band = device(x, y, (z + 1) % 4, z_hi)
    down_band = device(x, y, (z + 3) % 4, z_hi)
    up_core = device(x, y, (z + 1) % 4, core)
    down_core = device(x, y, (z + 3) % 4, core)
    relay_step = by_delta(3, 1, 1, 3)
    relay_on = device(x, y, (z + relay_step) % 4, core)

    def owner(r):
        return device(x, y, core * 2 + r // 2, r % 2)

    def remote(src, dst, send, recv, target):
        return pltpu.make_async_remote_copy(
            src_ref=src, dst_ref=dst, send_sem=send, recv_sem=recv,
            device_id=target, device_id_type=MESH,
        )

    barrier = pltpu.get_barrier_semaphore()
    friends = [device(x, y, (z + dz) % 4, (core + dk) % 2)
               for dz in range(4) for dk in range(2) if dz or dk]
    friends += [on_ring(axis, step) for axis in (0, 1) for step in (1, 2, 3)]
    for friend in friends:
        pl.semaphore_signal(barrier, inc=1, device_id=friend, device_id_type=MESH)

    meta_own[...] = jnp.zeros_like(meta_own)
    meta_own[0:1, 0:slots] = jnp.clip(tr[...], 0, 63)
    meta_own[1:2, 0:slots] = jnp.clip(tc[...], 0, 7)
    lane = lax.broadcasted_iota(I32, (128, 128), 1)
    sub = lax.broadcasted_iota(I32, (128, 128), 0)
    alive = sub < tn[0]
    for k in range(2):
        across = jnp.broadcast_to(meta_own[k:k + 1, :], (128, 128))
        down = across.T
        same = (down == across) & (sub < lane) & alive
        found = jnp.max(jnp.where(same, sub, -1), axis=0, keepdims=True)
        meta_own[2 + k:3 + k, :] = jnp.where(found < 0, slots, found)
        same = (down == lane) & alive
        found = jnp.max(jnp.where(same, sub, -1), axis=0, keepdims=True)
        meta_own[4 + k:5 + k, :] = jnp.where(found < 0, slots, found)
    index = meta_own[0:1, :]
    share = index // 2
    sx, sh, sy = share // 8, (share // 4) % 2, share % 4
    even = ((sh * 2 + 0) * 4 + sx) * 4 + sy
    odd = ((sh * 2 + 1) * 4 + sy) * 4 + sx
    meta_own[6:7, :] = jnp.where(index % 2 == 0, even, odd)

    for k in range(2):
        src_own[0, k] = sd[k * tile:(k + 1) * tile, :].astype(F32).T.astype(BF16)
        s_mass[k] = sm[k * tile:(k + 1) * tile, :].T

    pl.semaphore_wait(barrier, len(friends))

    points_out = remote(tp, tp_in, p_send.at[0], p_recv.at[0], sibling)
    sp_copy = remote(sp, sp_in, p_send.at[1], p_recv.at[1], partner)
    meta_copy = remote(meta_own, meta_in, p_send.at[2], p_recv.at[2], partner)
    tm_copy = remote(tm, tm_in, p_send.at[3], p_recv.at[3], partner)

    @pl.when(own_role)
    def _():
        points_out.start()
        sp_in[...] = sp[...]
        tp_in[...] = tp[...]
        tm_in[...] = tm[...]
        meta_in[...] = meta_own[...]

    @pl.when(swapped)
    def _():
        meta_copy.start()
        sp_copy.start()

    def rows_of(h):
        return slice(h * mh, (h + 1) * mh)

    def source_copy(it, h, step):
        target = (sibling, up_band, None, down_band)[step]
        return remote(
            src_own.at[it, :, rows_of(h)], s_band.at[it, pl.ds(2 * row, 2), rows_of(h)],
            s_send.at[h, step], s_recv.at[it, h, row], target,
        )

    def source_relay(it, h):
        ref = s_band.at[it, pl.ds(2 * relayed, 2), rows_of(h)]
        return remote(ref, ref, s_send.at[h, 2], s_recv.at[it, h, relayed], relay_on)

    def source_send(it, h):
        source_copy(it, h, 1).start()
        source_copy(it, h, 3).start()

        @pl.when(swapped)
        def _():
            source_copy(it, h, 0).start()

        @pl.when(own_role)
        def _():
            s_band[it, pl.ds(2 * row, 2), rows_of(h)] = src_own[it, :, rows_of(h)]

    def source_sent(it, h):
        source_copy(it, h, 1).wait_send()
        source_copy(it, h, 3).wait_send()
        source_relay(it, h).wait_send()

        @pl.when(swapped)
        def _():
            source_copy(it, h, 0).wait_send()

    def source_pass_on(it, h):
        source_relay(it, h).wait_recv()
        source_relay(it, h).start()

    def source_arrived(it, h):
        for r in range(4):
            @pl.when(jnp.logical_and(jnp.logical_or(swapped, row != r), relayed != r))
            def _():
                remote(src_own.at[it, :, rows_of(h)],
                       s_band.at[it, 2 * r:2 * r + 2, rows_of(h)], s_send.at[h, 0],
                       s_recv.at[it, h, r], sibling).wait_recv()

    for h in range(CHAINS):
        source_send(0, h)

    @pl.when(swapped)
    def _():
        meta_copy.wait_recv()
        sp_copy.wait_recv()
        points_out.wait_recv()

    to_scalar = pltpu.make_async_copy(meta_in, meta, m_sem)
    to_scalar.start()

    @pl.loop(0, 8)
    def _(c):
        start = pl.multiple_of(c * tile, tile)
        for k in range(3):
            line = sp_in[k:k + 1, pl.ds(start, tile)] * SCALE
            sb[c, k] = jnp.broadcast_to(line, (128, tile)).T

    @pl.loop(0, 64)
    def _(r):
        tt[r, 0:3] = tp_in[:, pl.ds(pl.multiple_of(r * tile, tile), tile)] * SCALE

    to_scalar.wait()

    acc[slots] = jnp.zeros((measures, tile), F32)

    def make_tile(s):
        r, c = meta[0, s], meta[1, s]
        for part_at in range(tile // 128):
            lanes = slice(part_at * 128, (part_at + 1) * 128)
            distance = (sb[c, 0] - tt[r, 0:1, lanes]) ** 2
            distance = distance + (sb[c, 1] - tt[r, 1:2, lanes]) ** 2
            distance = distance + (sb[c, 2] - tt[r, 2:3, lanes]) ** 2
            kt[s, :, lanes] = jnp.exp2(-8.0 - distance).astype(BF16)

    def row_product(it, s):
        acc[s] = acc[meta[2, s]] + jnp.dot(s_band[it, meta[1, s]], kt[s],
                                           preferred_element_type=F32)

    steps = 14
    first_tiles = slots - 2 * steps

    @pl.loop(0, first_tiles // 2)
    def _(pair):
        make_tile(2 * pair)
        make_tile(2 * pair + 1)

    for h in range(CHAINS):
        source_pass_on(0, h)

    @pl.when(swapped)
    def _():
        tm_copy.start()

    for h in range(CHAINS):
        source_arrived(0, h)

    @pl.loop(0, steps)
    def _(step):
        for m in range(3):
            row_product(0, 3 * step + m)
        for m in range(2):
            make_tile(first_tiles + 2 * step + m)

    for s in range(3 * steps, slots):
        row_product(0, s)

    def write_block(ref, value, n=2):
        line = lax.broadcasted_iota(I32, (16, tile), 0)
        refs = jnp.zeros((16, tile), I32)
        for i in range(n):
            code, ref_row = encode(value(i))
            ref[i * mh:(i + 1) * mh, :] = code
            refs = jnp.where(line == i, ref_row, refs)
        ref[n * mh:n * mh + 16, :] = refs.astype(I16)

    def read_block(ref, i, n=2):
        refs = ref[n * mh:n * mh + 16, :].astype(I32)
        return decode(ref[i * mh:(i + 1) * mh, :], refs[i:i + 1])

    place = ((x, y), (y, x))
    out_copy = remote(td_own, td_out, o_send, o_recv, partner)

    def total(a, d, u, side):
        g = (place[a][0] + d) % 4
        gx, gy = (g, u) if a == 0 else (u, g)
        return meta[4, 2 * (gx * 8 + side * 4 + gy) + a]

    class Chain:
        def __init__(self, h, it):
            self.h, self.it, self.rows = h, it, rows_of(h)

        def x0_copy(self, d):
            h = self.h
            return remote(x0_send.at[h, d], x0_recv.at[h, d], x_send.at[h, d],
                          x_recv.at[self.it, h, d], sibling)

        def r1_copy(self, a, kind):
            h, it = self.h, self.it
            return remote(r1_send.at[h, a, kind], r1_recv.at[it, h, a, kind],
                          a_send.at[h, a, kind], a_recv.at[it, h, a, kind],
                          on_ring(a, 1 if kind % 2 == 0 else 3))

        def r2_copy(self, a, kind):
            h, it, step = self.h, self.it, (1, 3, 2)[kind]
            return remote(part.at[h, a, (place[a][1] + step) % 4], r2_recv.at[it, h, a, kind],
                          b_send.at[h, a, kind], b_recv.at[it, h, a, kind], on_ring(1 - a, step))

        def spot(self, a, g, u, side=None):
            return (((core if side is None else side) * 2 + a) * 4 + g) * 4 + u

        def q_copy(self, a, kind):
            p, q = place[a]
            ref = t_band.at[self.it, self.spot(a, p, q), self.rows]
            return remote(ref, ref, q_send.at[self.h, a, kind],
                          q_recv.at[self.it, self.h, a, kind], on_ring(1 - a, (1, 3, 2)[kind]))

        def q_got(self, a, kind):
            p, q = place[a]
            ref = t_band.at[self.it, self.spot(a, p, (q + (3, 1, 2)[kind]) % 4), self.rows]
            remote(ref, ref, q_send.at[self.h, a, kind],
                   q_recv.at[self.it, self.h, a, kind], sibling).wait_recv()

        def pair(self, a, g, far):
            q = place[a][1]
            begin = 2 * (1 - q // 2) if far else 2 * (q // 2)
            return t_band.at[self.it, pl.ds(self.spot(a, g, begin), 2), self.rows]

        def g_copy(self, a, kind):
            p = place[a][0]
            g = (p, p, p, p, (p + 3) % 4, (p + 1) % 4)[kind]
            ref = self.pair(a, g, kind % 2 == 1)
            return remote(ref, ref, g_send.at[self.h, a, kind], g_recv.at[self.it, self.h, a, kind],
                          on_ring(a, (1, 1, 3, 3, 1, 3)[kind]))

        def g_got(self, a, kind):
            p = place[a][0]
            g = ((p + 3) % 4, (p + 3) % 4, (p + 1) % 4, (p + 1) % 4,
                 (p + 2) % 4, (p + 2) % 4)[kind]
            ref = self.pair(a, g, kind % 2 == 1)
            remote(ref, ref, g_send.at[self.h, a, kind], g_recv.at[self.it, self.h, a, kind],
                   sibling).wait_recv()

        def c_copy(self, a, dg):
            base = self.spot(a, (place[a][0] + dg) % 4, 0)
            ref = t_band.at[self.it, pl.ds(base, 4), self.rows]
            return remote(ref, ref, c_send.at[self.h, a, dg],
                          c_recv.at[self.it, self.h, a, dg], sibling)

        def c_got(self, a, dg):
            base = self.spot(a, (place[a][0] + dg) % 4, 0, other)
            ref = t_band.at[self.it, pl.ds(base, 4), self.rows]
            remote(ref, ref, c_send.at[self.h, a, dg],
                   c_recv.at[self.it, self.h, a, dg], sibling).wait_recv()

        def z_copy(self, kind, r):
            h, it = self.h, self.it
            return remote(z_send.at[h, r], z_recv.at[it, h, kind], w_send.at[h, r],
                          w_recv.at[it, h, kind], owner(r))

        def z_far(self, r, target):
            h, it = self.h, self.it
            return remote(z_send.at[h, r], z_recv.at[it, h, 3], w_send.at[h, r],
                          w_recv.at[it, h, 3], target)

        def to_next(self, r, fn):
            below = (core * 2 + r // 2 + 3) % 4 == z

            @pl.when(below)
            def _():
                fn(self.z_copy(1, r))

            @pl.when(jnp.logical_not(below))
            def _():
                fn(self.z_copy(2, r))

        def own(self, a, d, u):
            return acc[total(a, d, u, core), self.rows] + read_block(
                x0_recv.at[self.h, d], a * 4 + u, 8)

        def stage(self, d):
            write_block(x0_send.at[self.h, d],
                        lambda i: acc[total(i // 4, d, i % 4, other), self.rows], 8)
            self.x0_copy(d).start()

        def ring_far(self):
            self.x0_copy(2).wait_recv()
            for a in range(2):
                for kind, d, u0 in ((0, 2, 0), (1, 2, 2)):
                    write_block(r1_send.at[self.h, a, kind], lambda i: self.own(a, d, u0 + i))
                    self.r1_copy(a, kind).start()

        def ring_near(self):
            for kind, d, u0 in ((2, 1, 2), (3, 3, 0)):
                self.x0_copy(d).wait_recv()
                for a in range(2):
                    write_block(r1_send.at[self.h, a, kind], lambda i: self.own(a, d, u0 + i))
                    self.r1_copy(a, kind).start()

        def ring_relay(self):
            for a in range(2):
                for kind, d, u0 in ((4, 1, 0), (5, 3, 2)):
                    self.r1_copy(a, kind - 4).wait_recv()
                    got = r1_recv.at[self.it, self.h, a, kind - 4]
                    write_block(r1_send.at[self.h, a, kind],
                                lambda i: self.own(a, d, u0 + i) + read_block(got, i))
                    self.r1_copy(a, kind).start()

        def ring_sum(self):
            h, it = self.h, self.it
            self.x0_copy(0).wait_recv()
            for a in range(2):
                self.r1_copy(a, 2).wait_recv()
                self.r1_copy(a, 3).wait_recv()

                for i in range(2):
                    part[h, a, i] = self.own(a, 0, i) + read_block(r1_recv.at[it, h, a, 3], i)
                    part[h, a, 2 + i] = self.own(a, 0, 2 + i) + read_block(
                        r1_recv.at[it, h, a, 2], i)

        def ring_total(self):
            h, it = self.h, self.it
            for a in range(2):
                self.r1_copy(a, 4).wait_recv()
                self.r1_copy(a, 5).wait_recv()
                for i in range(2):
                    part[h, a, i] += read_block(r1_recv.at[it, h, a, 4], i)
                    part[h, a, 2 + i] += read_block(r1_recv.at[it, h, a, 5], i)
                for kind in (2, 0, 1):
                    self.r2_copy(a, kind).start()

        def target(self):
            h, it = self.h, self.it
            for a in range(2):
                p, q = place[a]
                for kind in range(3):
                    self.r2_copy(a, kind).wait_recv()
                sums = (part[h, a, q] + r2_recv[it, h, a, 0]) + (
                    r2_recv[it, h, a, 1] + r2_recv[it, h, a, 2])
                dual = t_mass[a, self.rows] / sums
                t_band[it, self.spot(a, p, q), self.rows] = dual.astype(BF16)
                for kind in (2, 0, 1):
                    self.q_copy(a, kind).start()
                t_all[a, self.rows] = dual

        def gather_near(self):
            for a in range(2):
                self.q_got(a, 0)
                self.q_got(a, 1)
                self.g_copy(a, 0).start()
                self.g_copy(a, 2).start()

        def gather_block(self):
            for a in range(2):
                self.q_got(a, 2)
                self.g_copy(a, 3).start()
                self.g_copy(a, 1).start()
                self.g_got(a, 0)
                self.g_copy(a, 4).start()
            for a in range(2):
                self.c_copy(a, 0).start()

        def gather_relay(self):
            for a in range(2):
                self.g_got(a, 3)
                self.g_copy(a, 5).start()
            for a in range(2):
                self.g_got(a, 1)
                self.c_copy(a, 3).start()
                self.g_got(a, 2)
                self.c_copy(a, 1).start()

        def gather_last(self):
            for a in range(2):
                self.g_got(a, 4)
                self.g_got(a, 5)
                self.c_copy(a, 2).start()

        def gathered(self):
            for dg in (0, 3, 1, 2):
                for a in range(2):
                    self.c_got(a, dg)

        def to_owner(self):
            h, it = self.h, self.it
            first = 2 * (delta % 2)
            for at in range(2):
                r = first + at
                write_block(z_send.at[h, r], lambda i: acc[meta[5, 2 * r + i], self.rows])

                @pl.when(swapped)
                def _():
                    self.z_far(r, device(
                        x, y, (z + jnp.where((delta == 2) == (at == 0), 3, 1)) % 4, core)).start()

                @pl.when(jnp.logical_and(own_role, core != at))
                def _():
                    self.z_copy(0, r).start()

                @pl.when(jnp.logical_and(own_role, core == at))
                def _():
                    z_recv[it, h, 0] = z_send[h, r]

            write_block(z_send.at[h, single], lambda i: acc[meta[5, 2 * single + i], self.rows])
            self.to_next(single, lambda copy: copy.start())

        def to_owner_relay(self):
            h, it = self.h, self.it
            self.z_far(0, sibling).wait_recv()
            got = z_recv.at[it, h, 3]
            write_block(z_send.at[h, relayed],
                        lambda i: acc[meta[5, 2 * relayed + i], self.rows] + read_block(got, i))
            self.to_next(relayed, lambda copy: copy.start())

        def source(self):
            h, it = self.h, self.it
            for kind in range(3):
                @pl.when(jnp.logical_or(swapped, kind != 0))
                def _():
                    self.z_copy(kind, 0).wait_recv()

            for k in range(2):
                sums = read_block(z_recv.at[it, h, 0], k)
                for kind in (1, 2):
                    sums = sums + read_block(z_recv.at[it, h, kind], k)
                dual = s_mass[k, self.rows] / sums
                s_all[k, self.rows] = dual

                @pl.when(it < ITERS - 1)
                def _():
                    src_own[1, k, self.rows] = dual.astype(BF16)

            source_sent(it, h)

            @pl.when(it < ITERS - 1)
            def _():
                source_send(1, h)

        def sent(self):
            h = self.h
            for d in range(4):
                self.x0_copy(d).wait_send()
            for a in range(2):
                for kind in range(6):
                    self.r1_copy(a, kind).wait_send()
                    self.g_copy(a, kind).wait_send()
                for kind in range(3):
                    self.r2_copy(a, kind).wait_send()
                    self.q_copy(a, kind).wait_send()
                for kind in range(4):
                    self.c_copy(a, kind).wait_send()
            first = 2 * (delta % 2)
            for at in range(2):
                @pl.when(jnp.logical_or(swapped, core != at))
                def _():
                    self.z_far(first + at, sibling).wait_send()
            for r in (single, relayed):
                self.z_copy(1, r).wait_send()

    def iteration(it, _):
        chains = [Chain(h, it) for h in range(CHAINS)]

        @pl.when(it > 0)
        def _():
            for h in range(CHAINS):
                source_arrived(1, h)

            @pl.loop(0, slots // GROUP)
            def _(group):
                for m in range(GROUP):
                    row_product(1, group * GROUP + m)

        for chain in chains:
            chain.stage(2)
        for chain in chains:
            chain.stage(1)
            chain.stage(3)
        for name in ("ring_far", "ring_near", "ring_relay", "ring_sum", "ring_total",
                     "target", "gather_near", "gather_block", "gather_relay",
                     "gather_last"):
            for chain in chains:
                getattr(chain, name)()
            if name == "ring_far":
                for chain in chains:
                    chain.stage(0)
            if name == "ring_near":
                @pl.when(it == 0)
                def _():
                    @pl.when(swapped)
                    def _():
                        tm_copy.wait_recv()

                    for k in range(2):
                        t_mass[k] = tm_in[k * tile:(k + 1) * tile, :].T

        @pl.when(it == ITERS - 1)
        def _():
            for a in range(2):
                td_own[a * tile:(a + 1) * tile, :] = t_all[a].T

            @pl.when(swapped)
            def _():
                out_copy.start()

            @pl.when(own_role)
            def _():
                td_out[...] = td_own[...]

        for chain in chains:
            chain.gathered()

        @pl.loop(0, slots // GROUP)
        def _(group):
            for m in range(GROUP):
                s = group * GROUP + m
                acc[s] = acc[meta[3, s]] + lax.dot_general(
                    t_band[it, meta[6, s]], kt[s], (((1,), (1,)), ((), ())),
                    preferred_element_type=F32)

        for name in ("to_owner", "to_owner_relay", "source"):
            for chain in chains:
                getattr(chain, name)()

        @pl.when(it < ITERS - 1)
        def _():
            for h in range(CHAINS):
                source_pass_on(1, h)

        for chain in chains:
            chain.sent()
        return 0

    lax.fori_loop(0, ITERS, iteration, 0)
    for k in range(2):
        so_out[k * tile:(k + 1) * tile, :] = s_all[k].T

    @pl.when(own_role)
    def _():
        points_out.wait_send()

    @pl.when(swapped)
    def _():
        out_copy.wait()
        meta_copy.wait_send()
        sp_copy.wait_send()
        tm_copy.wait_send()


def local(target_points, source_points, target_mass, source_mass, start_dual,
          tile_row, tile_column, tile_count):
    slots = tile_row.shape[0]
    rows, measures = target_mass.shape
    tile = rows // 2
    mh = measures // CHAINS
    dma = pltpu.SemaphoreType.DMA
    vmem = pltpu.VMEM
    whole = pl.BlockSpec(memory_space=pltpu.VMEM)
    block = 2 * mh + 16
    return pl.pallas_call(
        functools.partial(kernel, slots),
        out_shape=(
            jax.ShapeDtypeStruct((rows, measures), F32),
            jax.ShapeDtypeStruct((rows, measures), F32),
        ),
        in_specs=[whole] * 7 + [pl.BlockSpec(memory_space=pltpu.SMEM)],
        out_specs=(whole, whole),
        scratch_shapes=[
            vmem((8, 128), I32),
            vmem((8, 128), I32),
            pltpu.SMEM((8, 128), I32),
            vmem(target_points.shape, F32),
            vmem(source_points.shape, F32),
            vmem((rows, measures), F32),
            vmem((64, 8, tile), F32),
            vmem((8, 3, tile, 128), F32),
            vmem((slots, tile, tile), BF16),
            vmem((slots + 1, measures, tile), F32),
            vmem((ITERS, 2, measures, tile), BF16),
            vmem((ITERS, 8, measures, tile), BF16),
            vmem((CHAINS, 4, 8 * mh + 16, tile), I16),
            vmem((CHAINS, 4, 8 * mh + 16, tile), I16),
            vmem((CHAINS, 2, 6, block, tile), I16),
            vmem((ITERS, CHAINS, 2, 6, block, tile), I16),
            vmem((ITERS, CHAINS, 2, 3, mh, tile), F32),
            vmem((CHAINS, 2, 4, mh, tile), F32),
            vmem((ITERS, 64, measures, tile), BF16),
            vmem((CHAINS, 4, block, tile), I16),
            vmem((ITERS, CHAINS, 4, block, tile), I16),
            vmem((rows, measures), F32),
            vmem((2, measures, tile), F32),
            vmem((2, measures, tile), F32),
            vmem((2, measures, tile), F32),
            vmem((2, measures, tile), F32),
            dma((4,)), dma((4,)),
            dma((CHAINS, 4)), dma((ITERS, CHAINS, 4)),
            dma((CHAINS, 4)), dma((ITERS, CHAINS, 4)),
            dma((CHAINS, 2, 6)), dma((ITERS, CHAINS, 2, 6)),
            dma((CHAINS, 2, 3)), dma((ITERS, CHAINS, 2, 3)),
            dma((CHAINS, 2, 3)), dma((ITERS, CHAINS, 2, 3)),
            dma((CHAINS, 2, 6)), dma((ITERS, CHAINS, 2, 6)),
            dma((CHAINS, 2, 4)), dma((ITERS, CHAINS, 2, 4)),
            dma((CHAINS, 4)), dma((ITERS, CHAINS, 4)),
            dma, dma, dma,
        ],
        compiler_params=pltpu.CompilerParams(
            collective_id=0, has_side_effects=True, vmem_limit_bytes=60 * 1024 * 1024
        ),
    )(target_points, source_points, target_mass, source_mass, start_dual,
      tile_row.reshape(1, slots), tile_column.reshape(1, slots), tile_count)


def solution(mesh):
    return jax.shard_map(
        local,
        mesh=mesh,
        in_specs=(
            P(None, "row"),
            P(None, "col"),
            P(("row", "col"), None),
            P(("col", "row"), None),
            P(("col", "row"), None),
            P(("row", "col")),
            P(("row", "col")),
            P(("row", "col")),
        ),
        out_specs=(P(("row", "col"), None), P(("col", "row"), None)),
        check_vma=False,
    )
```

```python
import functools

import jax
import jax.numpy as jnp
from jax import lax
from jax.experimental import pallas as pl
from jax.experimental.pallas import tpu as pltpu
from jax.sharding import PartitionSpec as P

MESH = pl.DeviceIdType.MESH
ITERS = 2
CHAINS = 2
GROUP = 16
SCALE = 2.6857913
FINE = 2896.0
COARSE = 256.0
F32 = jnp.float32
BF16 = jnp.bfloat16
I16 = jnp.int16
I32 = jnp.int32


def encode(x):
    level = jnp.log(jnp.maximum(x, 1e-37))
    ref = (level[0:1] * COARSE + 32768.5).astype(I32) - 32768
    fine = level * FINE + (32768.5 - ref.astype(F32) * (FINE / COARSE))
    return (fine.astype(I32) - 32768).astype(I16), ref


def decode(code, ref):
    return jnp.exp(
        code.astype(I32).astype(F32) * (1.0 / FINE) + ref.astype(F32) * (1.0 / COARSE)
    )


def kernel(
    slots,
    tp, sp, tm, sm, sd, tr, tc, tn,
    td_out, so_out,
    meta_own, meta_in, meta, tp_in, sp_in, tm_in, tt, sb, kt, acc,
    src_own, s_band, x0_send, x0_recv, r1_send, r1_recv, r2_send, r2_recv, part,
    t_band, z_send, z_recv, td_own, t_mass, s_mass, t_all, s_all,
    p_send, p_recv, s_send, s_recv, x_send, x_recv, a_send, a_recv, b_send, b_recv,
    q_send, q_recv, g_send, g_recv, c_send, c_recv, w_send, w_recv, o_send, o_recv, m_sem,
):
    tile = kt.shape[1]
    measures = acc.shape[1]
    mh = measures // CHAINS
    row = lax.axis_index("row")
    col = lax.axis_index("col")
    z_lo, core = row // 2, row % 2
    x, z_hi, y = col // 8, (col // 4) % 2, col % 4
    z = z_hi * 2 + z_lo
    other = 1 - core
    own_role = core == z_hi
    swapped = core != z_hi

    def device(x_, y_, z_, core_):
        return ((z_ % 2) * 2 + core_, x_ * 8 + (z_ // 2) * 4 + y_)

    sibling = device(x, y, z, other)
    partner = device(x, y, core * 2 + z_lo, z_hi)

    ring = {(0, step): device((x + step) % 4, y, z, core) for step in (1, 2, 3)}
    ring.update({(1, step): device(x, (y + step) % 4, z, core) for step in (1, 2, 3)})

    def on_ring(axis, step):
        return ring[axis, step]

    delta = (z + 4 - 2 * core) % 4

    def by_delta(*values):
        return jnp.where(delta < 2, jnp.where(delta == 0, values[0], values[1]),
                         jnp.where(delta == 2, values[2], values[3]))

    relayed, single = by_delta(2, 0, 3, 1), by_delta(3, 1, 2, 0)
    up_band = device(x, y, (z + 1) % 4, z_hi)
    down_band = device(x, y, (z + 3) % 4, z_hi)
    up_core = device(x, y, (z + 1) % 4, core)
    down_core = device(x, y, (z + 3) % 4, core)
    relay_step = by_delta(3, 1, 1, 3)
    relay_on = device(x, y, (z + relay_step) % 4, core)

    def owner(r):
        return device(x, y, core * 2 + r // 2, r % 2)

    def remote(src, dst, send, recv, target):
        return pltpu.make_async_remote_copy(
            src_ref=src, dst_ref=dst, send_sem=send, recv_sem=recv,
            device_id=target, device_id_type=MESH,
        )

    barrier = pltpu.get_barrier_semaphore()
    friends = [device(x, y, (z + dz) % 4, (core + dk) % 2)
               for dz in range(4) for dk in range(2) if dz or dk]
    friends += [on_ring(axis, step) for axis in (0, 1) for step in (1, 2, 3)]
    for friend in friends:
        pl.semaphore_signal(barrier, inc=1, device_id=friend, device_id_type=MESH)

    meta_own[...] = jnp.zeros_like(meta_own)
    meta_own[0:1, 0:slots] = jnp.clip(tr[...], 0, 63)
    meta_own[1:2, 0:slots] = jnp.clip(tc[...], 0, 7)
    lane = lax.broadcasted_iota(I32, (128, 128), 1)
    sub = lax.broadcasted_iota(I32, (128, 128), 0)
    alive = sub < tn[0]
    for k in range(2):
        across = jnp.broadcast_to(meta_own[k:k + 1, :], (128, 128))
        down = across.T
        same = (down == across) & (sub < lane) & alive
        found = jnp.max(jnp.where(same, sub, -1), axis=0, keepdims=True)
        meta_own[2 + k:3 + k, :] = jnp.where(found < 0, slots, found)
        same = (down == lane) & alive
        found = jnp.max(jnp.where(same, sub, -1), axis=0, keepdims=True)
        meta_own[4 + k:5 + k, :] = jnp.where(found < 0, slots, found)
    index = meta_own[0:1, :]
    share = index // 2
    sx, sh, sy = share // 8, (share // 4) % 2, share % 4
    even = ((sh * 2 + 0) * 4 + sx) * 4 + sy
    odd = ((sh * 2 + 1) * 4 + sy) * 4 + sx
    meta_own[6:7, :] = jnp.where(index % 2 == 0, even, odd)

    for k in range(2):
        src_own[0, k] = sd[k * tile:(k + 1) * tile, :].astype(F32).T.astype(BF16)
        s_mass[k] = sm[k * tile:(k + 1) * tile, :].T

    pl.semaphore_wait(barrier, len(friends))

    points_out = remote(tp, tp_in, p_send.at[0], p_recv.at[0], sibling)
    sp_copy = remote(sp, sp_in, p_send.at[1], p_recv.at[1], partner)
    meta_copy = remote(meta_own, meta_in, p_send.at[2], p_recv.at[2], partner)
    tm_copy = remote(tm, tm_in, p_send.at[3], p_recv.at[3], partner)

    @pl.when(own_role)
    def _():
        points_out.start()
        sp_in[...] = sp[...]
        tp_in[...] = tp[...]
        tm_in[...] = tm[...]
        meta_in[...] = meta_own[...]

    @pl.when(swapped)
    def _():
        meta_copy.start()
        sp_copy.start()

    def rows_of(h):
        return slice(h * mh, (h + 1) * mh)

    def source_copy(it, h, step):
        target = (sibling, up_band, None, down_band)[step]
        return remote(
            src_own.at[it, :, rows_of(h)], s_band.at[it, pl.ds(2 * row, 2), rows_of(h)],
            s_send.at[h, step], s_recv.at[it, h, row], target,
        )

    def source_relay(it, h):
        ref = s_band.at[it, pl.ds(2 * relayed, 2), rows_of(h)]
        return remote(ref, ref, s_send.at[h, 2], s_recv.at[it, h, relayed], relay_on)

    def source_send(it, h):
        source_copy(it, h, 1).start()
        source_copy(it, h, 3).start()

        @pl.when(swapped)
        def _():
            source_copy(it, h, 0).start()

        @pl.when(own_role)
        def _():
            s_band[it, pl.ds(2 * row, 2), rows_of(h)] = src_own[it, :, rows_of(h)]

    def source_sent(it, h):
        source_copy(it, h, 1).wait_send()
        source_copy(it, h, 3).wait_send()
        source_relay(it, h).wait_send()

        @pl.when(swapped)
        def _():
            source_copy(it, h, 0).wait_send()

    def source_pass_on(it, h):
        source_relay(it, h).wait_recv()
        source_relay(it, h).start()

    def source_arrived(it, h):
        for r in range(4):
            @pl.when(jnp.logical_and(jnp.logical_or(swapped, row != r), relayed != r))
            def _():
                remote(src_own.at[it, :, rows_of(h)],
                       s_band.at[it, 2 * r:2 * r + 2, rows_of(h)], s_send.at[h, 0],
                       s_recv.at[it, h, r], sibling).wait_recv()

    for h in range(CHAINS):
        source_send(0, h)

    @pl.when(swapped)
    def _():
        meta_copy.wait_recv()
        sp_copy.wait_recv()
        points_out.wait_recv()

    to_scalar = pltpu.make_async_copy(meta_in, meta, m_sem)
    to_scalar.start()

    @pl.loop(0, 8)
    def _(c):
        start = pl.multiple_of(c * tile, tile)
        for k in range(3):
            line = sp_in[k:k + 1, pl.ds(start, tile)] * SCALE
            sb[c, k] = jnp.broadcast_to(line, (128, tile)).T

    @pl.loop(0, 64)
    def _(r):
        tt[r, 0:3] = tp_in[:, pl.ds(pl.multiple_of(r * tile, tile), tile)] * SCALE

    to_scalar.wait()

    acc[slots] = jnp.zeros((measures, tile), F32)

    def make_tile(s):
        r, c = meta[0, s], meta[1, s]
        for part_at in range(tile // 128):
            lanes = slice(part_at * 128, (part_at + 1) * 128)
            distance = (sb[c, 0] - tt[r, 0:1, lanes]) ** 2
            distance = distance + (sb[c, 1] - tt[r, 1:2, lanes]) ** 2
            distance = distance + (sb[c, 2] - tt[r, 2:3, lanes]) ** 2
            kt[s, :, lanes] = jnp.exp2(-8.0 - distance).astype(BF16)

    def row_product(it, s):
        acc[s] = acc[meta[2, s]] + jnp.dot(s_band[it, meta[1, s]], kt[s],
                                           preferred_element_type=F32)

    steps = 14
    first_tiles = slots - 2 * steps

    @pl.loop(0, first_tiles // 2)
    def _(pair):
        make_tile(2 * pair)
        make_tile(2 * pair + 1)

    for h in range(CHAINS):
        source_pass_on(0, h)

    @pl.when(swapped)
    def _():
        tm_copy.start()

    for h in range(CHAINS):
        source_arrived(0, h)

    @pl.loop(0, steps)
    def _(step):
        for m in range(3):
            row_product(0, 3 * step + m)
        for m in range(2):
            make_tile(first_tiles + 2 * step + m)

    for s in range(3 * steps, slots):
        row_product(0, s)

    def write_block(ref, values):
        n = len(values)
        line = lax.broadcasted_iota(I32, (16, tile), 0)
        refs = jnp.zeros((16, tile), I32)
        for i in range(n):
            code, ref_row = encode(values[i]())
            ref[i * mh:(i + 1) * mh, :] = code
            refs = jnp.where(line == i, ref_row, refs)
        ref[n * mh:n * mh + 16, :] = refs.astype(I16)

    def read_block(ref, i, n=2):
        refs = ref[n * mh:n * mh + 16, :].astype(I32)
        return decode(ref[i * mh:(i + 1) * mh, :], refs[i:i + 1])

    place = ((x, y), (y, x))
    out_copy = remote(td_own, td_out, o_send, o_recv, partner)

    def total(a, d, u, side):
        g = (place[a][0] + d) % 4
        gx, gy = (g, u) if a == 0 else (u, g)
        return meta[4, 2 * (gx * 8 + side * 4 + gy) + a]

    class Chain:
        def __init__(self, h, it):
            self.h, self.it, self.rows = h, it, rows_of(h)

        def x0_copy(self, d):
            h = self.h
            return remote(x0_send.at[h, d], x0_recv.at[h, d], x_send.at[h, d],
                          x_recv.at[self.it, h, d], sibling)

        def r1_rows(self, kind):
            return slice(0, (4 if kind < 2 else 2) * mh + 16)

        def r1_copy(self, a, kind):
            h, it, rows = self.h, self.it, self.r1_rows(kind)
            return remote(r1_send.at[h, a, kind, rows], r1_recv.at[it, h, a, kind, rows],
                          a_send.at[h, a, kind], a_recv.at[it, h, a, kind],
                          on_ring(a, 1 if kind % 2 == 0 else 3))

        def r2_copy(self, a, kind):
            h, it, step = self.h, self.it, (1, 3, 2)[kind]
            return remote(r2_send.at[h, a, kind], r2_recv.at[it, h, a, kind],
                          b_send.at[h, a, kind], b_recv.at[it, h, a, kind], on_ring(1 - a, step))

        def spot(self, a, g, u, side=None):
            return (((core if side is None else side) * 2 + a) * 4 + g) * 4 + u

        def q_copy(self, a, kind):
            p, q = place[a]
            ref = t_band.at[self.it, self.spot(a, p, q), self.rows]
            return remote(ref, ref, q_send.at[self.h, a, kind],
                          q_recv.at[self.it, self.h, a, kind], on_ring(1 - a, (1, 3, 2)[kind]))

        def q_got(self, a, kind):
            p, q = place[a]
            ref = t_band.at[self.it, self.spot(a, p, (q + (3, 1, 2)[kind]) % 4), self.rows]
            remote(ref, ref, q_send.at[self.h, a, kind],
                   q_recv.at[self.it, self.h, a, kind], sibling).wait_recv()

        def pair(self, a, g, far):
            q = place[a][1]
            begin = 2 * (1 - q // 2) if far else 2 * (q // 2)
            return t_band.at[self.it, pl.ds(self.spot(a, g, begin), 2), self.rows]

        def g_copy(self, a, kind):
            p = place[a][0]
            g = (p, p, p, p, (p + 3) % 4, (p + 1) % 4)[kind]
            ref = self.pair(a, g, kind % 2 == 1)
            return remote(ref, ref, g_send.at[self.h, a, kind], g_recv.at[self.it, self.h, a, kind],
                          on_ring(a, (1, 1, 3, 3, 1, 3)[kind]))

        def g_got(self, a, kind):
            p = place[a][0]
            g = ((p + 3) % 4, (p + 3) % 4, (p + 1) % 4, (p + 1) % 4,
                 (p + 2) % 4, (p + 2) % 4)[kind]
            ref = self.pair(a, g, kind % 2 == 1)
            remote(ref, ref, g_send.at[self.h, a, kind], g_recv.at[self.it, self.h, a, kind],
                   sibling).wait_recv()

        def c_copy(self, a, dg):
            base = self.spot(a, (place[a][0] + dg) % 4, 0)
            ref = t_band.at[self.it, pl.ds(base, 4), self.rows]
            return remote(ref, ref, c_send.at[self.h, a, dg],
                          c_recv.at[self.it, self.h, a, dg], sibling)

        def c_got(self, a, dg):
            base = self.spot(a, (place[a][0] + dg) % 4, 0, other)
            ref = t_band.at[self.it, pl.ds(base, 4), self.rows]
            remote(ref, ref, c_send.at[self.h, a, dg],
                   c_recv.at[self.it, self.h, a, dg], sibling).wait_recv()

        def z_copy(self, kind, r):
            h, it = self.h, self.it
            return remote(z_send.at[h, r], z_recv.at[it, h, kind], w_send.at[h, r],
                          w_recv.at[it, h, kind], owner(r))

        def z_far(self, r, target):
            h, it = self.h, self.it
            return remote(z_send.at[h, r], z_recv.at[it, h, 3], w_send.at[h, r],
                          w_recv.at[it, h, 3], target)

        def to_next(self, r, fn):
            below = (core * 2 + r // 2 + 3) % 4 == z

            @pl.when(below)
            def _():
                fn(self.z_copy(1, r))

            @pl.when(jnp.logical_not(below))
            def _():
                fn(self.z_copy(2, r))

        def own(self, a, d, u):
            return acc[total(a, d, u, core), self.rows] + x0_recv[self.h, d, a, u]

        def stage(self, d):
            for a in range(2):
                @pl.loop(0, 4)
                def _(u):
                    x0_send[self.h, d, a, u] = acc[total(a, d, u, other), self.rows]

            self.x0_copy(d).start()

        def ring_first(self):
            for d in (2, 1, 3):
                self.x0_copy(d).wait_recv()
            for a in range(2):
                for kind, d, far, near in ((0, 1, 0, 2), (1, 3, 2, 0)):
                    write_block(r1_send.at[self.h, a, kind],
                                [functools.partial(self.own, a, 2, far + i) for i in range(2)]
                                + [functools.partial(self.own, a, d, near + i) for i in range(2)])
                    self.r1_copy(a, kind).start()

        def ring_relay(self):
            h, it = self.h, self.it
            for a in range(2):
                for kind, d, u0 in ((2, 1, 0), (3, 3, 2)):
                    self.r1_copy(a, kind - 2).wait_recv()
                    got = r1_recv.at[it, h, a, kind - 2]
                    write_block(r1_send.at[h, a, kind],
                                [lambda i=i: self.own(a, d, u0 + i) + read_block(got, i, 4)
                                 for i in range(2)])
                    self.r1_copy(a, kind).start()

        def ring_sum(self):
            h, it = self.h, self.it
            self.x0_copy(0).wait_recv()
            for a in range(2):
                for i in range(2):
                    part[h, a, i] = self.own(a, 0, i) + read_block(
                        r1_recv.at[it, h, a, 1], 2 + i, 4)
                    part[h, a, 2 + i] = self.own(a, 0, 2 + i) + read_block(
                        r1_recv.at[it, h, a, 0], 2 + i, 4)

        def ring_total(self):
            h, it = self.h, self.it
            for a in range(2):
                q = place[a][1]
                self.r1_copy(a, 2).wait_recv()
                self.r1_copy(a, 3).wait_recv()
                for i in range(2):
                    part[h, a, i] += read_block(r1_recv.at[it, h, a, 2], i)
                    part[h, a, 2 + i] += read_block(r1_recv.at[it, h, a, 3], i)
                for kind in (2, 0, 1):
                    write_block(r2_send.at[h, a, kind],
                                [lambda: part[h, a, (q + (1, 3, 2)[kind]) % 4]])
                    self.r2_copy(a, kind).start()

        def target(self):
            h, it = self.h, self.it
            for a in range(2):
                p, q = place[a]
                for kind in range(3):
                    self.r2_copy(a, kind).wait_recv()
                sums = part[h, a, q]
                for kind in range(3):
                    sums = sums + read_block(r2_recv.at[it, h, a, kind], 0, 1)
                dual = t_mass[a, self.rows] / sums
                t_band[it, self.spot(a, p, q), self.rows] = dual.astype(BF16)
                for kind in (2, 0, 1):
                    self.q_copy(a, kind).start()
                t_all[a, self.rows] = dual

        def gather_near(self):
            for a in range(2):
                self.q_got(a, 0)
                self.q_got(a, 1)
                self.g_copy(a, 0).start()
                self.g_copy(a, 2).start()

        def gather_block(self):
            for a in range(2):
                self.q_got(a, 2)
                self.g_copy(a, 3).start()
                self.g_copy(a, 1).start()
                self.g_got(a, 0)
                self.g_copy(a, 4).start()
            for a in range(2):
                self.c_copy(a, 0).start()

        def gather_relay(self):
            for a in range(2):
                self.g_got(a, 3)
                self.g_copy(a, 5).start()
            for a in range(2):
                self.g_got(a, 1)
                self.c_copy(a, 3).start()
                self.g_got(a, 2)
                self.c_copy(a, 1).start()

        def gather_last(self):
            for a in range(2):
                self.g_got(a, 4)
                self.g_got(a, 5)
                self.c_copy(a, 2).start()

        def gathered(self):
            for dg in (0, 3, 1, 2):
                for a in range(2):
                    self.c_got(a, dg)

        def to_owner(self):
            h, it = self.h, self.it
            first = 2 * (delta % 2)
            for at in range(2):
                r = first + at
                write_block(z_send.at[h, r],
                            [lambda i=i: acc[meta[5, 2 * r + i], self.rows] for i in range(2)])

                @pl.when(swapped)
                def _():
                    self.z_far(r, device(
                        x, y, (z + jnp.where((delta == 2) == (at == 0), 3, 1)) % 4, core)).start()

                @pl.when(jnp.logical_and(own_role, core != at))
                def _():
                    self.z_copy(0, r).start()

                @pl.when(jnp.logical_and(own_role, core == at))
                def _():
                    z_recv[it, h, 0] = z_send[h, r]

            write_block(z_send.at[h, single],
                        [lambda i=i: acc[meta[5, 2 * single + i], self.rows] for i in range(2)])
            self.to_next(single, lambda copy: copy.start())

        def to_owner_relay(self):
            h, it = self.h, self.it
            self.z_far(0, sibling).wait_recv()
            got = z_recv.at[it, h, 3]
            write_block(z_send.at[h, relayed],
                        [lambda i=i: acc[meta[5, 2 * relayed + i], self.rows]
                         + read_block(got, i) for i in range(2)])
            self.to_next(relayed, lambda copy: copy.start())

        def source(self):
            h, it = self.h, self.it
            for kind in range(3):
                @pl.when(jnp.logical_or(swapped, kind != 0))
                def _():
                    self.z_copy(kind, 0).wait_recv()

            for k in range(2):
                sums = read_block(z_recv.at[it, h, 0], k)
                for kind in (1, 2):
                    sums = sums + read_block(z_recv.at[it, h, kind], k)
                dual = s_mass[k, self.rows] / sums
                s_all[k, self.rows] = dual

                @pl.when(it < ITERS - 1)
                def _():
                    src_own[1, k, self.rows] = dual.astype(BF16)

            source_sent(it, h)

            @pl.when(it < ITERS - 1)
            def _():
                source_send(1, h)

        def sent(self):
            h = self.h
            for d in range(4):
                self.x0_copy(d).wait_send()
            for a in range(2):
                for kind in range(4):
                    self.r1_copy(a, kind).wait_send()
                for kind in range(6):
                    self.g_copy(a, kind).wait_send()
                for kind in range(3):
                    self.r2_copy(a, kind).wait_send()
                    self.q_copy(a, kind).wait_send()
                for kind in range(4):
                    self.c_copy(a, kind).wait_send()
            first = 2 * (delta % 2)
            for at in range(2):
                @pl.when(jnp.logical_or(swapped, core != at))
                def _():
                    self.z_far(first + at, sibling).wait_send()
            for r in (single, relayed):
                self.z_copy(1, r).wait_send()

    def iteration(it, _):
        chains = [Chain(h, it) for h in range(CHAINS)]

        @pl.when(it > 0)
        def _():
            for h in range(CHAINS):
                source_arrived(1, h)

            @pl.loop(0, slots // GROUP)
            def _(group):
                for m in range(GROUP):
                    row_product(1, group * GROUP + m)

        for d in (2, 1, 3, 0):
            for chain in chains:
                chain.stage(d)
        for name in ("ring_first", "ring_relay", "ring_sum", "ring_total",
                     "target", "gather_near", "gather_block", "gather_relay",
                     "gather_last"):
            for chain in chains:
                getattr(chain, name)()
            if name == "ring_first":
                @pl.when(it == 0)
                def _():
                    @pl.when(swapped)
                    def _():
                        tm_copy.wait_recv()

                    for k in range(2):
                        t_mass[k] = tm_in[k * tile:(k + 1) * tile, :].T

        @pl.when(it == ITERS - 1)
        def _():
            for a in range(2):
                td_own[a * tile:(a + 1) * tile, :] = t_all[a].T

            @pl.when(swapped)
            def _():
                out_copy.start()

            @pl.when(own_role)
            def _():
                td_out[...] = td_own[...]

        for chain in chains:
            chain.gathered()

        @pl.loop(0, slots // GROUP)
        def _(group):
            for m in range(GROUP):
                s = group * GROUP + m
                acc[s] = acc[meta[3, s]] + lax.dot_general(
                    t_band[it, meta[6, s]], kt[s], (((1,), (1,)), ((), ())),
                    preferred_element_type=F32)

        for name in ("to_owner", "to_owner_relay", "source"):
            for chain in chains:
                getattr(chain, name)()

        @pl.when(it < ITERS - 1)
        def _():
            for h in range(CHAINS):
                source_pass_on(1, h)

        for chain in chains:
            chain.sent()
        return 0

    lax.fori_loop(0, ITERS, iteration, 0)
    for k in range(2):
        so_out[k * tile:(k + 1) * tile, :] = s_all[k].T

    @pl.when(own_role)
    def _():
        points_out.wait_send()

    @pl.when(swapped)
    def _():
        out_copy.wait()
        meta_copy.wait_send()
        sp_copy.wait_send()
        tm_copy.wait_send()


def local(target_points, source_points, target_mass, source_mass, start_dual,
          tile_row, tile_column, tile_count):
    slots = tile_row.shape[0]
    rows, measures = target_mass.shape
    tile = rows // 2
    mh = measures // CHAINS
    dma = pltpu.SemaphoreType.DMA
    vmem = pltpu.VMEM
    whole = pl.BlockSpec(memory_space=pltpu.VMEM)
    block = 2 * mh + 16
    return pl.pallas_call(
        functools.partial(kernel, slots),
        out_shape=(
            jax.ShapeDtypeStruct((rows, measures), F32),
            jax.ShapeDtypeStruct((rows, measures), F32),
        ),
        in_specs=[whole] * 7 + [pl.BlockSpec(memory_space=pltpu.SMEM)],
        out_specs=(whole, whole),
        scratch_shapes=[
            vmem((8, 128), I32),
            vmem((8, 128), I32),
            pltpu.SMEM((8, 128), I32),
            vmem(target_points.shape, F32),
            vmem(source_points.shape, F32),
            vmem((rows, measures), F32),
            vmem((64, 8, tile), F32),
            vmem((8, 3, tile, 128), F32),
            vmem((slots, tile, tile), BF16),
            vmem((slots + 1, measures, tile), F32),
            vmem((ITERS, 2, measures, tile), BF16),
            vmem((ITERS, 8, measures, tile), BF16),
            vmem((CHAINS, 4, 2, 4, mh, tile), F32),
            vmem((CHAINS, 4, 2, 4, mh, tile), F32),
            vmem((CHAINS, 2, 4, 4 * mh + 16, tile), I16),
            vmem((ITERS, CHAINS, 2, 4, 4 * mh + 16, tile), I16),
            vmem((CHAINS, 2, 3, mh + 16, tile), I16),
            vmem((ITERS, CHAINS, 2, 3, mh + 16, tile), I16),
            vmem((CHAINS, 2, 4, mh, tile), F32),
            vmem((ITERS, 64, measures, tile), BF16),
            vmem((CHAINS, 4, block, tile), I16),
            vmem((ITERS, CHAINS, 4, block, tile), I16),
            vmem((rows, measures), F32),
            vmem((2, measures, tile), F32),
            vmem((2, measures, tile), F32),
            vmem((2, measures, tile), F32),
            vmem((2, measures, tile), F32),
            dma((4,)), dma((4,)),
            dma((CHAINS, 4)), dma((ITERS, CHAINS, 4)),
            dma((CHAINS, 4)), dma((ITERS, CHAINS, 4)),
            dma((CHAINS, 2, 4)), dma((ITERS, CHAINS, 2, 4)),
            dma((CHAINS, 2, 3)), dma((ITERS, CHAINS, 2, 3)),
            dma((CHAINS, 2, 3)), dma((ITERS, CHAINS, 2, 3)),
            dma((CHAINS, 2, 6)), dma((ITERS, CHAINS, 2, 6)),
            dma((CHAINS, 2, 4)), dma((ITERS, CHAINS, 2, 4)),
            dma((CHAINS, 4)), dma((ITERS, CHAINS, 4)),
            dma, dma, dma,
        ],
        compiler_params=pltpu.CompilerParams(
            collective_id=0, has_side_effects=True, vmem_limit_bytes=60 * 1024 * 1024
        ),
    )(target_points, source_points, target_mass, source_mass, start_dual,
      tile_row.reshape(1, slots), tile_column.reshape(1, slots), tile_count)


def solution(mesh):
    return jax.shard_map(
        local,
        mesh=mesh,
        in_specs=(
            P(None, "row"),
            P(None, "col"),
            P(("row", "col"), None),
            P(("col", "row"), None),
            P(("col", "row"), None),
            P(("row", "col")),
            P(("row", "col")),
            P(("row", "col")),
        ),
        out_specs=(P(("row", "col"), None), P(("col", "row"), None)),
        check_vma=False,
    )
```

```python
import functools

import jax
import jax.numpy as jnp
from jax import lax
from jax.experimental import pallas as pl
from jax.experimental.pallas import tpu as pltpu
from jax.sharding import PartitionSpec as P

MESH = pl.DeviceIdType.MESH
ITERS = 2
CHAINS = 2
GROUP = 16
SCALE = 2.6857913
FINE = 2896.0
COARSE = 256.0
F32 = jnp.float32
BF16 = jnp.bfloat16
I16 = jnp.int16
I32 = jnp.int32


def encode(x):
    level = jnp.log(jnp.maximum(x, 1e-37))
    ref = (level[0:1] * COARSE + 32768.5).astype(I32) - 32768
    fine = level * FINE + (32768.5 - ref.astype(F32) * (FINE / COARSE))
    return (fine.astype(I32) - 32768).astype(I16), ref


def decode(code, ref):
    return jnp.exp(
        code.astype(I32).astype(F32) * (1.0 / FINE) + ref.astype(F32) * (1.0 / COARSE)
    )


def kernel(
    slots,
    tp, sp, tm, sm, sd, tr, tc, tn,
    td_out, so_out,
    meta_own, meta_in, meta, tp_in, sp_in, tm_in, tt, sb, kt, acc,
    src_own, s_band, x0_send, x0_recv, r1_send, r1_recv, r2_send, r2_recv, part,
    t_band, z_send, z_recv, td_own, t_mass, s_mass, t_all, s_all,
    p_send, p_recv, s_send, s_recv, x_send, x_recv, a_send, a_recv, b_send, b_recv,
    q_send, q_recv, g_send, g_recv, c_send, c_recv, w_send, w_recv, o_send, o_recv, m_sem,
):
    tile = kt.shape[1]
    measures = acc.shape[1]
    mh = measures // CHAINS
    row = lax.axis_index("row")
    col = lax.axis_index("col")
    z_lo, core = row // 2, row % 2
    x, z_hi, y = col // 8, (col // 4) % 2, col % 4
    z = z_hi * 2 + z_lo
    other = 1 - core
    own_role = core == z_hi
    swapped = core != z_hi

    def device(x_, y_, z_, core_):
        return ((z_ % 2) * 2 + core_, x_ * 8 + (z_ // 2) * 4 + y_)

    sibling = device(x, y, z, other)
    partner = device(x, y, core * 2 + z_lo, z_hi)

    ring = {(0, step): device((x + step) % 4, y, z, core) for step in (1, 2, 3)}
    ring.update({(1, step): device(x, (y + step) % 4, z, core) for step in (1, 2, 3)})

    def on_ring(axis, step):
        return ring[axis, step]

    delta = (z + 4 - 2 * core) % 4

    def by_delta(*values):
        return jnp.where(delta < 2, jnp.where(delta == 0, values[0], values[1]),
                         jnp.where(delta == 2, values[2], values[3]))

    relayed, single = by_delta(2, 0, 3, 1), by_delta(3, 1, 2, 0)
    up_band = device(x, y, (z + 1) % 4, z_hi)
    down_band = device(x, y, (z + 3) % 4, z_hi)
    up_core = device(x, y, (z + 1) % 4, core)
    down_core = device(x, y, (z + 3) % 4, core)
    relay_step = by_delta(3, 1, 1, 3)
    relay_on = device(x, y, (z + relay_step) % 4, core)

    def owner(r):
        return device(x, y, core * 2 + r // 2, r % 2)

    def remote(src, dst, send, recv, target):
        return pltpu.make_async_remote_copy(
            src_ref=src, dst_ref=dst, send_sem=send, recv_sem=recv,
            device_id=target, device_id_type=MESH,
        )

    barrier = pltpu.get_barrier_semaphore()
    friends = [device(x, y, (z + dz) % 4, (core + dk) % 2)
               for dz in range(4) for dk in range(2) if dz or dk]
    friends += [on_ring(axis, step) for axis in (0, 1) for step in (1, 2, 3)]
    for friend in friends:
        pl.semaphore_signal(barrier, inc=1, device_id=friend, device_id_type=MESH)

    meta_own[...] = jnp.zeros_like(meta_own)
    meta_own[0:1, 0:slots] = jnp.clip(tr[...], 0, 63)
    meta_own[1:2, 0:slots] = jnp.clip(tc[...], 0, 7)
    lane = lax.broadcasted_iota(I32, (128, 128), 1)
    sub = lax.broadcasted_iota(I32, (128, 128), 0)
    alive = sub < tn[0]
    for k in range(2):
        across = jnp.broadcast_to(meta_own[k:k + 1, :], (128, 128))
        down = across.T
        same = (down == across) & (sub < lane) & alive
        found = jnp.max(jnp.where(same, sub, -1), axis=0, keepdims=True)
        meta_own[2 + k:3 + k, :] = jnp.where(found < 0, slots, found)
        same = (down == lane) & alive
        found = jnp.max(jnp.where(same, sub, -1), axis=0, keepdims=True)
        meta_own[4 + k:5 + k, :] = jnp.where(found < 0, slots, found)
    index = meta_own[0:1, :]
    share = index // 2
    sx, sh, sy = share // 8, (share // 4) % 2, share % 4
    even = ((sh * 2 + 0) * 4 + sx) * 4 + sy
    odd = ((sh * 2 + 1) * 4 + sy) * 4 + sx
    meta_own[6:7, :] = jnp.where(index % 2 == 0, even, odd)

    for k in range(2):
        src_own[0, k] = sd[k * tile:(k + 1) * tile, :].astype(F32).T.astype(BF16)
        s_mass[k] = sm[k * tile:(k + 1) * tile, :].T

    pl.semaphore_wait(barrier, len(friends))

    points_out = remote(tp, tp_in, p_send.at[0], p_recv.at[0], sibling)
    sp_copy = remote(sp, sp_in, p_send.at[1], p_recv.at[1], partner)
    meta_copy = remote(meta_own, meta_in, p_send.at[2], p_recv.at[2], partner)
    tm_copy = remote(tm, tm_in, p_send.at[3], p_recv.at[3], partner)

    @pl.when(own_role)
    def _():
        points_out.start()
        sp_in[...] = sp[...]
        tp_in[...] = tp[...]
        tm_in[...] = tm[...]
        meta_in[...] = meta_own[...]

    @pl.when(swapped)
    def _():
        meta_copy.start()
        sp_copy.start()

    def rows_of(h):
        return slice(h * mh, (h + 1) * mh)

    def source_copy(it, h, step):
        target = (sibling, up_band, None, down_band)[step]
        return remote(
            src_own.at[it, :, rows_of(h)], s_band.at[it, pl.ds(2 * row, 2), rows_of(h)],
            s_send.at[h, step], s_recv.at[it, h, row], target,
        )

    def source_relay(it, h):
        ref = s_band.at[it, pl.ds(2 * relayed, 2), rows_of(h)]
        return remote(ref, ref, s_send.at[h, 2], s_recv.at[it, h, relayed], relay_on)

    def source_send(it, h):
        source_copy(it, h, 1).start()
        source_copy(it, h, 3).start()

        @pl.when(swapped)
        def _():
            source_copy(it, h, 0).start()

        @pl.when(own_role)
        def _():
            s_band[it, pl.ds(2 * row, 2), rows_of(h)] = src_own[it, :, rows_of(h)]

    def source_sent(it, h):
        source_copy(it, h, 1).wait_send()
        source_copy(it, h, 3).wait_send()
        source_relay(it, h).wait_send()

        @pl.when(swapped)
        def _():
            source_copy(it, h, 0).wait_send()

    def source_pass_on(it, h):
        source_relay(it, h).wait_recv()
        source_relay(it, h).start()

    def source_arrived(it, h):
        for r in range(4):
            @pl.when(jnp.logical_and(jnp.logical_or(swapped, row != r), relayed != r))
            def _():
                remote(src_own.at[it, :, rows_of(h)],
                       s_band.at[it, 2 * r:2 * r + 2, rows_of(h)], s_send.at[h, 0],
                       s_recv.at[it, h, r], sibling).wait_recv()

    for h in range(CHAINS):
        source_send(0, h)

    @pl.when(swapped)
    def _():
        meta_copy.wait_recv()
        sp_copy.wait_recv()
        points_out.wait_recv()

    to_scalar = pltpu.make_async_copy(meta_in, meta, m_sem)
    to_scalar.start()

    @pl.loop(0, 8)
    def _(c):
        start = pl.multiple_of(c * tile, tile)
        for k in range(3):
            line = sp_in[k:k + 1, pl.ds(start, tile)] * SCALE
            column = jnp.broadcast_to(line, (8, tile)).T[:, 0:1]
            sb[c, k] = jnp.broadcast_to(column, (tile, 128))

    @pl.loop(0, 64, unroll=8)
    def _(r):
        tt[r, 0:3] = tp_in[:, pl.ds(pl.multiple_of(r * tile, tile), tile)] * SCALE

    to_scalar.wait()

    acc[slots] = jnp.zeros((measures, tile), F32)

    def make_tile(s):
        r, c = meta[0, s], meta[1, s]
        for part_at in range(tile // 128):
            lanes = slice(part_at * 128, (part_at + 1) * 128)
            distance = (sb[c, 0] - tt[r, 0:1, lanes]) ** 2
            distance = distance + (sb[c, 1] - tt[r, 1:2, lanes]) ** 2
            distance = distance + (sb[c, 2] - tt[r, 2:3, lanes]) ** 2
            kt[s, :, lanes] = jnp.exp2(-8.0 - distance).astype(BF16)

    def row_product(it, s):
        acc[s] = acc[meta[2, s]] + jnp.dot(s_band[it, meta[1, s]], kt[s],
                                           preferred_element_type=F32)

    steps = 14
    first_tiles = slots - 2 * steps

    @pl.loop(0, first_tiles // 2)
    def _(pair):
        make_tile(2 * pair)
        make_tile(2 * pair + 1)

    for h in range(CHAINS):
        source_pass_on(0, h)

    @pl.when(swapped)
    def _():
        tm_copy.start()

    for h in range(CHAINS):
        source_arrived(0, h)

    @pl.loop(0, steps)
    def _(step):
        for m in range(3):
            row_product(0, 3 * step + m)
        for m in range(2):
            make_tile(first_tiles + 2 * step + m)

    for s in range(3 * steps, slots):
        row_product(0, s)

    def write_block(ref, values):
        n = len(values)
        line = lax.broadcasted_iota(I32, (16, tile), 0)
        refs = jnp.zeros((16, tile), I32)
        for i in range(n):
            code, ref_row = encode(values[i]())
            ref[i * mh:(i + 1) * mh, :] = code
            refs = jnp.where(line == i, ref_row, refs)
        ref[n * mh:n * mh + 16, :] = refs.astype(I16)

    def read_block(ref, i, n=2):
        refs = ref[n * mh:n * mh + 16, :].astype(I32)
        return decode(ref[i * mh:(i + 1) * mh, :], refs[i:i + 1])

    place = ((x, y), (y, x))
    out_copy = remote(td_own, td_out, o_send, o_recv, partner)

    def total(a, d, u, side):
        g = (place[a][0] + d) % 4
        gx, gy = (g, u) if a == 0 else (u, g)
        return meta[4, 2 * (gx * 8 + side * 4 + gy) + a]

    class Chain:
        def __init__(self, h, it):
            self.h, self.it, self.rows = h, it, rows_of(h)

        def x0_copy(self, d):
            h = self.h
            return remote(x0_send.at[h, d], x0_recv.at[h, d], x_send.at[h, d],
                          x_recv.at[self.it, h, d], sibling)

        def r1_rows(self, kind):
            return slice(0, (4 if kind < 2 else 2) * mh + 16)

        def r1_copy(self, a, kind):
            h, it, rows = self.h, self.it, self.r1_rows(kind)
            return remote(r1_send.at[h, a, kind, rows], r1_recv.at[it, h, a, kind, rows],
                          a_send.at[h, a, kind], a_recv.at[it, h, a, kind],
                          on_ring(a, 1 if kind % 2 == 0 else 3))

        def r2_copy(self, a, kind):
            h, it, step = self.h, self.it, (1, 3, 2)[kind]
            return remote(r2_send.at[h, a, kind], r2_recv.at[it, h, a, kind],
                          b_send.at[h, a, kind], b_recv.at[it, h, a, kind], on_ring(1 - a, step))

        def spot(self, a, g, u, side=None):
            return (((core if side is None else side) * 2 + a) * 4 + g) * 4 + u

        def q_copy(self, a, kind):
            p, q = place[a]
            ref = t_band.at[self.it, self.spot(a, p, q), self.rows]
            return remote(ref, ref, q_send.at[self.h, a, kind],
                          q_recv.at[self.it, self.h, a, kind], on_ring(1 - a, (1, 3, 2)[kind]))

        def q_got(self, a, kind):
            p, q = place[a]
            ref = t_band.at[self.it, self.spot(a, p, (q + (3, 1, 2)[kind]) % 4), self.rows]
            remote(ref, ref, q_send.at[self.h, a, kind],
                   q_recv.at[self.it, self.h, a, kind], sibling).wait_recv()

        def pair(self, a, g, far):
            q = place[a][1]
            begin = 2 * (1 - q // 2) if far else 2 * (q // 2)
            return t_band.at[self.it, pl.ds(self.spot(a, g, begin), 2), self.rows]

        def g_copy(self, a, kind):
            p = place[a][0]
            g = (p, p, p, p, (p + 3) % 4, (p + 1) % 4)[kind]
            ref = self.pair(a, g, kind % 2 == 1)
            return remote(ref, ref, g_send.at[self.h, a, kind], g_recv.at[self.it, self.h, a, kind],
                          on_ring(a, (1, 1, 3, 3, 1, 3)[kind]))

        def g_got(self, a, kind):
            p = place[a][0]
            g = ((p + 3) % 4, (p + 3) % 4, (p + 1) % 4, (p + 1) % 4,
                 (p + 2) % 4, (p + 2) % 4)[kind]
            ref = self.pair(a, g, kind % 2 == 1)
            remote(ref, ref, g_send.at[self.h, a, kind], g_recv.at[self.it, self.h, a, kind],
                   sibling).wait_recv()

        def c_copy(self, a, dg):
            base = self.spot(a, (place[a][0] + dg) % 4, 0)
            ref = t_band.at[self.it, pl.ds(base, 4), self.rows]
            return remote(ref, ref, c_send.at[self.h, a, dg],
                          c_recv.at[self.it, self.h, a, dg], sibling)

        def c_got(self, a, dg):
            base = self.spot(a, (place[a][0] + dg) % 4, 0, other)
            ref = t_band.at[self.it, pl.ds(base, 4), self.rows]
            remote(ref, ref, c_send.at[self.h, a, dg],
                   c_recv.at[self.it, self.h, a, dg], sibling).wait_recv()

        def z_copy(self, kind, r):
            h, it = self.h, self.it
            return remote(z_send.at[h, r], z_recv.at[it, h, kind], w_send.at[h, r],
                          w_recv.at[it, h, kind], owner(r))

        def z_far(self, r, target):
            h, it = self.h, self.it
            return remote(z_send.at[h, r], z_recv.at[it, h, 3], w_send.at[h, r],
                          w_recv.at[it, h, 3], target)

        def to_next(self, r, fn):
            below = (core * 2 + r // 2 + 3) % 4 == z

            @pl.when(below)
            def _():
                fn(self.z_copy(1, r))

            @pl.when(jnp.logical_not(below))
            def _():
                fn(self.z_copy(2, r))

        def own(self, a, d, u):
            return acc[total(a, d, u, core), self.rows] + x0_recv[self.h, d, a, u]

        def stage(self, d):
            for a in range(2):
                @pl.loop(0, 4)
                def _(u):
                    x0_send[self.h, d, a, u] = acc[total(a, d, u, other), self.rows]

            self.x0_copy(d).start()

        def ring_first(self):
            self.x0_copy(2).wait_recv()
            for kind, d, far, near in ((0, 1, 0, 2), (1, 3, 2, 0)):
                self.x0_copy(d).wait_recv()
                for a in range(2):
                    write_block(r1_send.at[self.h, a, kind],
                                [functools.partial(self.own, a, 2, far + i) for i in range(2)]
                                + [functools.partial(self.own, a, d, near + i) for i in range(2)])
                    self.r1_copy(a, kind).start()

        def ring_relay(self):
            h, it = self.h, self.it
            for a in range(2):
                for kind, d, u0 in ((2, 1, 0), (3, 3, 2)):
                    self.r1_copy(a, kind - 2).wait_recv()
                    got = r1_recv.at[it, h, a, kind - 2]
                    write_block(r1_send.at[h, a, kind],
                                [lambda i=i: self.own(a, d, u0 + i) + read_block(got, i, 4)
                                 for i in range(2)])
                    self.r1_copy(a, kind).start()

        def ring_sum(self):
            h, it = self.h, self.it
            self.x0_copy(0).wait_recv()
            for a in range(2):
                for i in range(2):
                    part[h, a, i] = self.own(a, 0, i) + read_block(
                        r1_recv.at[it, h, a, 1], 2 + i, 4)
                    part[h, a, 2 + i] = self.own(a, 0, 2 + i) + read_block(
                        r1_recv.at[it, h, a, 0], 2 + i, 4)

        def ring_total(self):
            h, it = self.h, self.it
            for a in range(2):
                q = place[a][1]
                self.r1_copy(a, 2).wait_recv()
                self.r1_copy(a, 3).wait_recv()
                for i in range(2):
                    part[h, a, i] += read_block(r1_recv.at[it, h, a, 2], i)
                    part[h, a, 2 + i] += read_block(r1_recv.at[it, h, a, 3], i)
                for kind in (2, 0, 1):
                    write_block(r2_send.at[h, a, kind],
                                [lambda: part[h, a, (q + (1, 3, 2)[kind]) % 4]])
                    self.r2_copy(a, kind).start()

        def target(self):
            h, it = self.h, self.it
            for a in range(2):
                p, q = place[a]
                for kind in range(3):
                    self.r2_copy(a, kind).wait_recv()
                sums = part[h, a, q]
                for kind in range(3):
                    sums = sums + read_block(r2_recv.at[it, h, a, kind], 0, 1)
                dual = t_mass[a, self.rows] / sums
                t_band[it, self.spot(a, p, q), self.rows] = dual.astype(BF16)
                for kind in (2, 0, 1):
                    self.q_copy(a, kind).start()
                t_all[a, self.rows] = dual

        def gather_near(self):
            for a in range(2):
                self.q_got(a, 0)
                self.q_got(a, 1)
                self.g_copy(a, 0).start()
                self.g_copy(a, 2).start()

        def gather_block(self):
            for a in range(2):
                self.q_got(a, 2)
                self.g_copy(a, 3).start()
                self.g_copy(a, 1).start()
                self.g_got(a, 0)
                self.g_copy(a, 4).start()
            for a in range(2):
                self.c_copy(a, 0).start()

        def gather_relay(self):
            for a in range(2):
                self.g_got(a, 3)
                self.g_copy(a, 5).start()
            for a in range(2):
                self.g_got(a, 1)
                self.c_copy(a, 3).start()
                self.g_got(a, 2)
                self.c_copy(a, 1).start()

        def gather_last(self):
            for a in range(2):
                self.g_got(a, 4)
                self.g_got(a, 5)
                self.c_copy(a, 2).start()

        def gathered(self):
            for dg in (0, 3, 1, 2):
                for a in range(2):
                    self.c_got(a, dg)

        def to_owner(self):
            h, it = self.h, self.it
            first = 2 * (delta % 2)
            for at in range(2):
                r = first + at
                write_block(z_send.at[h, r],
                            [lambda i=i: acc[meta[5, 2 * r + i], self.rows] for i in range(2)])

                @pl.when(swapped)
                def _():
                    self.z_far(r, device(
                        x, y, (z + jnp.where((delta == 2) == (at == 0), 3, 1)) % 4, core)).start()

                @pl.when(jnp.logical_and(own_role, core != at))
                def _():
                    self.z_copy(0, r).start()

                @pl.when(jnp.logical_and(own_role, core == at))
                def _():
                    z_recv[it, h, 0] = z_send[h, r]

            write_block(z_send.at[h, single],
                        [lambda i=i: acc[meta[5, 2 * single + i], self.rows] for i in range(2)])
            self.to_next(single, lambda copy: copy.start())

        def to_owner_relay(self):
            h, it = self.h, self.it
            self.z_far(0, sibling).wait_recv()
            got = z_recv.at[it, h, 3]
            write_block(z_send.at[h, relayed],
                        [lambda i=i: acc[meta[5, 2 * relayed + i], self.rows]
                         + read_block(got, i) for i in range(2)])
            self.to_next(relayed, lambda copy: copy.start())

        def source(self):
            h, it = self.h, self.it
            for kind in range(3):
                @pl.when(jnp.logical_or(swapped, kind != 0))
                def _():
                    self.z_copy(kind, 0).wait_recv()

            for k in range(2):
                sums = read_block(z_recv.at[it, h, 0], k)
                for kind in (1, 2):
                    sums = sums + read_block(z_recv.at[it, h, kind], k)
                dual = s_mass[k, self.rows] / sums
                s_all[k, self.rows] = dual

                @pl.when(it < ITERS - 1)
                def _():
                    src_own[1, k, self.rows] = dual.astype(BF16)

            source_sent(it, h)

            @pl.when(it < ITERS - 1)
            def _():
                source_send(1, h)

        def sent(self):
            h = self.h
            for d in range(4):
                self.x0_copy(d).wait_send()
            for a in range(2):
                for kind in range(4):
                    self.r1_copy(a, kind).wait_send()
                for kind in range(6):
                    self.g_copy(a, kind).wait_send()
                for kind in range(3):
                    self.r2_copy(a, kind).wait_send()
                    self.q_copy(a, kind).wait_send()
                for kind in range(4):
                    self.c_copy(a, kind).wait_send()
            first = 2 * (delta % 2)
            for at in range(2):
                @pl.when(jnp.logical_or(swapped, core != at))
                def _():
                    self.z_far(first + at, sibling).wait_send()
            for r in (single, relayed):
                self.z_copy(1, r).wait_send()

    def iteration(it, _):
        chains = [Chain(h, it) for h in range(CHAINS)]

        @pl.when(it > 0)
        def _():
            for h in range(CHAINS):
                source_arrived(1, h)

            @pl.loop(0, slots // GROUP)
            def _(group):
                for m in range(GROUP):
                    row_product(1, group * GROUP + m)

        for chain in chains:
            for d in (2, 1, 3):
                chain.stage(d)
        for name in ("ring_first", "ring_relay", "ring_sum", "ring_total",
                     "target", "gather_near", "gather_block", "gather_relay",
                     "gather_last"):
            for chain in chains:
                getattr(chain, name)()
            if name == "gather_block":
                @pl.when(it == ITERS - 1)
                def _():
                    for a in range(2):
                        td_own[a * tile:(a + 1) * tile, :] = t_all[a].T

                    @pl.when(swapped)
                    def _():
                        out_copy.start()

                    @pl.when(own_role)
                    def _():
                        td_out[...] = td_own[...]

            if name == "ring_first":
                for chain in chains:
                    chain.stage(0)

                @pl.when(it == 0)
                def _():
                    @pl.when(swapped)
                    def _():
                        tm_copy.wait_recv()

                    for k in range(2):
                        t_mass[k] = tm_in[k * tile:(k + 1) * tile, :].T

        for chain in chains:
            chain.gathered()

        @pl.loop(0, slots // GROUP)
        def _(group):
            for m in range(GROUP):
                s = group * GROUP + m
                acc[s] = acc[meta[3, s]] + lax.dot_general(
                    t_band[it, meta[6, s]], kt[s], (((1,), (1,)), ((), ())),
                    preferred_element_type=F32)

        for name in ("to_owner", "to_owner_relay", "source"):
            for chain in chains:
                getattr(chain, name)()

        @pl.when(it < ITERS - 1)
        def _():
            for h in range(CHAINS):
                source_pass_on(1, h)

        for chain in chains:
            chain.sent()
        return 0

    lax.fori_loop(0, ITERS, iteration, 0)
    for k in range(2):
        so_out[k * tile:(k + 1) * tile, :] = s_all[k].T

    @pl.when(own_role)
    def _():
        points_out.wait_send()

    @pl.when(swapped)
    def _():
        out_copy.wait()
        meta_copy.wait_send()
        sp_copy.wait_send()
        tm_copy.wait_send()


def local(target_points, source_points, target_mass, source_mass, start_dual,
          tile_row, tile_column, tile_count):
    slots = tile_row.shape[0]
    rows, measures = target_mass.shape
    tile = rows // 2
    mh = measures // CHAINS
    dma = pltpu.SemaphoreType.DMA
    vmem = pltpu.VMEM
    whole = pl.BlockSpec(memory_space=pltpu.VMEM)
    block = 2 * mh + 16
    return pl.pallas_call(
        functools.partial(kernel, slots),
        out_shape=(
            jax.ShapeDtypeStruct((rows, measures), F32),
            jax.ShapeDtypeStruct((rows, measures), F32),
        ),
        in_specs=[whole] * 7 + [pl.BlockSpec(memory_space=pltpu.SMEM)],
        out_specs=(whole, whole),
        scratch_shapes=[
            vmem((8, 128), I32),
            vmem((8, 128), I32),
            pltpu.SMEM((8, 128), I32),
            vmem(target_points.shape, F32),
            vmem(source_points.shape, F32),
            vmem((rows, measures), F32),
            vmem((64, 8, tile), F32),
            vmem((8, 3, tile, 128), F32),
            vmem((slots, tile, tile), BF16),
            vmem((slots + 1, measures, tile), F32),
            vmem((ITERS, 2, measures, tile), BF16),
            vmem((ITERS, 8, measures, tile), BF16),
            vmem((CHAINS, 4, 2, 4, mh, tile), F32),
            vmem((CHAINS, 4, 2, 4, mh, tile), F32),
            vmem((CHAINS, 2, 4, 4 * mh + 16, tile), I16),
            vmem((ITERS, CHAINS, 2, 4, 4 * mh + 16, tile), I16),
            vmem((CHAINS, 2, 3, mh + 16, tile), I16),
            vmem((ITERS, CHAINS, 2, 3, mh + 16, tile), I16),
            vmem((CHAINS, 2, 4, mh, tile), F32),
            vmem((ITERS, 64, measures, tile), BF16),
            vmem((CHAINS, 4, block, tile), I16),
            vmem((ITERS, CHAINS, 4, block, tile), I16),
            vmem((rows, measures), F32),
            vmem((2, measures, tile), F32),
            vmem((2, measures, tile), F32),
            vmem((2, measures, tile), F32),
            vmem((2, measures, tile), F32),
            dma((4,)), dma((4,)),
            dma((CHAINS, 4)), dma((ITERS, CHAINS, 4)),
            dma((CHAINS, 4)), dma((ITERS, CHAINS, 4)),
            dma((CHAINS, 2, 4)), dma((ITERS, CHAINS, 2, 4)),
            dma((CHAINS, 2, 3)), dma((ITERS, CHAINS, 2, 3)),
            dma((CHAINS, 2, 3)), dma((ITERS, CHAINS, 2, 3)),
            dma((CHAINS, 2, 6)), dma((ITERS, CHAINS, 2, 6)),
            dma((CHAINS, 2, 4)), dma((ITERS, CHAINS, 2, 4)),
            dma((CHAINS, 4)), dma((ITERS, CHAINS, 4)),
            dma, dma, dma,
        ],
        compiler_params=pltpu.CompilerParams(
            collective_id=0, has_side_effects=True, vmem_limit_bytes=60 * 1024 * 1024
        ),
    )(target_points, source_points, target_mass, source_mass, start_dual,
      tile_row.reshape(1, slots), tile_column.reshape(1, slots), tile_count)


def solution(mesh):
    return jax.shard_map(
        local,
        mesh=mesh,
        in_specs=(
            P(None, "row"),
            P(None, "col"),
            P(("row", "col"), None),
            P(("col", "row"), None),
            P(("col", "row"), None),
            P(("row", "col")),
            P(("row", "col")),
            P(("row", "col")),
        ),
        out_specs=(P(("row", "col"), None), P(("col", "row"), None)),
        check_vma=False,
    )
```

```python
import functools

import jax
import jax.numpy as jnp
from jax import lax
from jax.experimental import pallas as pl
from jax.experimental.pallas import tpu as pltpu
from jax.sharding import PartitionSpec as P

MESH = pl.DeviceIdType.MESH
ITERS = 2
CHAINS = 2
GROUP = 16
SCALE = 2.6857913
FINE = 2896.0
COARSE = 256.0
F32 = jnp.float32
BF16 = jnp.bfloat16
I16 = jnp.int16
I32 = jnp.int32


def encode(x):
    level = jnp.log(jnp.maximum(x, 1e-37))
    ref = (level[0:1] * COARSE + 32768.5).astype(I32) - 32768
    fine = level * FINE + (32768.5 - ref.astype(F32) * (FINE / COARSE))
    return (fine.astype(I32) - 32768).astype(I16), ref


def decode(code, ref):
    return jnp.exp(
        code.astype(I32).astype(F32) * (1.0 / FINE) + ref.astype(F32) * (1.0 / COARSE)
    )


def kernel(
    slots,
    tp, sp, tm, sm, sd, tr, tc, tn,
    td_out, so_out,
    meta_own, meta_in, meta, tp_in, sp_in, tm_in, tt, sb, kt, acc,
    src_own, s_band, x0_send, x0_recv, r1_send, r1_recv, r2_send, r2_recv, part,
    t_band, z_send, z_recv, td_own, t_mass, s_mass, t_all, s_all,
    p_send, p_recv, s_send, s_recv, x_send, x_recv, a_send, a_recv, b_send, b_recv,
    q_send, q_recv, g_send, g_recv, c_send, c_recv, w_send, w_recv, o_send, o_recv, m_sem,
):
    tile = kt.shape[1]
    measures = acc.shape[1]
    mh = measures // CHAINS
    row = lax.axis_index("row")
    col = lax.axis_index("col")
    z_lo, core = row // 2, row % 2
    x, z_hi, y = col // 8, (col // 4) % 2, col % 4
    z = z_hi * 2 + z_lo
    other = 1 - core
    own_role = core == z_hi
    swapped = core != z_hi

    def device(x_, y_, z_, core_):
        return ((z_ % 2) * 2 + core_, x_ * 8 + (z_ // 2) * 4 + y_)

    sibling = device(x, y, z, other)
    partner = device(x, y, core * 2 + z_lo, z_hi)

    ring = {(0, step): device((x + step) % 4, y, z, core) for step in (1, 2, 3)}
    ring.update({(1, step): device(x, (y + step) % 4, z, core) for step in (1, 2, 3)})

    def on_ring(axis, step):
        return ring[axis, step]

    delta = (z + 4 - 2 * core) % 4

    def by_delta(*values):
        return jnp.where(delta < 2, jnp.where(delta == 0, values[0], values[1]),
                         jnp.where(delta == 2, values[2], values[3]))

    relayed, single = by_delta(2, 0, 3, 1), by_delta(3, 1, 2, 0)
    up_band = device(x, y, (z + 1) % 4, z_hi)
    down_band = device(x, y, (z + 3) % 4, z_hi)
    up_core = device(x, y, (z + 1) % 4, core)
    down_core = device(x, y, (z + 3) % 4, core)
    relay_step = by_delta(3, 1, 1, 3)
    relay_on = device(x, y, (z + relay_step) % 4, core)

    def owner(r):
        return device(x, y, core * 2 + r // 2, r % 2)

    def remote(src, dst, send, recv, target):
        return pltpu.make_async_remote_copy(
            src_ref=src, dst_ref=dst, send_sem=send, recv_sem=recv,
            device_id=target, device_id_type=MESH,
        )

    barrier = pltpu.get_barrier_semaphore()
    friends = [device(x, y, (z + dz) % 4, (core + dk) % 2)
               for dz in range(4) for dk in range(2) if dz or dk]
    friends += [on_ring(axis, step) for axis in (0, 1) for step in (1, 2, 3)]
    for friend in friends:
        pl.semaphore_signal(barrier, inc=1, device_id=friend, device_id_type=MESH)

    meta_own[...] = jnp.zeros_like(meta_own)
    meta_own[0:1, 0:slots] = jnp.clip(tr[...], 0, 63)
    meta_own[1:2, 0:slots] = jnp.clip(tc[...], 0, 7)
    lane = lax.broadcasted_iota(I32, (128, 128), 1)
    sub = lax.broadcasted_iota(I32, (128, 128), 0)
    alive = sub < tn[0]
    for k in range(2):
        across = jnp.broadcast_to(meta_own[k:k + 1, :], (128, 128))
        down = across.T
        same = (down == across) & (sub < lane) & alive
        found = jnp.max(jnp.where(same, sub, -1), axis=0, keepdims=True)
        meta_own[2 + k:3 + k, :] = jnp.where(found < 0, slots, found)
        same = (down == lane) & alive
        found = jnp.max(jnp.where(same, sub, -1), axis=0, keepdims=True)
        meta_own[4 + k:5 + k, :] = jnp.where(found < 0, slots, found)
    index = meta_own[0:1, :]
    share = index // 2
    sx, sh, sy = share // 8, (share // 4) % 2, share % 4
    even = ((sh * 2 + 0) * 4 + sx) * 4 + sy
    odd = ((sh * 2 + 1) * 4 + sy) * 4 + sx
    meta_own[6:7, :] = jnp.where(index % 2 == 0, even, odd)

    for k in range(2):
        src_own[0, k] = sd[k * tile:(k + 1) * tile, :].astype(F32).T.astype(BF16)
        s_mass[k] = sm[k * tile:(k + 1) * tile, :].T

    pl.semaphore_wait(barrier, len(friends))

    points_out = remote(tp, tp_in, p_send.at[0], p_recv.at[0], sibling)
    sp_copy = remote(sp, sp_in, p_send.at[1], p_recv.at[1], partner)
    meta_copy = remote(meta_own, meta_in, p_send.at[2], p_recv.at[2], partner)
    tm_copy = remote(tm, tm_in, p_send.at[3], p_recv.at[3], partner)

    @pl.when(own_role)
    def _():
        points_out.start()
        sp_in[...] = sp[...]
        tp_in[...] = tp[...]
        tm_in[...] = tm[...]
        meta_in[...] = meta_own[...]

    @pl.when(swapped)
    def _():
        meta_copy.start()
        sp_copy.start()

    def rows_of(h):
        return slice(h * mh, (h + 1) * mh)

    def source_copy(it, h, step):
        target = (sibling, up_band, None, down_band)[step]
        return remote(
            src_own.at[it, :, rows_of(h)], s_band[h].at[it, pl.ds(2 * row, 2)],
            s_send.at[h, step], s_recv.at[it, h, row], target,
        )

    def source_relay(it, h):
        ref = s_band[h].at[it, pl.ds(2 * relayed, 2)]
        return remote(ref, ref, s_send.at[h, 2], s_recv.at[it, h, relayed], relay_on)

    def source_send(it, h):
        source_copy(it, h, 1).start()
        source_copy(it, h, 3).start()

        @pl.when(swapped)
        def _():
            source_copy(it, h, 0).start()

        @pl.when(own_role)
        def _():
            s_band[h][it, pl.ds(2 * row, 2)] = src_own[it, :, rows_of(h)]

    def source_sent(it, h):
        source_copy(it, h, 1).wait_send()
        source_copy(it, h, 3).wait_send()
        source_relay(it, h).wait_send()

        @pl.when(swapped)
        def _():
            source_copy(it, h, 0).wait_send()

    def source_pass_on(it, h):
        source_relay(it, h).wait_recv()
        source_relay(it, h).start()

    def source_arrived(it, h):
        for r in range(4):
            @pl.when(jnp.logical_and(jnp.logical_or(swapped, row != r), relayed != r))
            def _():
                remote(src_own.at[it, :, rows_of(h)],
                       s_band[h].at[it, 2 * r:2 * r + 2], s_send.at[h, 0],
                       s_recv.at[it, h, r], sibling).wait_recv()

    for h in range(CHAINS):
        source_send(0, h)

    @pl.when(swapped)
    def _():
        meta_copy.wait_recv()
        sp_copy.wait_recv()
        points_out.wait_recv()

    to_scalar = pltpu.make_async_copy(meta_in, meta, m_sem)
    to_scalar.start()

    @pl.loop(0, 8)
    def _(c):
        start = pl.multiple_of(c * tile, tile)
        for k in range(3):
            line = sp_in[k:k + 1, pl.ds(start, tile)] * SCALE
            column = jnp.broadcast_to(line, (8, tile)).T[:, 0:1]
            sb[c, k] = jnp.broadcast_to(column, (tile, 128))

    @pl.loop(0, 64, unroll=8)
    def _(r):
        tt[r, 0:3] = tp_in[:, pl.ds(pl.multiple_of(r * tile, tile), tile)] * SCALE

    to_scalar.wait()

    acc[slots] = jnp.zeros((measures, tile), F32)

    def make_tile(s):
        r, c = meta[0, s], meta[1, s]
        for part_at in range(tile // 128):
            lanes = slice(part_at * 128, (part_at + 1) * 128)
            distance = (sb[c, 0] - tt[r, 0:1, lanes]) ** 2
            distance = distance + (sb[c, 1] - tt[r, 1:2, lanes]) ** 2
            distance = distance + (sb[c, 2] - tt[r, 2:3, lanes]) ** 2
            kt[s, :, lanes] = jnp.exp2(-8.0 - distance).astype(BF16)

    def row_product(it, h, s):
        rows = rows_of(h)
        acc[s, rows] = acc[meta[2, s], rows] + jnp.dot(
            s_band[h][it, meta[1, s]], kt[s], preferred_element_type=F32)

    def column_product(it, h, s):
        rows = rows_of(h)
        acc[s, rows] = acc[meta[3, s], rows] + lax.dot_general(
            t_band[h][it, meta[6, s]], kt[s], (((1,), (1,)), ((), ())),
            preferred_element_type=F32)

    def products(one, it, h):
        @pl.loop(0, slots // GROUP)
        def _(group):
            for m in range(GROUP):
                one(it, h, group * GROUP + m)

    steps = 14
    first_tiles = slots - 2 * steps

    @pl.loop(0, first_tiles // 2)
    def _(pair):
        make_tile(2 * pair)
        make_tile(2 * pair + 1)

    for h in range(CHAINS):
        source_pass_on(0, h)

    @pl.when(swapped)
    def _():
        tm_copy.start()

    for h in range(CHAINS):
        source_arrived(0, h)

    @pl.loop(0, steps)
    def _(step):
        for m in range(3):
            for h in range(CHAINS):
                row_product(0, h, 3 * step + m)
        for m in range(2):
            make_tile(first_tiles + 2 * step + m)

    for s in range(3 * steps, slots):
        for h in range(CHAINS):
            row_product(0, h, s)

    def write_block(ref, values):
        n = len(values)
        line = lax.broadcasted_iota(I32, (16, tile), 0)
        refs = jnp.zeros((16, tile), I32)
        for i in range(n):
            code, ref_row = encode(values[i]())
            ref[i * mh:(i + 1) * mh, :] = code
            refs = jnp.where(line == i, ref_row, refs)
        ref[n * mh:n * mh + 16, :] = refs.astype(I16)

    def read_block(ref, i, n=2):
        refs = ref[n * mh:n * mh + 16, :].astype(I32)
        return decode(ref[i * mh:(i + 1) * mh, :], refs[i:i + 1])

    place = ((x, y), (y, x))
    out_copy = remote(td_own, td_out, o_send, o_recv, partner)

    def total(a, d, u, side):
        g = (place[a][0] + d) % 4
        gx, gy = (g, u) if a == 0 else (u, g)
        return meta[4, 2 * (gx * 8 + side * 4 + gy) + a]

    class Chain:
        def __init__(self, h, it):
            self.h, self.it, self.rows = h, it, rows_of(h)

        def x0_copy(self, d):
            h = self.h
            return remote(x0_send.at[h, d], x0_recv.at[h, d], x_send.at[h, d],
                          x_recv.at[self.it, h, d], sibling)

        def r1_rows(self, kind):
            return slice(0, (4 if kind < 2 else 2) * mh + 16)

        def r1_copy(self, a, kind):
            h, it, rows = self.h, self.it, self.r1_rows(kind)
            return remote(r1_send.at[h, a, kind, rows], r1_recv.at[it, h, a, kind, rows],
                          a_send.at[h, a, kind], a_recv.at[it, h, a, kind],
                          on_ring(a, 1 if kind % 2 == 0 else 3))

        def r2_copy(self, a, kind):
            h, it, step = self.h, self.it, (1, 3, 2)[kind]
            return remote(r2_send.at[h, a, kind], r2_recv.at[it, h, a, kind],
                          b_send.at[h, a, kind], b_recv.at[it, h, a, kind], on_ring(1 - a, step))

        def spot(self, a, g, u, side=None):
            return (((core if side is None else side) * 2 + a) * 4 + g) * 4 + u

        def q_copy(self, a, kind):
            p, q = place[a]
            ref = t_band[self.h].at[self.it, self.spot(a, p, q)]
            return remote(ref, ref, q_send.at[self.h, a, kind],
                          q_recv.at[self.it, self.h, a, kind], on_ring(1 - a, (1, 3, 2)[kind]))

        def q_got(self, a, kind):
            p, q = place[a]
            ref = t_band[self.h].at[self.it, self.spot(a, p, (q + (3, 1, 2)[kind]) % 4)]
            remote(ref, ref, q_send.at[self.h, a, kind],
                   q_recv.at[self.it, self.h, a, kind], sibling).wait_recv()

        def pair(self, a, g, far):
            q = place[a][1]
            begin = 2 * (1 - q // 2) if far else 2 * (q // 2)
            return t_band[self.h].at[self.it, pl.ds(self.spot(a, g, begin), 2)]

        def g_copy(self, a, kind):
            p = place[a][0]
            g = (p, p, p, p, (p + 3) % 4, (p + 1) % 4)[kind]
            ref = self.pair(a, g, kind % 2 == 1)
            return remote(ref, ref, g_send.at[self.h, a, kind], g_recv.at[self.it, self.h, a, kind],
                          on_ring(a, (1, 1, 3, 3, 1, 3)[kind]))

        def g_got(self, a, kind):
            p = place[a][0]
            g = ((p + 3) % 4, (p + 3) % 4, (p + 1) % 4, (p + 1) % 4,
                 (p + 2) % 4, (p + 2) % 4)[kind]
            ref = self.pair(a, g, kind % 2 == 1)
            remote(ref, ref, g_send.at[self.h, a, kind], g_recv.at[self.it, self.h, a, kind],
                   sibling).wait_recv()

        def c_copy(self, a, dg):
            base = self.spot(a, (place[a][0] + dg) % 4, 0)
            ref = t_band[self.h].at[self.it, pl.ds(base, 4)]
            return remote(ref, ref, c_send.at[self.h, a, dg],
                          c_recv.at[self.it, self.h, a, dg], sibling)

        def c_got(self, a, dg):
            base = self.spot(a, (place[a][0] + dg) % 4, 0, other)
            ref = t_band[self.h].at[self.it, pl.ds(base, 4)]
            remote(ref, ref, c_send.at[self.h, a, dg],
                   c_recv.at[self.it, self.h, a, dg], sibling).wait_recv()

        def z_copy(self, kind, r):
            h, it = self.h, self.it
            return remote(z_send.at[h, r], z_recv.at[it, h, kind], w_send.at[h, r],
                          w_recv.at[it, h, kind], owner(r))

        def z_far(self, r, target):
            h, it = self.h, self.it
            return remote(z_send.at[h, r], z_recv.at[it, h, 3], w_send.at[h, r],
                          w_recv.at[it, h, 3], target)

        def to_next(self, r, fn):
            below = (core * 2 + r // 2 + 3) % 4 == z

            @pl.when(below)
            def _():
                fn(self.z_copy(1, r))

            @pl.when(jnp.logical_not(below))
            def _():
                fn(self.z_copy(2, r))

        def own(self, a, d, u):
            return acc[total(a, d, u, core), self.rows] + x0_recv[self.h, d, a, u]

        def stage(self, d):
            for a in range(2):
                @pl.loop(0, 4)
                def _(u):
                    x0_send[self.h, d, a, u] = acc[total(a, d, u, other), self.rows]

            self.x0_copy(d).start()

        def ring_first(self):
            self.x0_copy(2).wait_recv()
            for kind, d, far, near in ((0, 1, 0, 2), (1, 3, 2, 0)):
                self.x0_copy(d).wait_recv()
                for a in range(2):
                    write_block(r1_send.at[self.h, a, kind],
                                [functools.partial(self.own, a, 2, far + i) for i in range(2)]
                                + [functools.partial(self.own, a, d, near + i) for i in range(2)])
                    self.r1_copy(a, kind).start()

        def ring_relay(self):
            h, it = self.h, self.it
            for a in range(2):
                for kind, d, u0 in ((2, 1, 0), (3, 3, 2)):
                    self.r1_copy(a, kind - 2).wait_recv()
                    got = r1_recv.at[it, h, a, kind - 2]
                    write_block(r1_send.at[h, a, kind],
                                [lambda i=i: self.own(a, d, u0 + i) + read_block(got, i, 4)
                                 for i in range(2)])
                    self.r1_copy(a, kind).start()

        def ring_sum(self):
            h, it = self.h, self.it
            self.x0_copy(0).wait_recv()
            for a in range(2):
                for i in range(2):
                    part[h, a, i] = self.own(a, 0, i) + read_block(
                        r1_recv.at[it, h, a, 1], 2 + i, 4)
                    part[h, a, 2 + i] = self.own(a, 0, 2 + i) + read_block(
                        r1_recv.at[it, h, a, 0], 2 + i, 4)

        def ring_total(self):
            h, it = self.h, self.it
            for a in range(2):
                q = place[a][1]
                self.r1_copy(a, 2).wait_recv()
                self.r1_copy(a, 3).wait_recv()
                for i in range(2):
                    part[h, a, i] += read_block(r1_recv.at[it, h, a, 2], i)
                    part[h, a, 2 + i] += read_block(r1_recv.at[it, h, a, 3], i)
                for kind in (2, 0, 1):
                    write_block(r2_send.at[h, a, kind],
                                [lambda: part[h, a, (q + (1, 3, 2)[kind]) % 4]])
                    self.r2_copy(a, kind).start()

        def target(self):
            h, it = self.h, self.it
            for a in range(2):
                p, q = place[a]
                for kind in range(3):
                    self.r2_copy(a, kind).wait_recv()
                sums = part[h, a, q]
                for kind in range(3):
                    sums = sums + read_block(r2_recv.at[it, h, a, kind], 0, 1)
                dual = t_mass[a, self.rows] / sums
                t_band[h][it, self.spot(a, p, q)] = dual.astype(BF16)
                for kind in (2, 0, 1):
                    self.q_copy(a, kind).start()
                t_all[a, self.rows] = dual

        def gather_near(self):
            for a in range(2):
                self.q_got(a, 0)
                self.q_got(a, 1)
                self.g_copy(a, 0).start()
                self.g_copy(a, 2).start()

        def gather_block(self):
            for a in range(2):
                self.q_got(a, 2)
                self.g_copy(a, 3).start()
                self.g_copy(a, 1).start()
                self.g_got(a, 0)
                self.g_copy(a, 4).start()
            for a in range(2):
                self.c_copy(a, 0).start()

        def gather_relay(self):
            for a in range(2):
                self.g_got(a, 3)
                self.g_copy(a, 5).start()
            for a in range(2):
                self.g_got(a, 1)
                self.c_copy(a, 3).start()
                self.g_got(a, 2)
                self.c_copy(a, 1).start()

        def gather_last(self):
            for a in range(2):
                self.g_got(a, 4)
                self.g_got(a, 5)
                self.c_copy(a, 2).start()

        def gathered(self):
            for dg in (0, 3, 1, 2):
                for a in range(2):
                    self.c_got(a, dg)

        def to_owner(self):
            h, it = self.h, self.it
            first = 2 * (delta % 2)
            for at in range(2):
                r = first + at
                write_block(z_send.at[h, r],
                            [lambda i=i: acc[meta[5, 2 * r + i], self.rows] for i in range(2)])

                @pl.when(swapped)
                def _():
                    self.z_far(r, device(
                        x, y, (z + jnp.where((delta == 2) == (at == 0), 3, 1)) % 4, core)).start()

                @pl.when(jnp.logical_and(own_role, core != at))
                def _():
                    self.z_copy(0, r).start()

                @pl.when(jnp.logical_and(own_role, core == at))
                def _():
                    z_recv[it, h, 0] = z_send[h, r]

            write_block(z_send.at[h, single],
                        [lambda i=i: acc[meta[5, 2 * single + i], self.rows] for i in range(2)])
            self.to_next(single, lambda copy: copy.start())

        def to_owner_relay(self):
            h, it = self.h, self.it
            self.z_far(0, sibling).wait_recv()
            got = z_recv.at[it, h, 3]
            write_block(z_send.at[h, relayed],
                        [lambda i=i: acc[meta[5, 2 * relayed + i], self.rows]
                         + read_block(got, i) for i in range(2)])
            self.to_next(relayed, lambda copy: copy.start())

        def source(self):
            h, it = self.h, self.it
            for kind in range(3):
                @pl.when(jnp.logical_or(swapped, kind != 0))
                def _():
                    self.z_copy(kind, 0).wait_recv()

            for k in range(2):
                sums = read_block(z_recv.at[it, h, 0], k)
                for kind in (1, 2):
                    sums = sums + read_block(z_recv.at[it, h, kind], k)
                dual = s_mass[k, self.rows] / sums
                s_all[k, self.rows] = dual

                @pl.when(it < ITERS - 1)
                def _():
                    src_own[1, k, self.rows] = dual.astype(BF16)

            source_sent(it, h)

            @pl.when(it < ITERS - 1)
            def _():
                source_send(1, h)

        def sent(self):
            h = self.h
            for d in range(4):
                self.x0_copy(d).wait_send()
            for a in range(2):
                for kind in range(4):
                    self.r1_copy(a, kind).wait_send()
                for kind in range(6):
                    self.g_copy(a, kind).wait_send()
                for kind in range(3):
                    self.r2_copy(a, kind).wait_send()
                    self.q_copy(a, kind).wait_send()
                for kind in range(4):
                    self.c_copy(a, kind).wait_send()
            first = 2 * (delta % 2)
            for at in range(2):
                @pl.when(jnp.logical_or(swapped, core != at))
                def _():
                    self.z_far(first + at, sibling).wait_send()
            for r in (single, relayed):
                self.z_copy(1, r).wait_send()

    def iteration(it, _):
        first, second = chains = [Chain(h, it) for h in range(CHAINS)]

        def both(*names):
            for name in names:
                for chain in chains:
                    getattr(chain, name)()

        for d in (2, 1, 3):
            first.stage(d)
        first.ring_first()

        @pl.when(it > 0)
        def _():
            source_arrived(1, 1)
            products(row_product, 1, 1)

        for d in (2, 1, 3):
            second.stage(d)
        second.ring_first()
        first.stage(0)
        second.stage(0)

        @pl.when(it == 0)
        def _():
            @pl.when(swapped)
            def _():
                tm_copy.wait_recv()

            for k in range(2):
                t_mass[k] = tm_in[k * tile:(k + 1) * tile, :].T

        both("ring_relay", "ring_sum", "ring_total", "target", "gather_near", "gather_block")

        @pl.when(it == ITERS - 1)
        def _():
            for a in range(2):
                td_own[a * tile:(a + 1) * tile, :] = t_all[a].T

            @pl.when(swapped)
            def _():
                out_copy.start()

            @pl.when(own_role)
            def _():
                td_out[...] = td_own[...]

        both("gather_relay")
        first.gather_last()
        first.gathered()
        products(column_product, it, 0)
        first.to_owner()
        second.gather_last()
        second.gathered()
        products(column_product, it, 1)
        first.to_owner_relay()
        second.to_owner()
        first.source()
        second.to_owner_relay()

        @pl.when(it < ITERS - 1)
        def _():
            source_pass_on(1, 0)

        second.source()

        @pl.when(it < ITERS - 1)
        def _():
            source_arrived(1, 0)
            products(row_product, 1, 0)
            source_pass_on(1, 1)

        for chain in chains:
            chain.sent()
        return 0

    lax.fori_loop(0, ITERS, iteration, 0)
    for k in range(2):
        so_out[k * tile:(k + 1) * tile, :] = s_all[k].T

    @pl.when(own_role)
    def _():
        points_out.wait_send()

    @pl.when(swapped)
    def _():
        out_copy.wait()
        meta_copy.wait_send()
        sp_copy.wait_send()
        tm_copy.wait_send()


def local(target_points, source_points, target_mass, source_mass, start_dual,
          tile_row, tile_column, tile_count):
    slots = tile_row.shape[0]
    rows, measures = target_mass.shape
    tile = rows // 2
    mh = measures // CHAINS
    dma = pltpu.SemaphoreType.DMA
    vmem = pltpu.VMEM
    whole = pl.BlockSpec(memory_space=pltpu.VMEM)
    block = 2 * mh + 16
    return pl.pallas_call(
        functools.partial(kernel, slots),
        out_shape=(
            jax.ShapeDtypeStruct((rows, measures), F32),
            jax.ShapeDtypeStruct((rows, measures), F32),
        ),
        in_specs=[whole] * 7 + [pl.BlockSpec(memory_space=pltpu.SMEM)],
        out_specs=(whole, whole),
        scratch_shapes=[
            vmem((8, 128), I32),
            vmem((8, 128), I32),
            pltpu.SMEM((8, 128), I32),
            vmem(target_points.shape, F32),
            vmem(source_points.shape, F32),
            vmem((rows, measures), F32),
            vmem((64, 8, tile), F32),
            vmem((8, 3, tile, 128), F32),
            vmem((slots, tile, tile), BF16),
            vmem((slots + 1, measures, tile), F32),
            vmem((ITERS, 2, measures, tile), BF16),
            [vmem((ITERS, 8, mh, tile), BF16)] * CHAINS,
            vmem((CHAINS, 4, 2, 4, mh, tile), F32),
            vmem((CHAINS, 4, 2, 4, mh, tile), F32),
            vmem((CHAINS, 2, 4, 4 * mh + 16, tile), I16),
            vmem((ITERS, CHAINS, 2, 4, 4 * mh + 16, tile), I16),
            vmem((CHAINS, 2, 3, mh + 16, tile), I16),
            vmem((ITERS, CHAINS, 2, 3, mh + 16, tile), I16),
            vmem((CHAINS, 2, 4, mh, tile), F32),
            [vmem((ITERS, 64, mh, tile), BF16)] * CHAINS,
            vmem((CHAINS, 4, block, tile), I16),
            vmem((ITERS, CHAINS, 4, block, tile), I16),
            vmem((rows, measures), F32),
            vmem((2, measures, tile), F32),
            vmem((2, measures, tile), F32),
            vmem((2, measures, tile), F32),
            vmem((2, measures, tile), F32),
            dma((4,)), dma((4,)),
            dma((CHAINS, 4)), dma((ITERS, CHAINS, 4)),
            dma((CHAINS, 4)), dma((ITERS, CHAINS, 4)),
            dma((CHAINS, 2, 4)), dma((ITERS, CHAINS, 2, 4)),
            dma((CHAINS, 2, 3)), dma((ITERS, CHAINS, 2, 3)),
            dma((CHAINS, 2, 3)), dma((ITERS, CHAINS, 2, 3)),
            dma((CHAINS, 2, 6)), dma((ITERS, CHAINS, 2, 6)),
            dma((CHAINS, 2, 4)), dma((ITERS, CHAINS, 2, 4)),
            dma((CHAINS, 4)), dma((ITERS, CHAINS, 4)),
            dma, dma, dma,
        ],
        compiler_params=pltpu.CompilerParams(
            collective_id=0, has_side_effects=True, vmem_limit_bytes=60 * 1024 * 1024
        ),
    )(target_points, source_points, target_mass, source_mass, start_dual,
      tile_row.reshape(1, slots), tile_column.reshape(1, slots), tile_count)


def solution(mesh):
    return jax.shard_map(
        local,
        mesh=mesh,
        in_specs=(
            P(None, "row"),
            P(None, "col"),
            P(("row", "col"), None),
            P(("col", "row"), None),
            P(("col", "row"), None),
            P(("row", "col")),
            P(("row", "col")),
            P(("row", "col")),
        ),
        out_specs=(P(("row", "col"), None), P(("col", "row"), None)),
        check_vma=False,
    )
```

```python
import functools

import jax
import jax.numpy as jnp
from jax import lax
from jax.experimental import pallas as pl
from jax.experimental.pallas import tpu as pltpu
from jax.sharding import PartitionSpec as P

MESH = pl.DeviceIdType.MESH
ITERS = 2
CHAINS = 2
GROUP = 24
SCALE = 2.6857913
FINE = 2896.0
COARSE = 256.0
F32 = jnp.float32
BF16 = jnp.bfloat16
I16 = jnp.int16
I32 = jnp.int32


def encode(x):
    level = jnp.log(jnp.maximum(x, 1e-37))
    ref = (level[0:1] * COARSE + 32768.5).astype(I32) - 32768
    fine = level * FINE + (32768.5 - ref.astype(F32) * (FINE / COARSE))
    return (fine.astype(I32) - 32768).astype(I16), ref


def decode(code, ref):
    return jnp.exp(
        code.astype(I32).astype(F32) * (1.0 / FINE) + ref.astype(F32) * (1.0 / COARSE)
    )


def kernel(
    slots,
    tp, sp, tm, sm, sd, tr, tc, tn,
    td_out, so_out,
    meta_own, meta_in, meta, tp_in, sp_in, tm_in, tt, sb, kt, acc,
    src_own, s_band, x0_send, x0_recv, r1_send, r1_recv, r2_send, r2_recv, part,
    t_band, z_send, z_recv, td_own, t_mass, s_mass, t_all, s_all,
    p_send, p_recv, s_send, s_recv, x_send, x_recv, a_send, a_recv, b_send, b_recv,
    q_send, q_recv, g_send, g_recv, c_send, c_recv, w_send, w_recv, o_send, o_recv, m_sem,
):
    tile = kt.shape[1]
    measures = acc.shape[1]
    mh = measures // CHAINS
    row = lax.axis_index("row")
    col = lax.axis_index("col")
    z_lo, core = row // 2, row % 2
    x, z_hi, y = col // 8, (col // 4) % 2, col % 4
    z = z_hi * 2 + z_lo
    other = 1 - core
    own_role = core == z_hi
    swapped = core != z_hi

    def device(x_, y_, z_, core_):
        return ((z_ % 2) * 2 + core_, x_ * 8 + (z_ // 2) * 4 + y_)

    sibling = device(x, y, z, other)
    partner = device(x, y, core * 2 + z_lo, z_hi)

    ring = {(0, step): device((x + step) % 4, y, z, core) for step in (1, 2, 3)}
    ring.update({(1, step): device(x, (y + step) % 4, z, core) for step in (1, 2, 3)})

    def on_ring(axis, step):
        return ring[axis, step]

    delta = (z + 4 - 2 * core) % 4

    def by_delta(*values):
        return jnp.where(delta < 2, jnp.where(delta == 0, values[0], values[1]),
                         jnp.where(delta == 2, values[2], values[3]))

    relayed, single = by_delta(2, 0, 3, 1), by_delta(3, 1, 2, 0)
    up_band = device(x, y, (z + 1) % 4, z_hi)
    down_band = device(x, y, (z + 3) % 4, z_hi)
    up_core = device(x, y, (z + 1) % 4, core)
    down_core = device(x, y, (z + 3) % 4, core)
    relay_step = by_delta(3, 1, 1, 3)
    relay_on = device(x, y, (z + relay_step) % 4, core)

    def owner(r):
        return device(x, y, core * 2 + r // 2, r % 2)

    def remote(src, dst, send, recv, target):
        return pltpu.make_async_remote_copy(
            src_ref=src, dst_ref=dst, send_sem=send, recv_sem=recv,
            device_id=target, device_id_type=MESH,
        )

    barrier = pltpu.get_barrier_semaphore()
    friends = [device(x, y, (z + dz) % 4, (core + dk) % 2)
               for dz in range(4) for dk in range(2) if dz or dk]
    friends += [on_ring(axis, step) for axis in (0, 1) for step in (1, 2, 3)]
    for friend in friends:
        pl.semaphore_signal(barrier, inc=1, device_id=friend, device_id_type=MESH)

    meta_own[...] = jnp.zeros_like(meta_own)
    meta_own[0:1, 0:slots] = jnp.clip(tr[...], 0, 63)
    meta_own[1:2, 0:slots] = jnp.clip(tc[...], 0, 7)
    lane = lax.broadcasted_iota(I32, (128, 128), 1)
    sub = lax.broadcasted_iota(I32, (128, 128), 0)
    alive = sub < tn[0]
    for k in range(2):
        across = jnp.broadcast_to(meta_own[k:k + 1, :], (128, 128))
        down = across.T
        same = (down == across) & (sub < lane) & alive
        found = jnp.max(jnp.where(same, sub, -1), axis=0, keepdims=True)
        meta_own[2 + k:3 + k, :] = jnp.where(found < 0, slots, found)
        same = (down == lane) & alive
        found = jnp.max(jnp.where(same, sub, -1), axis=0, keepdims=True)
        meta_own[4 + k:5 + k, :] = jnp.where(found < 0, slots, found)
    index = meta_own[0:1, :]
    share = index // 2
    sx, sh, sy = share // 8, (share // 4) % 2, share % 4
    even = ((sh * 2 + 0) * 4 + sx) * 4 + sy
    odd = ((sh * 2 + 1) * 4 + sy) * 4 + sx
    meta_own[6:7, :] = jnp.where(index % 2 == 0, even, odd)

    for k in range(2):
        src_own[0, k] = sd[k * tile:(k + 1) * tile, :].astype(F32).T.astype(BF16)
        s_mass[k] = sm[k * tile:(k + 1) * tile, :].T

    pl.semaphore_wait(barrier, len(friends))

    points_out = remote(tp, tp_in, p_send.at[0], p_recv.at[0], sibling)
    sp_copy = remote(sp, sp_in, p_send.at[1], p_recv.at[1], partner)
    meta_copy = remote(meta_own, meta_in, p_send.at[2], p_recv.at[2], partner)
    tm_copy = remote(tm, tm_in, p_send.at[3], p_recv.at[3], partner)

    @pl.when(own_role)
    def _():
        points_out.start()
        sp_in[...] = sp[...]
        tp_in[...] = tp[...]
        tm_in[...] = tm[...]
        meta_in[...] = meta_own[...]

    @pl.when(swapped)
    def _():
        meta_copy.start()
        sp_copy.start()

    def rows_of(h):
        return slice(h * mh, (h + 1) * mh)

    def source_copy(it, h, step):
        target = (sibling, up_band, None, down_band)[step]
        return remote(
            src_own.at[it, :, rows_of(h)], s_band.at[it, pl.ds(2 * row, 2), rows_of(h)],
            s_send.at[h, step], s_recv.at[it, h, row], target,
        )

    def source_relay(it, h):
        ref = s_band.at[it, pl.ds(2 * relayed, 2), rows_of(h)]
        return remote(ref, ref, s_send.at[h, 2], s_recv.at[it, h, relayed], relay_on)

    def source_send(it, h):
        source_copy(it, h, 1).start()
        source_copy(it, h, 3).start()

        @pl.when(swapped)
        def _():
            source_copy(it, h, 0).start()

        @pl.when(own_role)
        def _():
            s_band[it, pl.ds(2 * row, 2), rows_of(h)] = src_own[it, :, rows_of(h)]

    def source_sent(it, h):
        source_copy(it, h, 1).wait_send()
        source_copy(it, h, 3).wait_send()
        source_relay(it, h).wait_send()

        @pl.when(swapped)
        def _():
            source_copy(it, h, 0).wait_send()

    def source_pass_on(it, h):
        source_relay(it, h).wait_recv()
        source_relay(it, h).start()

    def source_arrived(it, h):
        for r in range(4):
            @pl.when(jnp.logical_and(jnp.logical_or(swapped, row != r), relayed != r))
            def _():
                remote(src_own.at[it, :, rows_of(h)],
                       s_band.at[it, 2 * r:2 * r + 2, rows_of(h)], s_send.at[h, 0],
                       s_recv.at[it, h, r], sibling).wait_recv()

    for h in range(CHAINS):
        source_send(0, h)

    @pl.when(swapped)
    def _():
        meta_copy.wait_recv()
        sp_copy.wait_recv()
        points_out.wait_recv()

    to_scalar = pltpu.make_async_copy(meta_in, meta, m_sem)
    to_scalar.start()

    @pl.loop(0, 8)
    def _(c):
        start = pl.multiple_of(c * tile, tile)
        for k in range(3):
            line = sp_in[k:k + 1, pl.ds(start, tile)] * SCALE
            column = jnp.broadcast_to(line, (8, tile)).T[:, 0:1]
            sb[c, k] = jnp.broadcast_to(column, (tile, 128))

    @pl.loop(0, 64, unroll=8)
    def _(r):
        tt[r, 0:3] = tp_in[:, pl.ds(pl.multiple_of(r * tile, tile), tile)] * SCALE

    to_scalar.wait()

    acc[slots] = jnp.zeros((measures, tile), F32)

    def make_tile(s):
        r, c = meta[0, s], meta[1, s]
        for part_at in range(tile // 128):
            lanes = slice(part_at * 128, (part_at + 1) * 128)
            distance = (sb[c, 0] - tt[r, 0:1, lanes]) ** 2
            distance = distance + (sb[c, 1] - tt[r, 1:2, lanes]) ** 2
            distance = distance + (sb[c, 2] - tt[r, 2:3, lanes]) ** 2
            kt[s, :, lanes] = jnp.exp2(-8.0 - distance).astype(BF16)

    def row_product(it, s):
        acc[s] = acc[meta[2, s]] + jnp.dot(s_band[it, meta[1, s]], kt[s],
                                           preferred_element_type=F32)

    steps = 14
    first_tiles = slots - 2 * steps

    @pl.loop(0, first_tiles // 2)
    def _(pair):
        make_tile(2 * pair)
        make_tile(2 * pair + 1)

    for h in range(CHAINS):
        source_pass_on(0, h)

    @pl.when(swapped)
    def _():
        tm_copy.start()

    for h in range(CHAINS):
        source_arrived(0, h)

    @pl.loop(0, steps)
    def _(step):
        for m in range(3):
            row_product(0, 3 * step + m)
        for m in range(2):
            make_tile(first_tiles + 2 * step + m)

    for s in range(3 * steps, slots):
        row_product(0, s)

    def write_block(ref, values):
        n = len(values)
        line = lax.broadcasted_iota(I32, (16, tile), 0)
        refs = jnp.zeros((16, tile), I32)
        for i in range(n):
            code, ref_row = encode(values[i]())
            ref[i * mh:(i + 1) * mh, :] = code
            refs = jnp.where(line == i, ref_row, refs)
        ref[n * mh:n * mh + 16, :] = refs.astype(I16)

    def read_block(ref, i, n=2):
        refs = ref[n * mh:n * mh + 16, :].astype(I32)
        return decode(ref[i * mh:(i + 1) * mh, :], refs[i:i + 1])

    place = ((x, y), (y, x))
    out_copy = remote(td_own, td_out, o_send, o_recv, partner)

    def total(a, d, u, side):
        g = (place[a][0] + d) % 4
        gx, gy = (g, u) if a == 0 else (u, g)
        return meta[4, 2 * (gx * 8 + side * 4 + gy) + a]

    class Chain:
        def __init__(self, h, it):
            self.h, self.it, self.rows = h, it, rows_of(h)

        def x0_copy(self, d):
            h = self.h
            return remote(x0_send.at[h, d], x0_recv.at[h, d], x_send.at[h, d],
                          x_recv.at[self.it, h, d], sibling)

        def r1_rows(self, kind):
            return slice(0, (4 if kind < 2 else 2) * mh + 16)

        def r1_copy(self, a, kind):
            h, it, rows = self.h, self.it, self.r1_rows(kind)
            return remote(r1_send.at[h, a, kind, rows], r1_recv.at[it, h, a, kind, rows],
                          a_send.at[h, a, kind], a_recv.at[it, h, a, kind],
                          on_ring(a, 1 if kind % 2 == 0 else 3))

        def r2_copy(self, a, kind):
            h, it, step = self.h, self.it, (1, 3, 2)[kind]
            return remote(r2_send.at[h, a, kind], r2_recv.at[it, h, a, kind],
                          b_send.at[h, a, kind], b_recv.at[it, h, a, kind], on_ring(1 - a, step))

        def spot(self, a, g, u, side=None):
            return (((core if side is None else side) * 2 + a) * 4 + g) * 4 + u

        def q_copy(self, a, kind):
            p, q = place[a]
            ref = t_band.at[self.it, self.spot(a, p, q), self.rows]
            return remote(ref, ref, q_send.at[self.h, a, kind],
                          q_recv.at[self.it, self.h, a, kind], on_ring(1 - a, (1, 3, 2)[kind]))

        def q_got(self, a, kind):
            p, q = place[a]
            ref = t_band.at[self.it, self.spot(a, p, (q + (3, 1, 2)[kind]) % 4), self.rows]
            remote(ref, ref, q_send.at[self.h, a, kind],
                   q_recv.at[self.it, self.h, a, kind], sibling).wait_recv()

        def pair(self, a, g, far):
            q = place[a][1]
            begin = 2 * (1 - q // 2) if far else 2 * (q // 2)
            return t_band.at[self.it, pl.ds(self.spot(a, g, begin), 2), self.rows]

        def g_copy(self, a, kind):
            p = place[a][0]
            g = (p, p, p, p, (p + 3) % 4, (p + 1) % 4)[kind]
            ref = self.pair(a, g, kind % 2 == 1)
            return remote(ref, ref, g_send.at[self.h, a, kind], g_recv.at[self.it, self.h, a, kind],
                          on_ring(a, (1, 1, 3, 3, 1, 3)[kind]))

        def g_got(self, a, kind):
            p = place[a][0]
            g = ((p + 3) % 4, (p + 3) % 4, (p + 1) % 4, (p + 1) % 4,
                 (p + 2) % 4, (p + 2) % 4)[kind]
            ref = self.pair(a, g, kind % 2 == 1)
            remote(ref, ref, g_send.at[self.h, a, kind], g_recv.at[self.it, self.h, a, kind],
                   sibling).wait_recv()

        def c_copy(self, a, dg):
            base = self.spot(a, (place[a][0] + dg) % 4, 0)
            ref = t_band.at[self.it, pl.ds(base, 4), self.rows]
            return remote(ref, ref, c_send.at[self.h, a, dg],
                          c_recv.at[self.it, self.h, a, dg], sibling)

        def c_got(self, a, dg):
            base = self.spot(a, (place[a][0] + dg) % 4, 0, other)
            ref = t_band.at[self.it, pl.ds(base, 4), self.rows]
            remote(ref, ref, c_send.at[self.h, a, dg],
                   c_recv.at[self.it, self.h, a, dg], sibling).wait_recv()

        def z_copy(self, kind, r):
            h, it = self.h, self.it
            return remote(z_send.at[h, r], z_recv.at[it, h, kind], w_send.at[h, r],
                          w_recv.at[it, h, kind], owner(r))

        def z_far(self, r, target):
            h, it = self.h, self.it
            return remote(z_send.at[h, r], z_recv.at[it, h, 3], w_send.at[h, r],
                          w_recv.at[it, h, 3], target)

        def to_next(self, r, fn):
            below = (core * 2 + r // 2 + 3) % 4 == z

            @pl.when(below)
            def _():
                fn(self.z_copy(1, r))

            @pl.when(jnp.logical_not(below))
            def _():
                fn(self.z_copy(2, r))

        def own(self, a, d, u):
            return acc[total(a, d, u, core), self.rows] + x0_recv[self.h, d, a, u]

        def stage(self, d):
            for a in range(2):
                @pl.loop(0, 4)
                def _(u):
                    x0_send[self.h, d, a, u] = acc[total(a, d, u, other), self.rows]

            self.x0_copy(d).start()

        def ring_first(self):
            self.x0_copy(2).wait_recv()
            for kind, d, far, near in ((0, 1, 0, 2), (1, 3, 2, 0)):
                self.x0_copy(d).wait_recv()
                for a in range(2):
                    write_block(r1_send.at[self.h, a, kind],
                                [functools.partial(self.own, a, 2, far + i) for i in range(2)]
                                + [functools.partial(self.own, a, d, near + i) for i in range(2)])
                    self.r1_copy(a, kind).start()

        def ring_relay(self):
            h, it = self.h, self.it
            for a in range(2):
                for kind, d, u0 in ((2, 1, 0), (3, 3, 2)):
                    self.r1_copy(a, kind - 2).wait_recv()
                    got = r1_recv.at[it, h, a, kind - 2]
                    write_block(r1_send.at[h, a, kind],
                                [lambda i=i: self.own(a, d, u0 + i) + read_block(got, i, 4)
                                 for i in range(2)])
                    self.r1_copy(a, kind).start()

        def ring_sum(self):
            h, it = self.h, self.it
            self.x0_copy(0).wait_recv()
            for a in range(2):
                for i in range(2):
                    part[h, a, i] = self.own(a, 0, i) + read_block(
                        r1_recv.at[it, h, a, 1], 2 + i, 4)
                    part[h, a, 2 + i] = self.own(a, 0, 2 + i) + read_block(
                        r1_recv.at[it, h, a, 0], 2 + i, 4)

        def ring_total(self):
            h, it = self.h, self.it
            for a in range(2):
                q = place[a][1]
                self.r1_copy(a, 2).wait_recv()
                self.r1_copy(a, 3).wait_recv()
                for i in range(2):
                    part[h, a, i] += read_block(r1_recv.at[it, h, a, 2], i)
                    part[h, a, 2 + i] += read_block(r1_recv.at[it, h, a, 3], i)
                for kind in (2, 0, 1):
                    write_block(r2_send.at[h, a, kind],
                                [lambda: part[h, a, (q + (1, 3, 2)[kind]) % 4]])
                    self.r2_copy(a, kind).start()

        def target(self):
            h, it = self.h, self.it
            for a in range(2):
                p, q = place[a]
                for kind in range(3):
                    self.r2_copy(a, kind).wait_recv()
                sums = part[h, a, q]
                for kind in range(3):
                    sums = sums + read_block(r2_recv.at[it, h, a, kind], 0, 1)
                dual = t_mass[a, self.rows] / sums
                t_band[it, self.spot(a, p, q), self.rows] = dual.astype(BF16)
                for kind in (2, 0, 1):
                    self.q_copy(a, kind).start()
                t_all[a, self.rows] = dual

        def gather_near(self):
            for a in range(2):
                self.q_got(a, 0)
                self.q_got(a, 1)
                self.g_copy(a, 0).start()
                self.g_copy(a, 2).start()

        def gather_block(self):
            for a in range(2):
                self.q_got(a, 2)
                self.g_copy(a, 3).start()
                self.g_copy(a, 1).start()
                self.g_got(a, 0)
                self.g_copy(a, 4).start()
            for a in range(2):
                self.c_copy(a, 0).start()

        def gather_relay(self):
            for a in range(2):
                self.g_got(a, 3)
                self.g_copy(a, 5).start()
            for a in range(2):
                self.g_got(a, 1)
                self.c_copy(a, 3).start()
                self.g_got(a, 2)
                self.c_copy(a, 1).start()

        def gather_last(self):
            for a in range(2):
                self.g_got(a, 4)
                self.g_got(a, 5)
                self.c_copy(a, 2).start()

        def gathered(self):
            for dg in (0, 3, 1, 2):
                for a in range(2):
                    self.c_got(a, dg)

        def to_owner(self):
            h, it = self.h, self.it
            first = 2 * (delta % 2)
            for at in range(2):
                r = first + at
                write_block(z_send.at[h, r],
                            [lambda i=i: acc[meta[5, 2 * r + i], self.rows] for i in range(2)])

                @pl.when(swapped)
                def _():
                    self.z_far(r, device(
                        x, y, (z + jnp.where((delta == 2) == (at == 0), 3, 1)) % 4, core)).start()

                @pl.when(jnp.logical_and(own_role, core != at))
                def _():
                    self.z_copy(0, r).start()

                @pl.when(jnp.logical_and(own_role, core == at))
                def _():
                    z_recv[it, h, 0] = z_send[h, r]

            write_block(z_send.at[h, single],
                        [lambda i=i: acc[meta[5, 2 * single + i], self.rows] for i in range(2)])
            self.to_next(single, lambda copy: copy.start())

        def to_owner_relay(self):
            h, it = self.h, self.it
            self.z_far(0, sibling).wait_recv()
            got = z_recv.at[it, h, 3]
            write_block(z_send.at[h, relayed],
                        [lambda i=i: acc[meta[5, 2 * relayed + i], self.rows]
                         + read_block(got, i) for i in range(2)])
            self.to_next(relayed, lambda copy: copy.start())

        def source(self):
            h, it = self.h, self.it
            for kind in range(3):
                @pl.when(jnp.logical_or(swapped, kind != 0))
                def _():
                    self.z_copy(kind, 0).wait_recv()

            for k in range(2):
                sums = read_block(z_recv.at[it, h, 0], k)
                for kind in (1, 2):
                    sums = sums + read_block(z_recv.at[it, h, kind], k)
                dual = s_mass[k, self.rows] / sums
                s_all[k, self.rows] = dual

                @pl.when(it < ITERS - 1)
                def _():
                    src_own[1, k, self.rows] = dual.astype(BF16)

            source_sent(it, h)

            @pl.when(it < ITERS - 1)
            def _():
                source_send(1, h)

        def sent(self):
            h = self.h
            for d in range(4):
                self.x0_copy(d).wait_send()
            for a in range(2):
                for kind in range(4):
                    self.r1_copy(a, kind).wait_send()
                for kind in range(6):
                    self.g_copy(a, kind).wait_send()
                for kind in range(3):
                    self.r2_copy(a, kind).wait_send()
                    self.q_copy(a, kind).wait_send()
                for kind in range(4):
                    self.c_copy(a, kind).wait_send()
            first = 2 * (delta % 2)
            for at in range(2):
                @pl.when(jnp.logical_or(swapped, core != at))
                def _():
                    self.z_far(first + at, sibling).wait_send()
            for r in (single, relayed):
                self.z_copy(1, r).wait_send()

    def iteration(it, _):
        chains = [Chain(h, it) for h in range(CHAINS)]

        @pl.when(it > 0)
        def _():
            for h in range(CHAINS):
                source_arrived(1, h)

            @pl.loop(0, slots // GROUP)
            def _(group):
                for m in range(GROUP):
                    row_product(1, group * GROUP + m)

        for chain in chains:
            for d in (2, 1, 3):
                chain.stage(d)
        order = [(name, h) for name in ("ring_first", "ring_relay") for h in range(CHAINS)]
        order += [("ring_sum", 0), ("ring_total", 0), ("ring_sum", 1), ("ring_total", 1),
                  ("target", 0), ("target", 1), ("gather_near", 0), ("gather_near", 1),
                  ("gather_block", 0), ("gather_block", 1), ("gather_relay", 0),
                  ("gather_relay", 1), ("gather_last", 0), ("gather_last", 1)]
        for name, h in order:
            getattr(chains[h], name)()
            if h < CHAINS - 1:
                continue
            if name == "gather_block":
                @pl.when(it == ITERS - 1)
                def _():
                    for a in range(2):
                        td_own[a * tile:(a + 1) * tile, :] = t_all[a].T

                    @pl.when(swapped)
                    def _():
                        out_copy.start()

                    @pl.when(own_role)
                    def _():
                        td_out[...] = td_own[...]

            if name == "ring_first":
                for chain in chains:
                    chain.stage(0)

                @pl.when(it == 0)
                def _():
                    @pl.when(swapped)
                    def _():
                        tm_copy.wait_recv()

                    for k in range(2):
                        t_mass[k] = tm_in[k * tile:(k + 1) * tile, :].T

        for chain in chains:
            chain.gathered()

        @pl.loop(0, slots // GROUP)
        def _(group):
            for m in range(GROUP):
                s = group * GROUP + m
                acc[s] = acc[meta[3, s]] + lax.dot_general(
                    t_band[it, meta[6, s]], kt[s], (((1,), (1,)), ((), ())),
                    preferred_element_type=F32)

        for name in ("to_owner", "to_owner_relay", "source"):
            for chain in chains:
                getattr(chain, name)()

        @pl.when(it < ITERS - 1)
        def _():
            for h in range(CHAINS):
                source_pass_on(1, h)

        for chain in chains:
            chain.sent()
        return 0

    lax.fori_loop(0, ITERS, iteration, 0)
    for k in range(2):
        so_out[k * tile:(k + 1) * tile, :] = s_all[k].T

    @pl.when(own_role)
    def _():
        points_out.wait_send()

    @pl.when(swapped)
    def _():
        out_copy.wait()
        meta_copy.wait_send()
        sp_copy.wait_send()
        tm_copy.wait_send()


def local(target_points, source_points, target_mass, source_mass, start_dual,
          tile_row, tile_column, tile_count):
    slots = tile_row.shape[0]
    rows, measures = target_mass.shape
    tile = rows // 2
    mh = measures // CHAINS
    dma = pltpu.SemaphoreType.DMA
    vmem = pltpu.VMEM
    whole = pl.BlockSpec(memory_space=pltpu.VMEM)
    block = 2 * mh + 16
    return pl.pallas_call(
        functools.partial(kernel, slots),
        out_shape=(
            jax.ShapeDtypeStruct((rows, measures), F32),
            jax.ShapeDtypeStruct((rows, measures), F32),
        ),
        in_specs=[whole] * 7 + [pl.BlockSpec(memory_space=pltpu.SMEM)],
        out_specs=(whole, whole),
        scratch_shapes=[
            vmem((8, 128), I32),
            vmem((8, 128), I32),
            pltpu.SMEM((8, 128), I32),
            vmem(target_points.shape, F32),
            vmem(source_points.shape, F32),
            vmem((rows, measures), F32),
            vmem((64, 8, tile), F32),
            vmem((8, 3, tile, 128), F32),
            vmem((slots, tile, tile), BF16),
            vmem((slots + 1, measures, tile), F32),
            vmem((ITERS, 2, measures, tile), BF16),
            vmem((ITERS, 8, measures, tile), BF16),
            vmem((CHAINS, 4, 2, 4, mh, tile), F32),
            vmem((CHAINS, 4, 2, 4, mh, tile), F32),
            vmem((CHAINS, 2, 4, 4 * mh + 16, tile), I16),
            vmem((ITERS, CHAINS, 2, 4, 4 * mh + 16, tile), I16),
            vmem((CHAINS, 2, 3, mh + 16, tile), I16),
            vmem((ITERS, CHAINS, 2, 3, mh + 16, tile), I16),
            vmem((CHAINS, 2, 4, mh, tile), F32),
            vmem((ITERS, 64, measures, tile), BF16),
            vmem((CHAINS, 4, block, tile), I16),
            vmem((ITERS, CHAINS, 4, block, tile), I16),
            vmem((rows, measures), F32),
            vmem((2, measures, tile), F32),
            vmem((2, measures, tile), F32),
            vmem((2, measures, tile), F32),
            vmem((2, measures, tile), F32),
            dma((4,)), dma((4,)),
            dma((CHAINS, 4)), dma((ITERS, CHAINS, 4)),
            dma((CHAINS, 4)), dma((ITERS, CHAINS, 4)),
            dma((CHAINS, 2, 4)), dma((ITERS, CHAINS, 2, 4)),
            dma((CHAINS, 2, 3)), dma((ITERS, CHAINS, 2, 3)),
            dma((CHAINS, 2, 3)), dma((ITERS, CHAINS, 2, 3)),
            dma((CHAINS, 2, 6)), dma((ITERS, CHAINS, 2, 6)),
            dma((CHAINS, 2, 4)), dma((ITERS, CHAINS, 2, 4)),
            dma((CHAINS, 4)), dma((ITERS, CHAINS, 4)),
            dma, dma, dma,
        ],
        compiler_params=pltpu.CompilerParams(
            collective_id=0, has_side_effects=True, vmem_limit_bytes=60 * 1024 * 1024
        ),
    )(target_points, source_points, target_mass, source_mass, start_dual,
      tile_row.reshape(1, slots), tile_column.reshape(1, slots), tile_count)


def solution(mesh):
    return jax.shard_map(
        local,
        mesh=mesh,
        in_specs=(
            P(None, "row"),
            P(None, "col"),
            P(("row", "col"), None),
            P(("col", "row"), None),
            P(("col", "row"), None),
            P(("row", "col")),
            P(("row", "col")),
            P(("row", "col")),
        ),
        out_specs=(P(("row", "col"), None), P(("col", "row"), None)),
        check_vma=False,
    )
```
